32 devices in a mesh: site: 2 (over x), gx: 16 (over z, y, core).
Axes of the slice: x: 2, y: 2, z: 4, core: 2. Of those that a mesh axis runs over, the one named last changes fastest.
Arguments:
- velocity: float32 [3, 256, 32, 128], P(None, ('site', 'gx')), parts along dimension 1, may hold values from -6 to 6
- stress: float32 [6, 256, 32, 128], P(None, ('site', 'gx')), parts along dimension 1, may hold values from -6 to 6
- material: int32 [128, 32, 128], P('gx'), may hold values from 0 to 7
- buoyancy_table: float32 [8], replicated, may hold values from 0.7 to 1.4
- lame_table: float32 [8], replicated, may hold values from 0.1 to 0.3
- shear_table: float32 [8], replicated, may hold values from 0.1 to 0.35
- fault_cells: int32 [64, 128], P('gx'), may hold values from 0 to 32767
- block_count: int32 [16], P('gx'), may hold values from 1 to 4, as said below
- strain_history: bfloat16 [128, 6, 128, 512], P(('site', 'gx')), parts along dimension 0, may hold values from -6 to 6
- slip_weights: bfloat16 [64, 256, 768], P('gx'), may hold values from -0.0390625 to 0.0390625
Outputs:
- velocity_out: float32 [3, 256, 32, 128], P(None, ('site', 'gx')), parts along dimension 1
- stress_out: float32 [6, 256, 32, 128], P(None, ('site', 'gx')), parts along dimension 1
- seismograms: float32 [512, 512], P(('site', 'gx')), parts along dimension 0
The draws below stay inside these ranges and needn't reach their ends.
There are 2 independent parts, one for each index of `site`. The reference program is written for one: setup_inputs(seed, part) draws one part's arguments, and reference() takes and returns one part's arrays. A program takes and returns all parts, laid end to end along the dimension named above; an argument that names none is the same for every part. Nothing has to cross between parts.
Inputs may be any that keep to these rules, and one draw needn't show every extreme that they name: `block_count`: live blocks of a device are its first slots; some device has 4 of them. `fault_cells`: cells are numbered row-major over one device's 8 x 32 x 128 slab.
All inputs are finite; a program needn't handle non-finite values.
Results may differ from the reference program's by a relative error of at most 0.00049.
Values may be sent and summed in bfloat16 or wider, within the bound.
No kernel may reach another device: no remote copies, remote signals or barrier semaphores. Data moves between devices by JAX's collectives and lax.ppermute only.
A program may use at most 128 MiB of HBM per device.

```python
import math
import jax
import jax.numpy as jnp
from jax import lax

CX = 8
NY = 32
NZ = 128
MATS = 8
PTS = 128
SAMP = 512
BLK_CAP = 4
RUPT = 256
NX = 128
NBLK = 64
N_GX = 16


def draw_block_count(key, part):
    key = jax.random.fold_in(key, 11)
    busy_key, peak_key = jax.random.split(key)
    busy = jax.random.randint(busy_key, (N_GX,), 0, 6) == 0
    counts = jnp.where(busy, BLK_CAP, 1)
    peak = jax.random.randint(peak_key, (), 0, N_GX)
    counts = jnp.where(jnp.arange(N_GX) == peak, BLK_CAP, counts)
    return counts.astype(jnp.int32)


def plant(entries, own_key, low, largest):
    longest = entries.shape.index(max(entries.shape))
    spots = []
    for shift in (0, 1):
        where = [jax.random.randint(jax.random.fold_in(own_key, axis), (), 0, length) for axis, length in enumerate(entries.shape)]
        where[longest] = (where[longest] + shift) % entries.shape[longest]
        spots.append(tuple(where))
    return entries.at[spots[0]].set(low).at[spots[1]].set(largest)


def with_spikes(values, stream_key, source, target, parts, factor):
    def block_of(dim):
        return (jnp.arange(values.shape[dim]) // (values.shape[dim] // parts)).reshape((-1,) + (1,) * (values.ndim - 1 - dim))

    one_side = jax.random.permutation(stream_key, parts)[block_of(target)]
    other_side = (block_of(target) + parts // 2) % parts
    return jnp.where((block_of(source) == one_side) | (block_of(source) == other_side), factor * values, values)


def level_of(own_key, shape, cuts, smallest, largest):
    loudness = 1.0
    for axis_at, shards_of in cuts:
        draws = jax.random.uniform(jax.random.fold_in(jax.random.fold_in(own_key, 6), axis_at), (shards_of,), jnp.float32, smallest / len(cuts), largest / len(cuts))
        loudness = loudness * jnp.repeat(jnp.exp(draws), shape[axis_at] // shards_of).reshape((-1,) + (1,) * (len(shape) - 1 - axis_at))
    return loudness


def noise(stream_key, dims, scale, limit, cuts=(), kind=jnp.bfloat16):
    loudness = level_of(stream_key, dims, cuts, -0.22, 0.18) if cuts else 1.0
    values = jax.random.normal(stream_key, dims, jnp.float32) * scale * loudness
    return jnp.minimum(jnp.maximum(values, -limit), limit).astype(kind)


def bell_draw_with(key, shape, spread, bound, shards, heavy, held_as=jnp.bfloat16):
    values = spread * jax.random.normal(key, shape, jnp.float32)
    if shards:
        values = values * level_of(key, shape, shards, -0.22, 0.18)
    return jnp.clip(with_spikes(values, jax.random.fold_in(key, 3), *heavy), -bound, bound).astype(held_as)


def setup_inputs(seed: int = 0, part: int = 0) -> dict:
    streams_of = jax.random.split(jax.random.key(seed), 11)
    part_splits = jax.random.split(jax.random.fold_in(streams_of[10], part), 11)
    velocity = noise(part_splits[0], (3, NX, NY, NZ), 1.0, 6.0, ((1, 16),), jnp.float32)
    stress = noise(part_splits[1], (6, NX, NY, NZ), 1.0, 6.0, ((1, 16),), jnp.float32)
    material = plant(jax.random.randint(streams_of[2], (NX, NY, NZ), 0, MATS), jax.random.fold_in(streams_of[2], 1), 0, MATS - 1).astype(jnp.int32)
    buoyancy_table = jnp.clip(jnp.exp(jax.random.uniform(streams_of[3], (MATS,), jnp.float32, math.log(0.7), math.log(1.4))), 0.7, 1.4)
    lame_table = jnp.clip(jnp.exp(jax.random.uniform(streams_of[4], (MATS,), jnp.float32, math.log(0.1), math.log(0.3))), 0.1, 0.3)
    shear_table = jnp.clip(jnp.exp(jax.random.uniform(streams_of[5], (MATS,), jnp.float32, math.log(0.1), math.log(0.35))), 0.1, 0.35)
    fault_cells = plant(jax.random.randint(streams_of[6], (NBLK, PTS), 0, CX * NY * NZ), jax.random.fold_in(streams_of[6], 1), 0, (CX * NY * NZ) - 1).astype(jnp.int32)
    block_count = draw_block_count(jax.random.fold_in(streams_of[10], 71), part)
    strain_history = noise(part_splits[8], (NBLK, 6, PTS, SAMP), 1.0, 6.0, ((0, 16),))
    slip_weights = bell_draw_with(streams_of[9], (NBLK, RUPT, 6 * PTS), (6 * PTS * NBLK) ** -0.5, 0.0390625, ((0, 16),), (0, 1, 16, 2.0))
    return {"velocity": velocity, "stress": stress, "material": material, "buoyancy_table": buoyancy_table, "lame_table": lame_table, "shear_table": shear_table, "fault_cells": fault_cells, "block_count": block_count, "strain_history": strain_history, "slip_weights": slip_weights}


first_coef = 9.0 / 8.0
second_coef = -1.0 / 24.0
time_step = 0.4


def lookup(material, table):
    result = jnp.zeros(material.shape, jnp.float32)
    for material_id in range(table.shape[0]):
        result = result + jnp.where(material == material_id, table[material_id], 0.0)
    return result


def difference(padded, axis, forward):
    extent = [padded.shape[dimension] - 4 for dimension in range(3)]
    offsets = (1, 2, 3, 4) if forward else (0, 1, 2, 3)
    pieces = []
    for offset in offsets:
        starts = [2, 2, 2]
        starts[axis] = offset
        limits = [starts[dimension] + extent[dimension] for dimension in range(3)]
        pieces.append(lax.slice(padded, starts, limits))
    return first_coef * (pieces[2] - pieces[1]) + second_coef * (pieces[3] - pieces[0])


def pad_sides(field):
    return jnp.pad(field, ((0, 0), (2, 2), (2, 2)))


def vel_update(velocity, stress_wide, buoyancy):
    padded = [pad_sides(stress_wide[component]) for component in range(6)]
    accel_x = difference(padded[0], 0, True) + difference(padded[3], 1, False) + difference(padded[4], 2, False)
    accel_y = difference(padded[3], 0, False) + difference(padded[1], 1, True) + difference(padded[5], 2, False)
    accel_z = difference(padded[4], 0, False) + difference(padded[5], 1, False) + difference(padded[2], 2, True)
    return velocity + time_step * buoyancy * jnp.stack([accel_x, accel_y, accel_z])


def stress_update(stress, velocity_wide, lame_field, shear_field):
    padded = [pad_sides(velocity_wide[component]) for component in range(3)]
    strain_xx = difference(padded[0], 0, False)
    strain_yy = difference(padded[1], 1, False)
    strain_zz = difference(padded[2], 2, False)
    strain_xy = difference(padded[0], 1, True) + difference(padded[1], 0, True)
    strain_xz = difference(padded[0], 2, True) + difference(padded[2], 0, True)
    strain_yz = difference(padded[1], 2, True) + difference(padded[2], 1, True)
    volumetric = strain_xx + strain_yy + strain_zz
    change = jnp.stack([
        lame_field * volumetric + 2.0 * shear_field * strain_xx,
        lame_field * volumetric + 2.0 * shear_field * strain_yy,
        lame_field * volumetric + 2.0 * shear_field * strain_zz,
        shear_field * strain_xy,
        shear_field * strain_xz,
        shear_field * strain_yz])
    return stress + time_step * change


def strain_at(stress_flat, lame_flat, shear_flat, point_cells):
    sampled = jnp.take(stress_flat, point_cells, axis=1)
    lame_picked = jnp.take(lame_flat, point_cells)
    shear_picked = jnp.take(shear_flat, point_cells)
    volumetric = sampled[0] + sampled[1] + sampled[2]
    bulk_part = lame_picked / (3.0 * lame_picked + 2.0 * shear_picked) * volumetric
    normal_parts = [(sampled[component] - bulk_part) / (2.0 * shear_picked) for component in range(3)]
    shear_parts = [sampled[component] / (2.0 * shear_picked) for component in range(3, 6)]
    return jnp.stack(normal_parts + shear_parts, 1).astype(jnp.bfloat16)


def reference(velocity, stress, material, buoyancy_table, lame_table, shear_table, fault_cells, block_count, strain_history, slip_weights):
    buoyancy = lookup(material, buoyancy_table)
    lame_field = lookup(material, lame_table)
    shear_field = lookup(material, shear_table)
    pad_rim = ((0, 0), (2, 2), (0, 0), (0, 0))
    velocity_one = vel_update(velocity, jnp.pad(stress, pad_rim), buoyancy)
    stress_one = stress_update(stress, jnp.pad(velocity_one, pad_rim), lame_field, shear_field)
    velocity_two = vel_update(velocity_one, jnp.pad(stress_one, pad_rim), buoyancy)
    stress_two = stress_update(stress_one, jnp.pad(velocity_two, pad_rim), lame_field, shear_field)
    owner = jnp.arange(BLK_CAP * N_GX, dtype=jnp.int32) // BLK_CAP
    global_cells = (owner[:, None] * (CX * NY * NZ) + fault_cells).astype(jnp.int32)
    lame_flat = lame_field.reshape(-1)
    shear_flat = shear_field.reshape(-1)
    new_one = strain_at(stress_one.reshape(6, -1), lame_flat, shear_flat, global_cells)
    new_two = strain_at(stress_two.reshape(6, -1), lame_flat, shear_flat, global_cells)
    record = jnp.concatenate([strain_history[..., 2:], new_one[..., None], new_two[..., None]], 3)
    block_slot = jnp.arange(BLK_CAP * N_GX, dtype=jnp.int32) % BLK_CAP
    is_live = block_slot < block_count[owner]
    flat_record = record.reshape(record.shape[0], -1, record.shape[3])

    def add_block(running, inputs):
        weight_block, record_block, live_flag = inputs
        product = jnp.dot(weight_block.astype(jnp.float32), record_block.astype(jnp.float32))
        return running + jnp.where(live_flag, product, 0.0), None

    seismograms, _ = lax.scan(add_block, jnp.zeros((RUPT, SAMP), jnp.float32), (slip_weights, flat_record, is_live))
    return velocity_two, stress_two, seismograms
```

```python
import functools

import jax
import jax.numpy as jnp
from jax import lax
from jax.experimental import pallas as pl
from jax.experimental.pallas import tpu as pltpu
from jax.sharding import PartitionSpec as P

first_coef = 9.0 / 8.0
second_coef = -1.0 / 24.0
time_step = 0.4

VX, VY, VZ, SXX, SYY, SZZ, SXY, SXZ, SYZ, MAT = range(10)
LOWER = (5, 4, 4, 6, 4, 4, 6, 6, 4, 5)
UPPER = (4, 5, 5, 6, 5, 5, 6, 6, 5, 5)
EDGE = 6
RIM = 8
LOWER_AT = [sum(LOWER[:field]) for field in range(11)]
UPPER_AT = [sum(UPPER[:field]) for field in range(11)]
LOWER_PLANES = LOWER_AT[10] + 9
UPPER_PLANES = UPPER_AT[10] + 9

f32 = jnp.float32
bf16 = jnp.bfloat16


def pack_kernel(velocity, stress, material, to_next, to_last):
    planes = velocity.shape[1]

    def source(field, plane):
        if field < 3:
            return velocity[field, plane]
        if field < 9:
            return stress[field - 3, plane]
        return (material[plane] + 1).astype(f32)

    for field in range(10):
        for step in range(LOWER[field]):
            values = source(field, planes - LOWER[field] + step)
            rounded = values.astype(bf16)
            to_next[LOWER_AT[field] + step] = rounded
            if field < 9 and step == LOWER[field] - 1:
                to_next[LOWER_AT[10] + field] = (values - rounded.astype(f32)).astype(bf16)
        for step in range(UPPER[field]):
            values = source(field, step)
            rounded = values.astype(bf16)
            to_last[UPPER_AT[field] + step] = rounded
            if field < 9 and step == 0:
                to_last[UPPER_AT[10] + field] = (values - rounded.astype(f32)).astype(bf16)


def looked_up(code, table, scale):
    result = jnp.zeros(code.shape, f32)
    for entry in range(table.shape[0]):
        result = jnp.where(code == entry + 1, scale * table[entry], result)
    return result


def one_hot_sum(rows_of_cells, picked):
    row = lax.broadcasted_iota(jnp.int32, picked.shape, 0)
    return jnp.sum(jnp.where(row == rows_of_cells, picked, 0.0), axis=0, keepdims=True)


def lane_hits(lanes_of_cells, depth):
    lane = lax.broadcasted_iota(jnp.int32, (depth, lanes_of_cells.shape[1]), 0)
    return (lane == lanes_of_cells).astype(f32).astype(bf16)


def history_kernel(
    live, material, buoyancy_table, lame_table, shear_table, cells, weights, history, partial, fields, points
):
    slot = pl.program_id(0)
    product = functools.partial(jnp.dot, preferred_element_type=f32)

    @pl.when(slot == 0)
    def _():
        partial[...] = product(weights[0], history[0])
        for plane in range(material.shape[0]):
            code = material[plane] + 1
            fields[0, plane] = looked_up(code, buoyancy_table, time_step)
            fields[1, plane] = looked_up(code, lame_table, time_step)
            fields[2, plane] = looked_up(code, shear_table, time_step)
        depth = material.shape[0] * material.shape[1]
        lanes = material.shape[2]
        cell = cells[...]
        codes = (material[...].reshape(depth, lanes) + 1).astype(f32).astype(bf16)
        picked = product(codes, lane_hits(cell % lanes, lanes))
        code = one_hot_sum(cell // lanes, picked).astype(jnp.int32)
        lame = looked_up(code, lame_table, 1.0)
        shear = looked_up(code, shear_table, 1.0)
        points[0:1] = lame / (3.0 * lame + 2.0 * shear)
        points[1:2] = 1.0 / (2.0 * shear)

    @pl.when((slot > 0) & (slot < live[0]))
    def _():
        partial[...] += product(weights[0], history[0])


def steps_kernel(
    live,
    buoyancy_table,
    lame_table,
    shear_table,
    velocity,
    stress,
    fields,
    weights,
    lower,
    upper,
    cells,
    points,
    velocity_out,
    stress_out,
    tail,
    grid,
    factors,
    split,
    slips,
    slab_sems,
    field_sems,
    slip_sem,
    out_sems,
):
    planes, rows, lanes = velocity.shape[1:]
    inner = pl.ds(RIM, rows)

    slab_copies = [
        pltpu.make_async_copy(
            velocity.at[field] if field < 3 else stress.at[field - 3],
            grid.at[field, pl.ds(EDGE, planes), inner],
            slab_sems.at[field],
        )
        for field in range(9)
    ]
    for copy in slab_copies:
        copy.start()
    field_copies = [
        pltpu.make_async_copy(fields.at[kind], factors.at[kind, pl.ds(EDGE, planes)], field_sems.at[kind])
        for kind in range(3)
    ]
    for copy in field_copies:
        copy.start()
    slip_copy = pltpu.make_async_copy(weights, slips, slip_sem)
    slip_copy.start()

    blank = jnp.zeros((grid.shape[1], RIM, lanes), f32)
    for field in (VX, VY, VZ, SXY, SYY, SYZ):
        grid[field, :, 0:RIM] = blank
        grid[field, :, RIM + rows : 2 * RIM + rows] = blank

    for field in range(9):
        for step in range(LOWER[field]):
            values = lower[LOWER_AT[field] + step].astype(f32)
            if step == LOWER[field] - 1:
                values = values + lower[LOWER_AT[10] + field].astype(f32)
            grid[field, EDGE - LOWER[field] + step, inner] = values
        for step in range(UPPER[field]):
            values = upper[UPPER_AT[field] + step].astype(f32)
            if step == 0:
                values = values + upper[UPPER_AT[10] + field].astype(f32)
            grid[field, EDGE + planes + step, inner] = values
    for step in range(LOWER[MAT]):
        code = lower[LOWER_AT[MAT] + step].astype(f32).astype(jnp.int32)
        place = EDGE - LOWER[MAT] + step
        factors[0, place] = looked_up(code, buoyancy_table, time_step)
        if place >= EDGE - 3:
            factors[1, place] = looked_up(code, lame_table, time_step)
            factors[2, place] = looked_up(code, shear_table, time_step)
    for step in range(UPPER[MAT]):
        code = upper[UPPER_AT[MAT] + step].astype(f32).astype(jnp.int32)
        place = EDGE + planes + step
        factors[0, place] = looked_up(code, buoyancy_table, time_step)
        if step < 3:
            factors[1, place] = looked_up(code, lame_table, time_step)
            factors[2, place] = looked_up(code, shear_table, time_step)

    lane = lax.broadcasted_iota(jnp.int32, (rows, lanes), 1)

    def combine(behind, here_low, here_high, ahead):
        return first_coef * (here_high - here_low) + second_coef * (ahead - behind)

    def along_x(field, place, forward):
        start = place - 1 if forward else place - 2
        return combine(*[grid[field, start + step, inner] for step in range(4)])

    def along_y(field, place, forward):
        start = RIM - 1 if forward else RIM - 2
        return combine(*[grid[field, place, pl.ds(start + step, rows)] for step in range(4)])

    def along_z(field, place, forward):
        here = grid[field, place, inner]
        behind = jnp.where(lane >= 1, pltpu.roll(here, 1, 1), 0.0)
        ahead = jnp.where(lane < lanes - 1, pltpu.roll(here, lanes - 1, 1), 0.0)
        if forward:
            further = jnp.where(lane < lanes - 2, pltpu.roll(here, lanes - 2, 1), 0.0)
            return combine(behind, here, ahead, further)
        further = jnp.where(lane >= 2, pltpu.roll(here, 2, 1), 0.0)
        return combine(further, behind, here, ahead)

    def move(place, do_x, do_yz):
        buoyancy = factors[0, place]
        if do_x:
            pull = along_x(SXX, place, True) + along_y(SXY, place, False) + along_z(SXZ, place, False)
            grid[VX, place, inner] = grid[VX, place, inner] + buoyancy * pull
        if do_yz:
            pull = along_x(SXY, place, False) + along_y(SYY, place, True) + along_z(SYZ, place, False)
            grid[VY, place, inner] = grid[VY, place, inner] + buoyancy * pull
            pull = along_x(SXZ, place, False) + along_y(SYZ, place, False) + along_z(SZZ, place, True)
            grid[VZ, place, inner] = grid[VZ, place, inner] + buoyancy * pull

    def strain(place, do_yz, keep):
        lame, shear = factors[1, place], factors[2, place]
        twice = 2.0 * shear
        exx = along_x(VX, place, False)
        eyy = along_y(VY, place, False)
        ezz = along_z(VZ, place, False)
        common = lame * (exx + eyy + ezz)
        changes = [(SXX, common + twice * exx)]
        changes.append((SXY, shear * (along_y(VX, place, True) + along_x(VY, place, True))))
        changes.append((SXZ, shear * (along_z(VX, place, True) + along_x(VZ, place, True))))
        if do_yz:
            changes.append((SYY, common + twice * eyy))
            changes.append((SZZ, common + twice * ezz))
            changes.append((SYZ, shear * (along_z(VY, place, True) + along_y(VZ, place, True))))
        for field, change in changes:
            values = grid[field, place, inner] + change
            grid[field, place, inner] = values
            if keep:
                high = values.astype(bf16)
                at = pl.ds(pl.multiple_of((place - EDGE) * rows, rows), rows)
                split[field - 3, at, pl.ds(0, lanes)] = high
                split[field - 3, at, pl.ds(lanes, lanes)] = (values - high.astype(f32)).astype(bf16)

    def over(first, last, body):
        def step(place, carry):
            body(place)
            return carry

        lax.fori_loop(EDGE + first, EDGE + last, step, 0)

    cell = cells[...]
    hits = lane_hits(cell % lanes, lanes)
    hits = jnp.concatenate([hits, hits], axis=0)
    rows_of_cells = cell // lanes
    trace_part, compliance = points[0:1], points[1:2]

    def sampled_strain():
        found = [
            one_hot_sum(rows_of_cells, jnp.dot(split[part], hits, preferred_element_type=f32)) for part in range(6)
        ]
        shift = trace_part * (found[0] + found[1] + found[2])
        parts = [(found[part] - shift) * compliance for part in range(3)]
        parts += [found[part] * compliance for part in range(3, 6)]
        return [part.astype(bf16).astype(f32) for part in parts]

    for copy in slab_copies:
        copy.wait()
    for copy in field_copies:
        copy.wait()

    top = planes
    move(EDGE - 5, True, False)
    over(-4, top + 4, lambda place: move(place, True, True))
    move(EDGE + top + 4, False, True)
    over(-3, -1, lambda place: strain(place, False, False))
    strain(EDGE - 1, True, False)
    over(0, top, lambda place: strain(place, True, True))
    over(top, top + 2, lambda place: strain(place, True, False))
    strain(EDGE + top + 2, False, False)
    first_sample = sampled_strain()
    move(EDGE - 2, True, False)
    over(-1, top + 1, lambda place: move(place, True, True))
    move(EDGE + top + 1, False, True)
    out_copies = [
        pltpu.make_async_copy(
            grid.at[field, pl.ds(EDGE, planes), inner],
            velocity_out.at[field] if field < 3 else stress_out.at[field - 3],
            out_sems.at[field],
        )
        for field in range(9)
    ]
    for copy in out_copies[:3]:
        copy.start()
    over(0, top, lambda place: strain(place, True, True))
    for copy in out_copies[3:]:
        copy.start()
    second_sample = sampled_strain()

    slip_copy.wait()
    points_each = weights.shape[2] // 6
    new = jnp.zeros((8, weights.shape[1]), f32)
    for slot in range(weights.shape[0]):
        at = slice(slot * points_each, (slot + 1) * points_each)
        pair = jnp.concatenate(
            [jnp.concatenate([part[:, at] for part in sample], axis=1) for sample in (first_sample, second_sample)]
            + [jnp.zeros((6, weights.shape[2]), f32)],
            axis=0,
        )
        pair = jnp.where(slot < live[0], pair, 0.0).astype(bf16)
        new = new + lax.dot_general(pair, slips[slot], (((1,), (1,)), ((), ())), preferred_element_type=f32)
    line = jnp.concatenate([new[0:1], new[1:2]], axis=1)
    for owner in range(tail.shape[0]):
        tail[owner] = line
    for copy in out_copies:
        copy.wait()


def finish_kernel(place, partials, tails, out):
    share, samples = out.shape
    devices = tails.shape[0]
    total = partials[0:share]
    new = tails[0]
    for device in range(1, devices):
        total = total + partials[device * share : (device + 1) * share]
        new = new + tails[device]
    ruptures = new.shape[1] // 2
    row = lax.broadcasted_iota(jnp.int32, (share, ruptures), 0)
    column = lax.broadcasted_iota(jnp.int32, (share, ruptures), 1)
    mine = column == row + place[0] * share
    sample = lax.broadcasted_iota(jnp.int32, (share, samples), 1)
    total = jnp.concatenate([total[:, 2:], jnp.zeros((share, 2), f32)], axis=1)
    for which in range(2):
        values = jnp.sum(
            jnp.where(mine, new[:, which * ruptures : (which + 1) * ruptures], 0.0), axis=1, keepdims=True
        )
        total = jnp.where(sample == samples - 2 + which, values, total)
    out[...] = total


def per_device(
    velocity,
    stress,
    material,
    buoyancy_table,
    lame_table,
    shear_table,
    fault_cells,
    block_count,
    strain_history,
    slip_weights,
):
    count = lax.axis_size("gx")
    planes, rows, lanes = material.shape
    slots, parts, points_each, samples = strain_history.shape
    ruptures = slip_weights.shape[1]
    spots = slots * points_each
    whole = pl.BlockSpec(memory_space=pltpu.VMEM)
    scalars = pl.BlockSpec(memory_space=pltpu.SMEM)
    anywhere = pl.BlockSpec(memory_space=pl.ANY)
    params = functools.partial(pltpu.CompilerParams, vmem_limit_bytes=40 * 1024 * 1024)

    to_next, to_last = pl.pallas_call(
        pack_kernel,
        out_shape=(
            jax.ShapeDtypeStruct((LOWER_PLANES, rows, lanes), bf16),
            jax.ShapeDtypeStruct((UPPER_PLANES, rows, lanes), bf16),
        ),
        in_specs=[whole] * 3,
        out_specs=(whole, whole),
        compiler_params=params(),
        name="pack_halos",
    )(velocity, stress, material)
    lower = lax.ppermute(to_next, "gx", [(i, i + 1) for i in range(count - 1)])
    upper = lax.ppermute(to_last, "gx", [(i + 1, i) for i in range(count - 1)])

    cells = fault_cells.reshape(1, spots)
    history = strain_history.reshape(slots, parts * points_each, samples)

    def live_slot(slot, live):
        return (jnp.minimum(slot, live[0] - 1), 0, 0)

    def at_start(*shape):
        return pl.BlockSpec(shape, lambda slot, live: (0,) * len(shape))

    partial, fields, points = pl.pallas_call(
        history_kernel,
        grid_spec=pltpu.PrefetchScalarGridSpec(
            num_scalar_prefetch=1,
            grid=(slots,),
            in_specs=[
                at_start(planes, rows, lanes),
                scalars,
                scalars,
                scalars,
                at_start(1, spots),
                pl.BlockSpec((1, ruptures, parts * points_each), live_slot),
                pl.BlockSpec((1, parts * points_each, samples), live_slot),
            ],
            out_specs=[at_start(ruptures, samples), at_start(3, planes, rows, lanes), at_start(8, spots)],
        ),
        out_shape=(
            jax.ShapeDtypeStruct((ruptures, samples), f32),
            jax.ShapeDtypeStruct((3, planes, rows, lanes), f32),
            jax.ShapeDtypeStruct((8, spots), f32),
        ),
        compiler_params=params(),
        cost_estimate=pl.CostEstimate(flops=2 * 805306368 // 2, bytes_accessed=5 * 1024 * 1024, transcendentals=0),
        name="history_product",
    )(block_count, material, buoyancy_table, lame_table, shear_table, cells, slip_weights, history)
    partials = lax.all_to_all(partial, "gx", 0, 0, tiled=True)

    velocity_two, stress_two, tail = pl.pallas_call(
        steps_kernel,
        out_shape=(
            jax.ShapeDtypeStruct(velocity.shape, f32),
            jax.ShapeDtypeStruct(stress.shape, f32),
            jax.ShapeDtypeStruct((count, 1, 2 * ruptures), f32),
        ),
        in_specs=[scalars] * 4 + [anywhere] * 4 + [whole] * 4,
        out_specs=(anywhere, anywhere, whole),
        scratch_shapes=[
            pltpu.VMEM((9, planes + 2 * EDGE, rows + 2 * RIM, lanes), f32),
            pltpu.VMEM((3, planes + 2 * EDGE, rows, lanes), f32),
            pltpu.VMEM((6, planes * rows, 2 * lanes), bf16),
            pltpu.VMEM(slip_weights.shape, bf16),
            pltpu.SemaphoreType.DMA((9,)),
            pltpu.SemaphoreType.DMA((3,)),
            pltpu.SemaphoreType.DMA,
            pltpu.SemaphoreType.DMA((9,)),
        ],
        compiler_params=params(),
        name="two_steps",
    )(
        block_count,
        buoyancy_table,
        lame_table,
        shear_table,
        velocity,
        stress,
        fields,
        slip_weights,
        lower,
        upper,
        cells,
        points,
    )
    tails = lax.all_to_all(tail, "gx", 0, 0, tiled=True)

    place = lax.axis_index("gx").astype(jnp.int32).reshape(1)
    seismograms = pl.pallas_call(
        finish_kernel,
        out_shape=jax.ShapeDtypeStruct((ruptures // count, samples), f32),
        in_specs=[scalars, whole, whole],
        out_specs=whole,
        compiler_params=params(),
        name="sum_partials",
    )(place, partials, tails)
    return (velocity_two, stress_two, seismograms)


def solution(mesh):
    in_specs = (
        P(None, ("site", "gx"), None, None),
        P(None, ("site", "gx"), None, None),
        P("gx", None, None),
        P(),
        P(),
        P(),
        P("gx", None),
        P("gx"),
        P(("site", "gx"), None, None, None),
        P("gx", None, None),
    )
    out_specs = (
        P(None, ("site", "gx"), None, None),
        P(None, ("site", "gx"), None, None),
        P(("site", "gx"), None),
    )
    return jax.shard_map(
        per_device, mesh=mesh, in_specs=in_specs, out_specs=out_specs, check_vma=False
    )
```

```python
import functools

import jax
import jax.numpy as jnp
from jax import lax
from jax.experimental import pallas as pl
from jax.experimental.pallas import tpu as pltpu
from jax.sharding import PartitionSpec as P

first_coef = 9.0 / 8.0
second_coef = -1.0 / 24.0
time_step = 0.4

VX, VY, VZ, SXX, SYY, SZZ, SXY, SXZ, SYZ, MAT = range(10)
LOWER = (5, 4, 4, 6, 4, 4, 6, 6, 4, 5)
UPPER = (4, 5, 5, 6, 5, 5, 6, 6, 5, 5)
EDGE = 6
RIM = 8
LOWER_AT = [sum(LOWER[:field]) for field in range(11)]
UPPER_AT = [sum(UPPER[:field]) for field in range(11)]
LOWER_PLANES = LOWER_AT[10] + 9
UPPER_PLANES = UPPER_AT[10] + 9

f32 = jnp.float32
bf16 = jnp.bfloat16


def pack_kernel(odd, velocity, stress, material, across, within):
    planes = velocity.shape[1]

    def source(field, plane):
        if field < 3:
            return velocity[field, plane]
        if field < 9:
            return stress[field - 3, plane]
        return (material[plane] + 1).astype(f32)

    def fill(out, depths, at, total, first, nearest):
        for field in range(10):
            for step in range(depths[field]):
                values = source(field, first(depths[field]) + step)
                rounded = values.astype(bf16)
                out[at[field] + step] = rounded
                if field < 9 and step == nearest(depths[field]):
                    out[at[10] + field] = (values - rounded.astype(f32)).astype(bf16)
        for spare in range(total, out.shape[0]):
            out[spare] = jnp.zeros(out.shape[1:], bf16)

    def upper_face(out):
        fill(out, LOWER, LOWER_AT, LOWER_PLANES, lambda depth: planes - depth, lambda depth: depth - 1)

    def lower_face(out):
        fill(out, UPPER, UPPER_AT, UPPER_PLANES, lambda depth: 0, lambda depth: 0)

    @pl.when(odd[0] == 0)
    def _():
        lower_face(across)
        upper_face(within)

    @pl.when(odd[0] != 0)
    def _():
        upper_face(across)
        lower_face(within)


def looked_up(code, tables):
    results = [jnp.zeros(code.shape, f32) for _ in tables]
    for entry in range(tables[0][0].shape[0]):
        hit = code == entry + 1
        results = [jnp.where(hit, scale * table[entry], result) for (table, scale), result in zip(tables, results)]
    return results


def one_hot_sum(rows_of_cells, picked):
    row = lax.broadcasted_iota(jnp.int32, picked.shape, 0)
    return jnp.sum(jnp.where(row == rows_of_cells, picked, 0.0), axis=0, keepdims=True)


def lane_hits(lanes_of_cells, depth):
    lane = lax.broadcasted_iota(jnp.int32, (depth, lanes_of_cells.shape[1]), 0)
    return (lane == lanes_of_cells).astype(f32).astype(bf16)


def history_kernel(
    live, material, buoyancy_table, lame_table, shear_table, cells, weights, history, partial, fields, points
):
    slot = pl.program_id(0)
    product = functools.partial(jnp.dot, preferred_element_type=f32)

    @pl.when(slot == 0)
    def _():
        partial[...] = product(weights[0], history[0])
        tables = [(table, time_step) for table in (buoyancy_table, lame_table, shear_table)]
        for plane in range(material.shape[0]):
            fields[0, plane], fields[1, plane], fields[2, plane] = looked_up(material[plane] + 1, tables)
        depth = material.shape[0] * material.shape[1]
        lanes = material.shape[2]
        cell = cells[...]
        codes = (material[...].reshape(depth, lanes) + 1).astype(f32).astype(bf16)
        picked = product(codes, lane_hits(cell % lanes, lanes))
        code = one_hot_sum(cell // lanes, picked).astype(jnp.int32)
        lame, shear = looked_up(code, [(lame_table, 1.0), (shear_table, 1.0)])
        points[0:1] = lame / (3.0 * lame + 2.0 * shear)
        points[1:2] = 1.0 / (2.0 * shear)

    @pl.when((slot > 0) & (slot < live[0]))
    def _():
        partial[...] += product(weights[0], history[0])


def steps_kernel(
    live,
    odd,
    buoyancy_table,
    lame_table,
    shear_table,
    velocity,
    stress,
    fields,
    weights,
    across,
    within,
    cells,
    points,
    velocity_out,
    stress_out,
    tail,
    moving,
    pulling,
    factors,
    halos,
    split,
    samples,
    slips,
    halo_sems,
    slab_sems,
    slip_sem,
    out_sems,
):
    planes, rows, lanes = velocity.shape[1:]
    inner = pl.ds(RIM, rows)
    slab = pl.ds(EDGE, planes)

    halo_copies = [
        pltpu.make_async_copy(across, halos.at[odd[0]], halo_sems.at[0]),
        pltpu.make_async_copy(within, halos.at[1 - odd[0]], halo_sems.at[1]),
    ]
    slab_copies = [
        pltpu.make_async_copy(velocity, moving.at[:, slab, inner], slab_sems.at[0]),
        pltpu.make_async_copy(stress, pulling.at[:, slab, inner], slab_sems.at[1]),
        pltpu.make_async_copy(fields, factors.at[:, slab], slab_sems.at[2]),
    ]
    slip_copy = pltpu.make_async_copy(weights, slips, slip_sem)
    for copy in halo_copies + slab_copies:
        copy.start()

    def store(field, place, values):
        if field < 3:
            moving[field, place, inner] = values
        else:
            pulling[field - 3, place, inner] = values

    def read(field, place, at):
        return moving[field, place, at] if field < 3 else pulling[field - 3, place, at]

    blank = jnp.zeros((moving.shape[1], RIM, lanes), f32)
    for ref, fields_along_y in ((moving, (0, 1, 2)), (pulling, (SXY - 3, SYY - 3, SYZ - 3))):
        for field in fields_along_y:
            ref[field, :, 0:RIM] = blank
            ref[field, :, RIM + rows : 2 * RIM + rows] = blank

    cell = cells[...]
    hits = lane_hits(cell % lanes, lanes)
    hits = jnp.concatenate([hits, hits], axis=0)
    rows_of_cells = cell // lanes
    trace_part, compliance = points[0:1], points[1:2]

    for copy in halo_copies:
        copy.wait()
    tables = [(table, time_step) for table in (buoyancy_table, lame_table, shear_table)]
    for side, depths, at, nearest in ((0, LOWER, LOWER_AT, -1), (1, UPPER, UPPER_AT, 0)):
        for field in range(10):
            depth = depths[field]
            for step in range(depth):
                place = EDGE - depth + step if side == 0 else EDGE + planes + step
                values = halos[side, at[field] + step].astype(f32)
                if field < 9:
                    if step == nearest % depth:
                        values = values + halos[side, at[10] + field].astype(f32)
                    store(field, place, values)
                else:
                    kinds = 3 if EDGE - 3 <= place < EDGE + planes + 3 else 1
                    found = looked_up(values.astype(jnp.int32), tables[:kinds])
                    for kind in range(kinds):
                        factors[kind, place] = found[kind]

    lane = lax.broadcasted_iota(jnp.int32, (rows, lanes), 1)

    def combine(behind, here_low, here_high, ahead):
        return first_coef * (here_high - here_low) + second_coef * (ahead - behind)

    def along_x(field, place, forward):
        start = place - 1 if forward else place - 2
        return combine(*[read(field, start + step, inner) for step in range(4)])

    def along_y(field, place, forward):
        start = RIM - 1 if forward else RIM - 2
        return combine(*[read(field, place, pl.ds(start + step, rows)) for step in range(4)])

    def along_z(field, place, forward):
        here = read(field, place, inner)
        behind = jnp.where(lane >= 1, pltpu.roll(here, 1, 1), 0.0)
        ahead = jnp.where(lane < lanes - 1, pltpu.roll(here, lanes - 1, 1), 0.0)
        if forward:
            further = jnp.where(lane < lanes - 2, pltpu.roll(here, lanes - 2, 1), 0.0)
            return combine(behind, here, ahead, further)
        further = jnp.where(lane >= 2, pltpu.roll(here, 2, 1), 0.0)
        return combine(further, behind, here, ahead)

    def move(place, do_x=True, do_yz=True):
        buoyancy = factors[0, place]
        if do_x:
            pull = along_x(SXX, place, True) + along_y(SXY, place, False) + along_z(SXZ, place, False)
            store(VX, place, read(VX, place, inner) + buoyancy * pull)
        if do_yz:
            pull = along_x(SXY, place, False) + along_y(SYY, place, True) + along_z(SYZ, place, False)
            store(VY, place, read(VY, place, inner) + buoyancy * pull)
            pull = along_x(SXZ, place, False) + along_y(SYZ, place, False) + along_z(SZZ, place, True)
            store(VZ, place, read(VZ, place, inner) + buoyancy * pull)

    def strain(place, do_yz=True, keep=False):
        lame, shear = factors[1, place], factors[2, place]
        twice = 2.0 * shear
        exx = along_x(VX, place, False)
        eyy = along_y(VY, place, False)
        ezz = along_z(VZ, place, False)
        common = lame * (exx + eyy + ezz)
        changes = [(SXX, common + twice * exx)]
        changes.append((SXY, shear * (along_y(VX, place, True) + along_x(VY, place, True))))
        changes.append((SXZ, shear * (along_z(VX, place, True) + along_x(VZ, place, True))))
        if do_yz:
            changes.append((SYY, common + twice * eyy))
            changes.append((SZZ, common + twice * ezz))
            changes.append((SYZ, shear * (along_z(VY, place, True) + along_y(VZ, place, True))))
        for field, change in changes:
            values = read(field, place, inner) + change
            store(field, place, values)
            if keep:
                high = values.astype(bf16)
                at = pl.ds(pl.multiple_of((place - EDGE) * rows, rows), rows)
                split[field - 3, at, pl.ds(0, lanes)] = high
                split[field - 3, at, pl.ds(lanes, lanes)] = (values - high.astype(f32)).astype(bf16)

    def over(first, last, body, width=2):
        def group(index, carry):
            for step in range(width):
                body(EDGE + first + index * width + step)
            return carry

        lax.fori_loop(0, (last - first) // width, group, 0)

    def sample(part):
        picked = jnp.dot(split[part], hits, preferred_element_type=f32)
        samples[pl.ds(part, 1)] = one_hot_sum(rows_of_cells, picked)

    def new_strain():
        found = [samples[part : part + 1] for part in range(6)]
        shift = trace_part * (found[0] + found[1] + found[2])
        parts = [(found[part] - shift) * compliance for part in range(3)]
        parts += [found[part] * compliance for part in range(3, 6)]
        return [part.astype(bf16).astype(f32) for part in parts]

    for copy in slab_copies:
        copy.wait()
    slip_copy.start()

    top = EDGE + planes
    move(EDGE - 5, do_yz=False)
    move(top + 4, do_x=False)
    over(-4, planes + 4, move)
    for place in range(EDGE - 3, EDGE):
        strain(place, do_yz=place == EDGE - 1)
    over(0, planes, functools.partial(strain, keep=True))
    for place in range(top, top + 3):
        strain(place, do_yz=place < top + 2)

    move(EDGE - 2, do_yz=False)
    move(top + 1, do_x=False)

    def move_and_sample(index, carry):
        for step in range(2):
            move(EDGE - 1 + 2 * index + step)
        sample(index)
        return carry

    pairs = (planes + 2) // 2
    together = min(pairs, 6)
    lax.fori_loop(0, together, move_and_sample, 0)
    over(2 * together - 1, planes + 1, move)
    for part in range(together, 6):
        sample(part)
    first_sample = new_strain()
    out_copies = [
        pltpu.make_async_copy(moving.at[:, slab, inner], velocity_out, out_sems.at[0]),
        pltpu.make_async_copy(pulling.at[:, slab, inner], stress_out, out_sems.at[1]),
    ]
    out_copies[0].start()
    over(0, planes, functools.partial(strain, keep=True))
    out_copies[1].start()

    def sample_all(part, carry):
        sample(part)
        return carry

    lax.fori_loop(0, 6, sample_all, 0)
    second_sample = new_strain()

    slip_copy.wait()
    points_each = weights.shape[2] // 6
    new = jnp.zeros((8, weights.shape[1]), f32)
    for slot in range(weights.shape[0]):
        at = slice(slot * points_each, (slot + 1) * points_each)
        pair = jnp.concatenate(
            [jnp.concatenate([part[:, at] for part in sample], axis=1) for sample in (first_sample, second_sample)]
            + [jnp.zeros((6, weights.shape[2]), f32)],
            axis=0,
        )
        pair = jnp.where(slot < live[0], pair, 0.0).astype(bf16)
        new = new + lax.dot_general(pair, slips[slot], (((1,), (1,)), ((), ())), preferred_element_type=f32)
    pieces = weights.shape[1] // lanes
    lines = [new[which : which + 1, piece * lanes : (piece + 1) * lanes] for which in range(2) for piece in range(pieces)]
    lines = jnp.concatenate(lines + [jnp.zeros((8 - 2 * pieces, lanes), f32)], axis=0)
    for owner in range(tail.shape[0]):
        tail[owner] = lines
    for copy in out_copies:
        copy.wait()


def sum_kernel(partials, out):
    share, samples = out.shape
    total = partials[0:share]
    for device in range(1, partials.shape[0] // share):
        total = total + partials[device * share : (device + 1) * share]
    out[...] = jnp.concatenate([total[:, 2:], jnp.zeros((share, 2), f32)], axis=1)


def finish_kernel(place, older, tails, out):
    share, samples = out.shape
    lanes = tails.shape[2]
    new = tails[0]
    for device in range(1, tails.shape[0]):
        new = new + tails[device]
    ruptures = share * tails.shape[0]
    pieces = ruptures // lanes
    row = lax.broadcasted_iota(jnp.int32, (share, lanes), 0) + place[0] * share
    column = lax.broadcasted_iota(jnp.int32, (share, lanes), 1)
    sample = lax.broadcasted_iota(jnp.int32, (share, samples), 1)
    total = older[...]
    for which in range(2):
        values = jnp.zeros((share, lanes), f32)
        for piece in range(pieces):
            line = which * pieces + piece
            values = values + jnp.where(row == column + piece * lanes, new[line : line + 1], 0.0)
        values = jnp.sum(values, axis=1, keepdims=True)
        total = jnp.where(sample == samples - 2 + which, values, total)
    out[...] = total


def per_device(
    velocity,
    stress,
    material,
    buoyancy_table,
    lame_table,
    shear_table,
    fault_cells,
    block_count,
    strain_history,
    slip_weights,
):
    count = lax.axis_size("gx")
    planes, rows, lanes = material.shape
    slots, parts, points_each, samples = strain_history.shape
    ruptures = slip_weights.shape[1]
    share = ruptures // count
    spots = slots * points_each
    whole = pl.BlockSpec(memory_space=pltpu.VMEM)
    scalars = pl.BlockSpec(memory_space=pltpu.SMEM)
    anywhere = pl.BlockSpec(memory_space=pl.ANY)
    params = pltpu.CompilerParams(vmem_limit_bytes=60 * 1024 * 1024)
    place = lax.axis_index("gx").astype(jnp.int32).reshape(1)
    odd = place % 2

    halo = jax.ShapeDtypeStruct((max(LOWER_PLANES, UPPER_PLANES), rows, lanes), bf16)
    across, within = pl.pallas_call(
        pack_kernel,
        out_shape=(halo, halo),
        in_specs=[scalars] + [whole] * 3,
        out_specs=(whole, whole),
        compiler_params=params,
        name="pack_halos",
    )(odd, velocity, stress, material)
    pairs = [(i, i + 1) for i in range(1, count - 1, 2)]
    across = lax.ppermute(across, "gx", pairs + [(j, i) for i, j in pairs])
    pairs = [(i, i + 1) for i in range(0, count - 1, 2)]
    within = lax.ppermute(within, "gx", pairs + [(j, i) for i, j in pairs])

    cells = fault_cells.reshape(1, spots)
    history = strain_history.reshape(slots, parts * points_each, samples)

    def live_slot(slot, live):
        return (jnp.minimum(slot, live[0] - 1), 0, 0)

    def at_start(*shape):
        return pl.BlockSpec(shape, lambda slot, live: (0,) * len(shape))

    partial, fields, points = pl.pallas_call(
        history_kernel,
        grid_spec=pltpu.PrefetchScalarGridSpec(
            num_scalar_prefetch=1,
            grid=(slots,),
            in_specs=[
                at_start(planes, rows, lanes),
                scalars,
                scalars,
                scalars,
                at_start(1, spots),
                pl.BlockSpec((1, ruptures, parts * points_each), live_slot),
                pl.BlockSpec((1, parts * points_each, samples), live_slot),
            ],
            out_specs=[at_start(ruptures, samples), at_start(3, planes, rows, lanes), at_start(8, spots)],
        ),
        out_shape=(
            jax.ShapeDtypeStruct((ruptures, samples), f32),
            jax.ShapeDtypeStruct((3, planes, rows, lanes), f32),
            jax.ShapeDtypeStruct((8, spots), f32),
        ),
        compiler_params=params,
        cost_estimate=pl.CostEstimate(
            flops=2 * slots * ruptures * parts * points_each * samples,
            bytes_accessed=2 * (slip_weights.size + strain_history.size),
            transcendentals=0,
        ),
        name="history_product",
    )(block_count, material, buoyancy_table, lame_table, shear_table, cells, slip_weights, history)
    partials = lax.all_to_all(partial, "gx", 0, 0, tiled=True)

    extent = planes + 2 * EDGE
    velocity_two, stress_two, tail = pl.pallas_call(
        steps_kernel,
        out_shape=(
            jax.ShapeDtypeStruct(velocity.shape, f32),
            jax.ShapeDtypeStruct(stress.shape, f32),
            jax.ShapeDtypeStruct((count, 8, lanes), f32),
        ),
        in_specs=[scalars] * 5 + [anywhere] * 6 + [whole] * 2,
        out_specs=(anywhere, anywhere, whole),
        scratch_shapes=[
            pltpu.VMEM((3, extent, rows + 2 * RIM, lanes), f32),
            pltpu.VMEM((6, extent, rows + 2 * RIM, lanes), f32),
            pltpu.VMEM((3, extent, rows, lanes), f32),
            pltpu.VMEM((2, *halo.shape), bf16),
            pltpu.VMEM((6, planes * rows, 2 * lanes), bf16),
            pltpu.VMEM((8, spots), f32),
            pltpu.VMEM(slip_weights.shape, bf16),
            pltpu.SemaphoreType.DMA((2,)),
            pltpu.SemaphoreType.DMA((3,)),
            pltpu.SemaphoreType.DMA,
            pltpu.SemaphoreType.DMA((2,)),
        ],
        compiler_params=params,
        cost_estimate=pl.CostEstimate(flops=10**10, bytes_accessed=30 * 1024 * 1024, transcendentals=0),
        name="two_steps",
    )(
        block_count,
        odd,
        buoyancy_table,
        lame_table,
        shear_table,
        velocity,
        stress,
        fields,
        slip_weights,
        across,
        within,
        cells,
        points,
    )
    tails = lax.all_to_all(tail, "gx", 0, 0, tiled=True)

    older = pl.pallas_call(
        sum_kernel,
        out_shape=jax.ShapeDtypeStruct((share, samples), f32),
        in_specs=[whole],
        out_specs=whole,
        compiler_params=params,
        cost_estimate=pl.CostEstimate(flops=10**6, bytes_accessed=4 * 1024 * 1024, transcendentals=0),
        name="sum_partials",
    )(partials)
    seismograms = pl.pallas_call(
        finish_kernel,
        out_shape=jax.ShapeDtypeStruct((share, samples), f32),
        in_specs=[scalars, whole, whole],
        out_specs=whole,
        compiler_params=params,
        name="join_samples",
    )(place, older, tails)
    return (velocity_two, stress_two, seismograms)


def solution(mesh):
    in_specs = (
        P(None, ("site", "gx"), None, None),
        P(None, ("site", "gx"), None, None),
        P("gx", None, None),
        P(),
        P(),
        P(),
        P("gx", None),
        P("gx"),
        P(("site", "gx"), None, None, None),
        P("gx", None, None),
    )
    out_specs = (
        P(None, ("site", "gx"), None, None),
        P(None, ("site", "gx"), None, None),
        P(("site", "gx"), None),
    )
    return jax.shard_map(
        per_device, mesh=mesh, in_specs=in_specs, out_specs=out_specs, check_vma=False
    )
```

```python
import functools

import jax
import jax.numpy as jnp
from jax import lax
from jax.experimental import pallas as pl
from jax.experimental.pallas import tpu as pltpu
from jax.sharding import PartitionSpec as P

first_coef = 9.0 / 8.0
second_coef = -1.0 / 24.0
time_step = 0.4

VX, VY, VZ, SXX, SYY, SZZ, SXY, SXZ, SYZ, MAT = range(10)
LOWER = (5, 4, 4, 6, 4, 4, 6, 6, 4, 5)
UPPER = (4, 5, 5, 6, 5, 5, 6, 6, 5, 5)
EDGE = 6
RIM = 8
LOWER_AT = [sum(LOWER[:field]) for field in range(11)]
UPPER_AT = [sum(UPPER[:field]) for field in range(11)]
LOWER_PLANES = LOWER_AT[10] + 9
UPPER_PLANES = UPPER_AT[10] + 9

f32 = jnp.float32
bf16 = jnp.bfloat16


def pack_kernel(odd, velocity, stress, material, across, within):
    planes = velocity.shape[1]

    def source(field, plane):
        if field < 3:
            return velocity[field, plane]
        if field < 9:
            return stress[field - 3, plane]
        return (material[plane] + 1).astype(f32)

    def fill(out, depths, at, total, first, nearest):
        for field in range(10):
            for step in range(depths[field]):
                values = source(field, first(depths[field]) + step)
                rounded = values.astype(bf16)
                out[at[field] + step] = rounded
                if field < 9 and step == nearest(depths[field]):
                    out[at[10] + field] = (values - rounded.astype(f32)).astype(bf16)
        for spare in range(total, out.shape[0]):
            out[spare] = jnp.zeros(out.shape[1:], bf16)

    def upper_face(out):
        fill(out, LOWER, LOWER_AT, LOWER_PLANES, lambda depth: planes - depth, lambda depth: depth - 1)

    def lower_face(out):
        fill(out, UPPER, UPPER_AT, UPPER_PLANES, lambda depth: 0, lambda depth: 0)

    @pl.when(odd[0] == 0)
    def _():
        lower_face(across)
        upper_face(within)

    @pl.when(odd[0] != 0)
    def _():
        upper_face(across)
        lower_face(within)


def looked_up(code, tables):
    results = [jnp.zeros(code.shape, f32) for _ in tables]
    for entry in range(tables[0][0].shape[0]):
        hit = code == entry + 1
        results = [jnp.where(hit, scale * table[entry], result) for (table, scale), result in zip(tables, results)]
    return results


def one_hot_sum(rows_of_cells, picked):
    row = lax.broadcasted_iota(jnp.int32, picked.shape, 0)
    return jnp.sum(jnp.where(row == rows_of_cells, picked, 0.0), axis=0, keepdims=True)


def lane_hits(lanes_of_cells, depth):
    lane = lax.broadcasted_iota(jnp.int32, (depth, lanes_of_cells.shape[1]), 0)
    return (lane == lanes_of_cells).astype(f32).astype(bf16)


def history_kernel(
    live, odd, weights, history, kept, sent, live_here, odd_here, slips, records, total, count_sems, slip_sems, record_sems
):
    slots = weights.shape[0]
    scalar_copies = [
        pltpu.make_async_copy(live, live_here, count_sems.at[0]),
        pltpu.make_async_copy(odd, odd_here, count_sems.at[1]),
    ]
    copies = [
        (
            pltpu.make_async_copy(weights.at[slot], slips.at[slot], slip_sems.at[slot]),
            pltpu.make_async_copy(history.at[slot], records.at[slot], record_sems.at[slot]),
        )
        for slot in range(slots)
    ]
    for copy in scalar_copies:
        copy.start()
    for copy in copies[0]:
        copy.start()
    for copy in scalar_copies:
        copy.wait()
    for slot in range(1, slots):

        @pl.when(slot < live_here[0])
        def _(slot=slot):
            for copy in copies[slot]:
                copy.start()

    for slot in range(slots):

        @pl.when(slot < live_here[0])
        def _(slot=slot):
            for copy in copies[slot]:
                copy.wait()
            product = jnp.dot(slips[slot], records[slot], preferred_element_type=f32)
            if slot == 0:
                total[...] = product
            else:
                total[...] += product

    share = kept.shape[1]
    for pair in range(kept.shape[0]):
        even = total[2 * pair * share : (2 * pair + 1) * share]
        other = total[(2 * pair + 1) * share : (2 * pair + 2) * share]
        kept[pair] = jnp.where(odd_here[0] == 0, even, other)
        sent[pair] = jnp.where(odd_here[0] == 0, other, even)


def add_kernel(first, second, out):
    out[...] = first[...] + second[...]


def model_kernel(after, material, buoyancy_table, lame_table, shear_table, cells, fields, points):
    del after
    tables = [(table, time_step) for table in (buoyancy_table, lame_table, shear_table)]
    for plane in range(material.shape[0]):
        fields[0, plane], fields[1, plane], fields[2, plane] = looked_up(material[plane] + 1, tables)
    depth = material.shape[0] * material.shape[1]
    lanes = material.shape[2]
    cell = cells[...]
    codes = (material[...].reshape(depth, lanes) + 1).astype(f32).astype(bf16)
    picked = jnp.dot(codes, lane_hits(cell % lanes, lanes), preferred_element_type=f32)
    code = one_hot_sum(cell // lanes, picked).astype(jnp.int32)
    lame, shear = looked_up(code, [(lame_table, 1.0), (shear_table, 1.0)])
    points[0:1] = lame / (3.0 * lame + 2.0 * shear)
    points[1:2] = 1.0 / (2.0 * shear)


def steps_kernel(
    live,
    odd,
    buoyancy_table,
    lame_table,
    shear_table,
    velocity,
    stress,
    fields,
    weights,
    across,
    within,
    cells,
    points,
    velocity_out,
    stress_out,
    tail,
    moving,
    pulling,
    factors,
    halos,
    split,
    samples,
    slips,
    halo_sems,
    slab_sems,
    slip_sem,
    out_sems,
):
    planes, rows, lanes = velocity.shape[1:]
    inner = pl.ds(RIM, rows)
    slab = pl.ds(EDGE, planes)

    halo_copies = [
        pltpu.make_async_copy(across, halos.at[odd[0]], halo_sems.at[0]),
        pltpu.make_async_copy(within, halos.at[1 - odd[0]], halo_sems.at[1]),
    ]
    slab_copies = [
        pltpu.make_async_copy(velocity, moving.at[:, slab, inner], slab_sems.at[0]),
        pltpu.make_async_copy(stress, pulling.at[:, slab, inner], slab_sems.at[1]),
        pltpu.make_async_copy(fields, factors.at[:, slab], slab_sems.at[2]),
    ]
    slip_copy = pltpu.make_async_copy(weights, slips, slip_sem)
    for copy in halo_copies + slab_copies:
        copy.start()

    def store(field, place, values):
        if field < 3:
            moving[field, place, inner] = values
        else:
            pulling[field - 3, place, inner] = values

    def read(field, place, at):
        return moving[field, place, at] if field < 3 else pulling[field - 3, place, at]

    blank = jnp.zeros((moving.shape[1], RIM, lanes), f32)
    for ref, fields_along_y in ((moving, (0, 1, 2)), (pulling, (SXY - 3, SYY - 3, SYZ - 3))):
        for field in fields_along_y:
            ref[field, :, 0:RIM] = blank
            ref[field, :, RIM + rows : 2 * RIM + rows] = blank

    cell = cells[...]
    hits = lane_hits(cell % lanes, lanes)
    hits = jnp.concatenate([hits, hits], axis=0)
    rows_of_cells = cell // lanes
    trace_part, compliance = points[0:1], points[1:2]

    for copy in halo_copies:
        copy.wait()
    tables = [(table, time_step) for table in (buoyancy_table, lame_table, shear_table)]
    for side, depths, at, nearest in ((0, LOWER, LOWER_AT, -1), (1, UPPER, UPPER_AT, 0)):
        for field in range(10):
            depth = depths[field]
            for step in range(depth):
                place = EDGE - depth + step if side == 0 else EDGE + planes + step
                values = halos[side, at[field] + step].astype(f32)
                if field < 9:
                    if step == nearest % depth:
                        values = values + halos[side, at[10] + field].astype(f32)
                    store(field, place, values)
                else:
                    kinds = 3 if EDGE - 3 <= place < EDGE + planes + 3 else 1
                    found = looked_up(values.astype(jnp.int32), tables[:kinds])
                    for kind in range(kinds):
                        factors[kind, place] = found[kind]

    lane = lax.broadcasted_iota(jnp.int32, (rows, lanes), 1)

    def combine(behind, here_low, here_high, ahead):
        return first_coef * (here_high - here_low) + second_coef * (ahead - behind)

    def along_x(field, place, forward):
        start = place - 1 if forward else place - 2
        return combine(*[read(field, start + step, inner) for step in range(4)])

    nothing = jnp.minimum(live[0], 0)

    def along_y(field, place, forward):
        start = nothing + (RIM - 1 if forward else RIM - 2)
        return combine(*[read(field, place, pl.ds(start + step, rows)) for step in range(4)])

    def along_z(field, place, forward):
        here = read(field, place, inner)
        behind = jnp.where(lane >= 1, pltpu.roll(here, 1, 1), 0.0)
        ahead = jnp.where(lane < lanes - 1, pltpu.roll(here, lanes - 1, 1), 0.0)
        if forward:
            further = jnp.where(lane < lanes - 2, pltpu.roll(here, lanes - 2, 1), 0.0)
            return combine(behind, here, ahead, further)
        further = jnp.where(lane >= 2, pltpu.roll(here, 2, 1), 0.0)
        return combine(further, behind, here, ahead)

    def move(place, do_x=True, do_yz=True):
        buoyancy = factors[0, place]
        if do_x:
            pull = along_x(SXX, place, True) + along_y(SXY, place, False) + along_z(SXZ, place, False)
            store(VX, place, read(VX, place, inner) + buoyancy * pull)
        if do_yz:
            pull = along_x(SXY, place, False) + along_y(SYY, place, True) + along_z(SYZ, place, False)
            store(VY, place, read(VY, place, inner) + buoyancy * pull)
            pull = along_x(SXZ, place, False) + along_y(SYZ, place, False) + along_z(SZZ, place, True)
            store(VZ, place, read(VZ, place, inner) + buoyancy * pull)

    def strain(place, do_yz=True, keep=False):
        lame, shear = factors[1, place], factors[2, place]
        twice = 2.0 * shear
        exx = along_x(VX, place, False)
        eyy = along_y(VY, place, False)
        ezz = along_z(VZ, place, False)
        common = lame * (exx + eyy + ezz)
        changes = [(SXX, common + twice * exx)]
        changes.append((SXY, shear * (along_y(VX, place, True) + along_x(VY, place, True))))
        changes.append((SXZ, shear * (along_z(VX, place, True) + along_x(VZ, place, True))))
        if do_yz:
            changes.append((SYY, common + twice * eyy))
            changes.append((SZZ, common + twice * ezz))
            changes.append((SYZ, shear * (along_z(VY, place, True) + along_y(VZ, place, True))))
        for field, change in changes:
            values = read(field, place, inner) + change
            store(field, place, values)
            if keep:
                high = values.astype(bf16)
                at = pl.ds(pl.multiple_of((place - EDGE) * rows, rows), rows)
                split[field - 3, at, pl.ds(0, lanes)] = high
                split[field - 3, at, pl.ds(lanes, lanes)] = (values - high.astype(f32)).astype(bf16)

    def over(first, last, body, width=2):
        def group(index, carry):
            for step in range(width):
                body(EDGE + first + index * width + step)
            return carry

        lax.fori_loop(0, (last - first) // width, group, 0)

    def sample(part):
        picked = jnp.dot(split[part], hits, preferred_element_type=f32)
        samples[pl.ds(part, 1)] = one_hot_sum(rows_of_cells, picked)

    def new_strain():
        found = [samples[part : part + 1] for part in range(6)]
        shift = trace_part * (found[0] + found[1] + found[2])
        parts = [(found[part] - shift) * compliance for part in range(3)]
        parts += [found[part] * compliance for part in range(3, 6)]
        return [part.astype(bf16).astype(f32) for part in parts]

    for copy in slab_copies:
        copy.wait()
    slip_copy.start()

    top = EDGE + planes
    move(EDGE - 5, do_yz=False)
    move(top + 4, do_x=False)
    over(-4, planes + 4, move)
    for place in range(EDGE - 3, EDGE):
        strain(place, do_yz=place == EDGE - 1)
    over(0, planes, functools.partial(strain, keep=True))
    for place in range(top, top + 3):
        strain(place, do_yz=place < top + 2)

    move(EDGE - 2, do_yz=False)
    move(top + 1, do_x=False)

    def move_and_sample(index, carry):
        for step in range(2):
            move(EDGE - 1 + 2 * index + step)
        sample(index)
        return carry

    pairs = (planes + 2) // 2
    together = min(pairs, 6)
    lax.fori_loop(0, together, move_and_sample, 0)
    over(2 * together - 1, planes + 1, move)
    for part in range(together, 6):
        sample(part)
    first_sample = new_strain()
    out_copies = [
        pltpu.make_async_copy(moving.at[:, slab, inner], velocity_out, out_sems.at[0]),
        pltpu.make_async_copy(pulling.at[:, slab, inner], stress_out, out_sems.at[1]),
    ]
    out_copies[0].start()
    over(0, planes, functools.partial(strain, keep=True))
    out_copies[1].start()

    def sample_all(part, carry):
        sample(part)
        return carry

    lax.fori_loop(0, 6, sample_all, 0)
    second_sample = new_strain()

    slip_copy.wait()
    points_each = weights.shape[2] // 6
    new = jnp.zeros((8, weights.shape[1]), f32)
    for slot in range(weights.shape[0]):
        at = slice(slot * points_each, (slot + 1) * points_each)
        pair = jnp.concatenate(
            [jnp.concatenate([part[:, at] for part in sample], axis=1) for sample in (first_sample, second_sample)]
            + [jnp.zeros((6, weights.shape[2]), f32)],
            axis=0,
        )
        pair = jnp.where(slot < live[0], pair, 0.0).astype(bf16)
        new = new + lax.dot_general(pair, slips[slot], (((1,), (1,)), ((), ())), preferred_element_type=f32)
    pieces = weights.shape[1] // lanes
    lines = [new[which : which + 1, piece * lanes : (piece + 1) * lanes] for which in range(2) for piece in range(pieces)]
    lines = jnp.concatenate(lines + [jnp.zeros((8 - 2 * pieces, lanes), f32)], axis=0)
    for owner in range(tail.shape[0]):
        tail[owner] = lines
    for copy in out_copies:
        copy.wait()


def sum_kernel(partials, out):
    share, samples = out.shape
    total = partials[0]
    for chip in range(1, partials.shape[0]):
        total = total + partials[chip]
    out[...] = jnp.concatenate([total[:, 2:], jnp.zeros((share, 2), f32)], axis=1)


def finish_kernel(place, older, tails, out):
    share, samples = out.shape
    lanes = tails.shape[2]
    new = tails[0]
    for device in range(1, tails.shape[0]):
        new = new + tails[device]
    ruptures = share * tails.shape[0]
    pieces = ruptures // lanes
    row = lax.broadcasted_iota(jnp.int32, (share, lanes), 0) + place[0] * share
    column = lax.broadcasted_iota(jnp.int32, (share, lanes), 1)
    sample = lax.broadcasted_iota(jnp.int32, (share, samples), 1)
    total = older[...]
    for which in range(2):
        values = jnp.zeros((share, lanes), f32)
        for piece in range(pieces):
            line = which * pieces + piece
            values = values + jnp.where(row == column + piece * lanes, new[line : line + 1], 0.0)
        values = jnp.sum(values, axis=1, keepdims=True)
        total = jnp.where(sample == samples - 2 + which, values, total)
    out[...] = total


def per_device(
    velocity,
    stress,
    material,
    buoyancy_table,
    lame_table,
    shear_table,
    fault_cells,
    block_count,
    strain_history,
    slip_weights,
):
    count = lax.axis_size("gx")
    planes, rows, lanes = material.shape
    slots, parts, points_each, samples = strain_history.shape
    ruptures = slip_weights.shape[1]
    share = ruptures // count
    spots = slots * points_each
    whole = pl.BlockSpec(memory_space=pltpu.VMEM)
    scalars = pl.BlockSpec(memory_space=pltpu.SMEM)
    anywhere = pl.BlockSpec(memory_space=pl.ANY)
    params = pltpu.CompilerParams(vmem_limit_bytes=60 * 1024 * 1024)
    small = pltpu.CompilerParams(vmem_limit_bytes=8 * 1024 * 1024)
    place = lax.axis_index("gx").astype(jnp.int32).reshape(1)
    odd = place % 2

    halo = jax.ShapeDtypeStruct((max(LOWER_PLANES, UPPER_PLANES), rows, lanes), bf16)
    across, within = pl.pallas_call(
        pack_kernel,
        out_shape=(halo, halo),
        in_specs=[scalars] + [whole] * 3,
        out_specs=(whole, whole),
        compiler_params=params,
        name="pack_halos",
    )(odd, velocity, stress, material)
    pairs = [(i, i + 1) for i in range(1, count - 1, 2)]
    across = lax.ppermute(across, "gx", pairs + [(j, i) for i, j in pairs])
    pairs = [(i, i + 1) for i in range(0, count - 1, 2)]
    within = lax.ppermute(within, "gx", pairs + [(j, i) for i, j in pairs])

    cells = fault_cells.reshape(1, spots)
    history = strain_history.reshape(slots, parts * points_each, samples)
    half = jax.ShapeDtypeStruct((count // 2, share, samples), f32)
    kept, sent = pl.pallas_call(
        history_kernel,
        out_shape=(half, half),
        in_specs=[anywhere] * 4,
        out_specs=(whole, whole),
        scratch_shapes=[
            pltpu.SMEM((1,), jnp.int32),
            pltpu.SMEM((1,), jnp.int32),
            pltpu.VMEM(slip_weights.shape, bf16),
            pltpu.VMEM(history.shape, bf16),
            pltpu.VMEM((ruptures, samples), f32),
            pltpu.SemaphoreType.DMA((2,)),
            pltpu.SemaphoreType.DMA((slots,)),
            pltpu.SemaphoreType.DMA((slots,)),
        ],
        compiler_params=params,
        cost_estimate=pl.CostEstimate(
            flops=2 * slots * ruptures * parts * points_each * samples,
            bytes_accessed=2 * (slip_weights.size + strain_history.size),
            transcendentals=0,
        ),
        name="history_product",
    )(block_count, odd, slip_weights, history)
    received = lax.ppermute(sent, "gx", pairs + [(j, i) for i, j in pairs])
    fields, points = pl.pallas_call(
        model_kernel,
        out_shape=(
            jax.ShapeDtypeStruct((3, planes, rows, lanes), f32),
            jax.ShapeDtypeStruct((8, spots), f32),
        ),
        in_specs=[anywhere, whole, scalars, scalars, scalars, whole],
        out_specs=(whole, whole),
        compiler_params=params,
        cost_estimate=pl.CostEstimate(flops=10**9, bytes_accessed=4 * 1024 * 1024, transcendentals=0),
        name="model_fields",
    )(kept, material, buoyancy_table, lame_table, shear_table, cells)
    chip_sum = pl.pallas_call(
        add_kernel,
        out_shape=half,
        in_specs=[whole] * 2,
        out_specs=whole,
        compiler_params=params,
        cost_estimate=pl.CostEstimate(flops=10**6, bytes_accessed=4 * 1024 * 1024, transcendentals=0),
        name="add_cores",
    )(kept, received)
    same_core = [list(range(core, count, 2)) for core in range(2)]
    partials = lax.all_to_all(chip_sum, "gx", 0, 0, axis_index_groups=same_core, tiled=True)

    extent = planes + 2 * EDGE
    velocity_two, stress_two, tail = pl.pallas_call(
        steps_kernel,
        out_shape=(
            jax.ShapeDtypeStruct(velocity.shape, f32),
            jax.ShapeDtypeStruct(stress.shape, f32),
            jax.ShapeDtypeStruct((count, 8, lanes), f32),
        ),
        in_specs=[scalars] * 5 + [anywhere] * 6 + [whole] * 2,
        out_specs=(anywhere, anywhere, whole),
        scratch_shapes=[
            pltpu.VMEM((3, extent, rows + 2 * RIM, lanes), f32),
            pltpu.VMEM((6, extent, rows + 2 * RIM, lanes), f32),
            pltpu.VMEM((3, extent, rows, lanes), f32),
            pltpu.VMEM((2, *halo.shape), bf16),
            pltpu.VMEM((6, planes * rows, 2 * lanes), bf16),
            pltpu.VMEM((8, spots), f32),
            pltpu.VMEM(slip_weights.shape, bf16),
            pltpu.SemaphoreType.DMA((2,)),
            pltpu.SemaphoreType.DMA((3,)),
            pltpu.SemaphoreType.DMA,
            pltpu.SemaphoreType.DMA((2,)),
        ],
        compiler_params=params,
        cost_estimate=pl.CostEstimate(flops=10**10, bytes_accessed=30 * 1024 * 1024, transcendentals=0),
        name="two_steps",
    )(
        block_count,
        odd,
        buoyancy_table,
        lame_table,
        shear_table,
        velocity,
        stress,
        fields,
        slip_weights,
        across,
        within,
        cells,
        points,
    )
    tails = lax.all_to_all(tail, "gx", 0, 0, tiled=True)

    older = pl.pallas_call(
        sum_kernel,
        out_shape=jax.ShapeDtypeStruct((share, samples), f32),
        in_specs=[whole],
        out_specs=whole,
        compiler_params=small,
        cost_estimate=pl.CostEstimate(flops=10**6, bytes_accessed=4 * 1024 * 1024, transcendentals=0),
        name="sum_partials",
    )(partials)
    seismograms = pl.pallas_call(
        finish_kernel,
        out_shape=jax.ShapeDtypeStruct((share, samples), f32),
        in_specs=[scalars, whole, whole],
        out_specs=whole,
        compiler_params=small,
        name="join_samples",
    )(place, older, tails)
    return (velocity_two, stress_two, seismograms)


def solution(mesh):
    in_specs = (
        P(None, ("site", "gx"), None, None),
        P(None, ("site", "gx"), None, None),
        P("gx", None, None),
        P(),
        P(),
        P(),
        P("gx", None),
        P("gx"),
        P(("site", "gx"), None, None, None),
        P("gx", None, None),
    )
    out_specs = (
        P(None, ("site", "gx"), None, None),
        P(None, ("site", "gx"), None, None),
        P(("site", "gx"), None),
    )
    return jax.shard_map(
        per_device, mesh=mesh, in_specs=in_specs, out_specs=out_specs, check_vma=False
    )
```

```python
import functools

import jax
import jax.numpy as jnp
from jax import lax
from jax.experimental import pallas as pl
from jax.experimental.pallas import tpu as pltpu
from jax.sharding import PartitionSpec as P

time_step = 0.4
scale = time_step / 24.0

VX, VY, VZ, SXX, SYY, SZZ, SXY, SXZ, SYZ, MAT = range(10)
LOWER = (5, 4, 4, 6, 4, 4, 6, 6, 4, 5)
UPPER = (4, 5, 5, 6, 5, 5, 6, 6, 5, 5)
EDGE = 6
RIM = 8
LOWER_AT = [sum(LOWER[:field]) for field in range(11)]
UPPER_AT = [sum(UPPER[:field]) for field in range(11)]
LOWER_PLANES = LOWER_AT[10] + 9
UPPER_PLANES = UPPER_AT[10] + 9

f32 = jnp.float32
bf16 = jnp.bfloat16


def second_core():
    return lax.axis_index("gx") % 2


def pack_kernel(velocity, stress, material, across, within):
    planes = velocity.shape[1]
    odd = second_core()

    def source(field, plane):
        if field < 3:
            return velocity[field, plane]
        if field < 9:
            return stress[field - 3, plane]
        return (material[plane] + 1).astype(f32)

    def fill(out, depths, at, total, first, nearest):
        for field in range(10):
            for step in range(depths[field]):
                values = source(field, first(depths[field]) + step)
                rounded = values.astype(bf16)
                out[at[field] + step] = rounded
                if field < 9 and step == nearest(depths[field]):
                    out[at[10] + field] = (values - rounded.astype(f32)).astype(bf16)
        for spare in range(total, out.shape[0]):
            out[spare] = jnp.zeros(out.shape[1:], bf16)

    def upper_face(out):
        fill(out, LOWER, LOWER_AT, LOWER_PLANES, lambda depth: planes - depth, lambda depth: depth - 1)

    def lower_face(out):
        fill(out, UPPER, UPPER_AT, UPPER_PLANES, lambda depth: 0, lambda depth: 0)

    @pl.when(odd == 0)
    def _():
        lower_face(across)
        upper_face(within)

    @pl.when(odd != 0)
    def _():
        upper_face(across)
        lower_face(within)


def looked_up(code, tables):
    results = [jnp.zeros(code.shape, f32) for _ in tables]
    for entry in range(tables[0].shape[0]):
        hit = code == entry + 1
        results = [jnp.where(hit, table[entry], result) for table, result in zip(tables, results)]
    return results


def history_kernel(live, weights, history, kept, sent, live_here, slips, records, total, live_sem, slip_sems, record_sems):
    slots = weights.shape[0]
    live_copy = pltpu.make_async_copy(live, live_here, live_sem)
    copies = [
        (
            pltpu.make_async_copy(weights.at[slot], slips.at[slot], slip_sems.at[slot]),
            pltpu.make_async_copy(history.at[slot], records.at[slot], record_sems.at[slot]),
        )
        for slot in range(slots)
    ]
    live_copy.start()
    for copy in copies[0]:
        copy.start()
    live_copy.wait()
    for slot in range(1, slots):

        @pl.when(slot < live_here[0])
        def _(slot=slot):
            for copy in copies[slot]:
                copy.start()

    for copy in copies[0]:
        copy.wait()
    total[...] = jnp.dot(slips[0], records[0], preferred_element_type=f32)
    for slot in range(1, slots):

        @pl.when(slot < live_here[0])
        def _(slot=slot):
            for copy in copies[slot]:
                copy.wait()
            total[...] += jnp.dot(slips[slot], records[slot], preferred_element_type=f32)

    share = kept.shape[1]
    odd = second_core()
    for pair in range(kept.shape[0]):
        even = total[2 * pair * share : (2 * pair + 1) * share]
        other = total[(2 * pair + 1) * share : (2 * pair + 2) * share]
        kept[pair] = jnp.where(odd == 0, even, other)
        sent[pair] = jnp.where(odd == 0, other, even)


def add_kernel(first, second, out):
    out[...] = first[...] + second[...]


def spread_kernel(first, second, out):
    total = first[...] + second[...]
    for chip in range(out.shape[0]):
        out[chip] = total


def fetch_all(sources, targets, sems):
    copies = [
        pltpu.make_async_copy(source, target, sems.at[index])
        for index, (source, target) in enumerate(zip(sources, targets))
    ]
    for copy in copies:
        copy.start()
    return copies


def model_kernel(after, material, buoyancy_from, lame_from, shear_from, fields, buoyancy_table, lame_table, shear_table, sems):
    del after
    tables = (buoyancy_table, lame_table, shear_table)
    for copy in fetch_all((buoyancy_from, lame_from, shear_from), tables, sems):
        copy.wait()
    for plane in range(material.shape[0]):
        code = material[plane] + 1
        buoyancy, lame, shear = looked_up(code, tables)
        fields[0, plane] = scale * buoyancy
        fields[1, plane] = scale * lame
        fields[2, plane] = scale * shear
        fields[3, plane] = lame / (3.0 * lame + 2.0 * shear)
        fields[4, plane] = 1.0 / (2.0 * shear)


def steps_kernel(
    live_from,
    cells_from,
    buoyancy_from,
    lame_from,
    shear_from,
    velocity,
    stress,
    weights,
    fields,
    across,
    within,
    velocity_out,
    stress_out,
    tail,
    moving,
    pulling,
    factors,
    strains,
    slips,
    live,
    cells,
    buoyancy_table,
    lame_table,
    shear_table,
    scalar_sems,
    slab_sems,
    slip_sem,
    out_sems,
):
    planes, rows, lanes = velocity.shape[1:]
    tables = (buoyancy_table, lame_table, shear_table)
    scalar_copies = fetch_all(
        (live_from, cells_from, buoyancy_from, lame_from, shear_from), (live, cells, *tables), scalar_sems
    )
    inner = pl.ds(RIM, rows)
    slab = pl.ds(EDGE, planes)
    odd = second_core()

    slab_copies = [
        pltpu.make_async_copy(stress, pulling.at[:, slab, inner], slab_sems.at[0]),
        pltpu.make_async_copy(velocity, moving.at[:, slab, inner], slab_sems.at[1]),
    ]
    slip_copy = pltpu.make_async_copy(weights, slips, slip_sem)
    for copy in slab_copies:
        copy.start()
    slip_copy.start()

    def store(field, place, values):
        if field < 3:
            moving[field, place, inner] = values
        else:
            pulling[field - 3, place, inner] = values

    def read(field, place, at):
        return moving[field, place, at] if field < 3 else pulling[field - 3, place, at]

    blank = jnp.zeros((moving.shape[1], RIM, lanes), f32)
    for ref, fields_along_y in ((moving, (0, 1, 2)), (pulling, (SXY - 3, SYY - 3, SYZ - 3))):
        for field in fields_along_y:
            ref[field, :, 0:RIM] = blank
            ref[field, :, RIM + rows : 2 * RIM + rows] = blank

    for kind in range(3):
        factors[kind, slab] = fields[kind]
    for copy in scalar_copies:
        copy.wait()

    def unpack(halo, upper):
        depths, at = (UPPER, UPPER_AT) if upper else (LOWER, LOWER_AT)
        for field in range(10):
            depth = depths[field]
            for step in range(depth):
                place = EDGE + planes + step if upper else EDGE - depth + step
                values = halo[at[field] + step].astype(f32)
                if field < 9:
                    if step == (0 if upper else depth - 1):
                        values = values + halo[at[10] + field].astype(f32)
                    store(field, place, values)
                else:
                    kinds = 3 if EDGE - 3 <= place < EDGE + planes + 3 else 1
                    found = looked_up(values.astype(jnp.int32), tables[:kinds])
                    for kind in range(kinds):
                        factors[kind, place] = scale * found[kind]

    @pl.when(odd == 0)
    def _():
        unpack(across, False)
        unpack(within, True)

    @pl.when(odd != 0)
    def _():
        unpack(within, False)
        unpack(across, True)

    lane = lax.broadcasted_iota(jnp.int32, (rows, lanes), 1)

    def parts_of(behind, here_low, here_high, ahead):
        return here_high - here_low, ahead - behind

    def along_x(field, place, forward):
        start = place - 1 if forward else place - 2
        return parts_of(*[read(field, start + step, inner) for step in range(4)])

    def along_y(field, place, forward):
        start = RIM - 1 if forward else RIM - 2
        return parts_of(*[read(field, place, pl.ds(start + step, rows)) for step in range(4)])

    def along_z(field, place, forward):
        here = read(field, place, inner)
        behind = jnp.where(lane >= 1, pltpu.roll(here, 1, 1), 0.0)
        ahead = jnp.where(lane < lanes - 1, pltpu.roll(here, lanes - 1, 1), 0.0)
        if forward:
            further = jnp.where(lane < lanes - 2, pltpu.roll(here, lanes - 2, 1), 0.0)
            return parts_of(behind, here, ahead, further)
        further = jnp.where(lane >= 2, pltpu.roll(here, 2, 1), 0.0)
        return parts_of(further, behind, here, ahead)

    def joined(*parts):
        near, far = parts[0]
        for more_near, more_far in parts[1:]:
            near, far = near + more_near, far + more_far
        return 27.0 * near - far

    def move(place, do_x=True, do_yz=True):
        buoyancy = factors[0, place]
        pulls = []
        if do_x:
            pulls.append((VX, along_x(SXX, place, True), along_y(SXY, place, False), along_z(SXZ, place, False)))
        if do_yz:
            pulls.append((VY, along_x(SXY, place, False), along_y(SYY, place, True), along_z(SYZ, place, False)))
            pulls.append((VZ, along_x(SXZ, place, False), along_y(SYZ, place, False), along_z(SZZ, place, True)))
        results = [(field, read(field, place, inner) + buoyancy * joined(*parts)) for field, *parts in pulls]
        for field, values in results:
            store(field, place, values)

    def strain(place, do_yz=True, keep=None):
        lame, shear = factors[1, place], factors[2, place]
        twice = 2.0 * shear
        exx = joined(along_x(VX, place, False))
        eyy = joined(along_y(VY, place, False))
        ezz = joined(along_z(VZ, place, False))
        common = lame * (exx + eyy + ezz)
        changes = [(SXX, common + twice * exx)]
        changes.append((SXY, shear * joined(along_y(VX, place, True), along_x(VY, place, True))))
        changes.append((SXZ, shear * joined(along_z(VX, place, True), along_x(VZ, place, True))))
        if do_yz:
            changes.append((SYY, common + twice * eyy))
            changes.append((SZZ, common + twice * ezz))
            changes.append((SYZ, shear * joined(along_z(VY, place, True), along_y(VZ, place, True))))
        results = {field: read(field, place, inner) + change for field, change in changes}
        for field, values in results.items():
            store(field, place, values)
        if keep is not None:
            compliance = fields[4, place - EDGE]
            shift = fields[3, place - EDGE] * (results[SXX] + results[SYY] + results[SZZ])
            first = pl.multiple_of((place - EDGE) * (8 * rows), 8 * rows)
            for field in range(3, 9):
                values = results[field] - shift if field < 6 else results[field]
                strains[keep, pl.ds(first + field - 3, rows, stride=8)] = values * compliance

    def over(first, last, body, width=2):
        def group(index, carry):
            for step in range(width):
                body(EDGE + first + index * width + step)
            return carry

        lax.fori_loop(0, (last - first) // width, group, 0)

    for copy in slab_copies:
        copy.wait()
    top = EDGE + planes
    move(EDGE - 5, do_yz=False)
    move(top + 4, do_x=False)
    over(-4, planes + 4, move)
    for place in range(EDGE - 3, EDGE):
        strain(place, do_yz=place == EDGE - 1)
    over(0, planes, functools.partial(strain, keep=0))
    for place in range(top, top + 3):
        strain(place, do_yz=place < top + 2)
    move(EDGE - 2, do_yz=False)
    move(top + 1, do_x=False)
    over(-1, planes + 1, move)
    out_copies = [
        pltpu.make_async_copy(moving.at[:, slab, inner], velocity_out, out_sems.at[0]),
        pltpu.make_async_copy(pulling.at[:, slab, inner], stress_out, out_sems.at[1]),
    ]
    out_copies[0].start()
    over(0, planes, functools.partial(strain, keep=1))
    out_copies[1].start()

    slip_copy.wait()
    points_each = cells.shape[1]
    tall = lax.broadcasted_iota(jnp.int32, (8, lanes), 1)

    def add_slot(slot, new):
        found = [jnp.zeros((8, lanes), f32) for _ in range(2)]
        for point in range(points_each):
            cell = cells[slot, point]
            first = pl.multiple_of((cell // lanes) * 8, 8)
            shift = (point + lanes - cell % lanes) % lanes
            hit = tall == point
            for which in range(2):
                turned = pltpu.roll(strains[which, pl.ds(first, 8)], shift, 1)
                found[which] = jnp.where(hit, turned, found[which])
        pair = [jnp.concatenate([values[part : part + 1] for part in range(6)], axis=1) for values in found]
        pair = jnp.concatenate(pair + [jnp.zeros((6, 6 * points_each), f32)], axis=0).astype(bf16)
        return new + lax.dot_general(pair, slips[slot], (((1,), (1,)), ((), ())), preferred_element_type=f32)

    new = lax.fori_loop(0, live[0], add_slot, jnp.zeros((8, weights.shape[1]), f32))
    pieces = weights.shape[1] // lanes
    for which in range(2):
        for piece in range(pieces):
            line = which * pieces + piece
            tail[line : line + 1] = new[which : which + 1, piece * lanes : (piece + 1) * lanes]
    tail[2 * pieces :] = jnp.zeros((8 - 2 * pieces, lanes), f32)
    for copy in out_copies:
        copy.wait()


def sum_kernel(partials, out):
    share, samples = out.shape
    total = partials[0]
    for chip in range(1, partials.shape[0]):
        total = total + partials[chip]
    out[...] = jnp.concatenate([total[:, 2:], jnp.zeros((share, 2), f32)], axis=1)


def finish_kernel(older, tails, out):
    share, samples = out.shape
    lanes = tails.shape[2]
    new = tails[0]
    for chip in range(1, tails.shape[0]):
        new = new + tails[chip]
    pieces = 2 * share * tails.shape[0] // lanes
    row = lax.broadcasted_iota(jnp.int32, (share, lanes), 0) + lax.axis_index("gx") * share
    column = lax.broadcasted_iota(jnp.int32, (share, lanes), 1)
    sample = lax.broadcasted_iota(jnp.int32, (share, samples), 1)
    total = older[...]
    for which in range(2):
        values = jnp.zeros((share, lanes), f32)
        for piece in range(pieces):
            line = which * pieces + piece
            values = values + jnp.where(row == column + piece * lanes, new[line : line + 1], 0.0)
        values = jnp.sum(values, axis=1, keepdims=True)
        total = jnp.where(sample == samples - 2 + which, values, total)
    out[...] = total


def per_device(
    velocity,
    stress,
    material,
    buoyancy_table,
    lame_table,
    shear_table,
    fault_cells,
    block_count,
    strain_history,
    slip_weights,
):
    count = lax.axis_size("gx")
    planes, rows, lanes = material.shape
    slots, parts, points_each, samples = strain_history.shape
    ruptures = slip_weights.shape[1]
    share = ruptures // count
    whole = pl.BlockSpec(memory_space=pltpu.VMEM)
    anywhere = pl.BlockSpec(memory_space=pl.ANY)
    params = pltpu.CompilerParams(vmem_limit_bytes=24 * 1024 * 1024)

    def stay(array):
        return pltpu.with_memory_space_constraint(array, pltpu.HBM)

    live = block_count
    velocity, stress, material, slip_weights, cells = [
        stay(array) for array in (velocity, stress, material, slip_weights, fault_cells)
    ]
    tables = [stay(table) for table in (buoyancy_table, lame_table, shear_table)]
    table_scratch = [pltpu.SMEM(table.shape, f32) for table in tables]
    history = stay(strain_history.reshape(slots, parts * points_each, samples))

    def cost(flops, size):
        return pl.CostEstimate(flops=flops, bytes_accessed=size, transcendentals=0)

    halo = pltpu.VMEM((max(LOWER_PLANES, UPPER_PLANES), rows, lanes), bf16)
    across, within = pl.pallas_call(
        pack_kernel,
        out_shape=(halo, halo),
        in_specs=[whole] * 3,
        out_specs=(whole, whole),
        compiler_params=params,
        name="pack_halos",
    )(velocity, stress, material)
    chips = [(i, i + 1) for i in range(1, count - 1, 2)]
    cores = [(i, i + 1) for i in range(0, count - 1, 2)]
    cores = cores + [(j, i) for i, j in cores]
    across = lax.ppermute(across, "gx", chips + [(j, i) for i, j in chips])
    within = lax.ppermute(within, "gx", cores)

    half = pltpu.VMEM((count // 2, share, samples), f32)
    kept, sent = pl.pallas_call(
        history_kernel,
        out_shape=(half, half),
        in_specs=[anywhere] * 3,
        out_specs=(whole, whole),
        scratch_shapes=[
            pltpu.SMEM((1,), jnp.int32),
            pltpu.VMEM(slip_weights.shape, bf16),
            pltpu.VMEM(history.shape, bf16),
            pltpu.VMEM((ruptures, samples), f32),
            pltpu.SemaphoreType.DMA,
            pltpu.SemaphoreType.DMA((slots,)),
            pltpu.SemaphoreType.DMA((slots,)),
        ],
        compiler_params=params,
        cost_estimate=cost(2 * slots * ruptures * parts * points_each * samples, 2 * history.size),
        name="history_product",
    )(live, slip_weights, history)
    received = lax.ppermute(sent, "gx", cores)
    fields = pl.pallas_call(
        model_kernel,
        out_shape=pltpu.VMEM((5, planes, rows, lanes), f32),
        in_specs=[anywhere, whole] + [anywhere] * 3,
        out_specs=whole,
        scratch_shapes=table_scratch + [pltpu.SemaphoreType.DMA((3,))],
        compiler_params=params,
        cost_estimate=cost(10**9, 4 * 1024 * 1024),
        name="model_fields",
    )(kept, material, *tables)
    chip_sum = pl.pallas_call(
        add_kernel,
        out_shape=half,
        in_specs=[whole] * 2,
        out_specs=whole,
        compiler_params=params,
        cost_estimate=cost(10**6, 1024 * 1024),
        name="add_cores",
    )(kept, received)
    same_core = [list(range(core, count, 2)) for core in range(2)]
    partials = lax.all_to_all(chip_sum, "gx", 0, 0, axis_index_groups=same_core, tiled=True)

    extent = planes + 2 * EDGE
    velocity_two, stress_two, tail = pl.pallas_call(
        steps_kernel,
        out_shape=(
            jax.ShapeDtypeStruct(velocity.shape, f32),
            jax.ShapeDtypeStruct(stress.shape, f32),
            pltpu.VMEM((8, lanes), f32),
        ),
        in_specs=[anywhere] * 8 + [whole] * 3,
        out_specs=(anywhere, anywhere, whole),
        scratch_shapes=[
            pltpu.VMEM((3, extent, rows + 2 * RIM, lanes), f32),
            pltpu.VMEM((6, extent, rows + 2 * RIM, lanes), f32),
            pltpu.VMEM((3, extent, rows, lanes), f32),
            pltpu.VMEM((2, planes * rows * 8, lanes), f32),
            pltpu.VMEM(slip_weights.shape, bf16),
            pltpu.SMEM(live.shape, jnp.int32),
            pltpu.SMEM(cells.shape, jnp.int32),
            *table_scratch,
            pltpu.SemaphoreType.DMA((5,)),
            pltpu.SemaphoreType.DMA((2,)),
            pltpu.SemaphoreType.DMA,
            pltpu.SemaphoreType.DMA((2,)),
        ],
        compiler_params=params,
        cost_estimate=cost(10**10, 30 * 1024 * 1024),
        name="two_steps",
    )(live, cells, *tables, velocity, stress, slip_weights, fields, across, within)
    other_tail = lax.ppermute(tail, "gx", cores)
    tails = pl.pallas_call(
        spread_kernel,
        out_shape=pltpu.VMEM((count // 2, 8, lanes), f32),
        in_specs=[whole] * 2,
        out_specs=whole,
        compiler_params=params,
        name="add_samples",
    )(tail, other_tail)
    tails = lax.all_to_all(tails, "gx", 0, 0, axis_index_groups=same_core, tiled=True)

    older = pl.pallas_call(
        sum_kernel,
        out_shape=pltpu.VMEM((share, samples), f32),
        in_specs=[whole],
        out_specs=whole,
        compiler_params=params,
        cost_estimate=cost(10**6, 1024 * 1024),
        name="sum_partials",
    )(partials)
    seismograms = pl.pallas_call(
        finish_kernel,
        out_shape=jax.ShapeDtypeStruct((share, samples), f32),
        in_specs=[whole, whole],
        out_specs=whole,
        compiler_params=params,
        name="join_samples",
    )(older, tails)
    return (velocity_two, stress_two, seismograms)


def solution(mesh):
    in_specs = (
        P(None, ("site", "gx"), None, None),
        P(None, ("site", "gx"), None, None),
        P("gx", None, None),
        P(),
        P(),
        P(),
        P("gx", None),
        P("gx"),
        P(("site", "gx"), None, None, None),
        P("gx", None, None),
    )
    out_specs = (
        P(None, ("site", "gx"), None, None),
        P(None, ("site", "gx"), None, None),
        P(("site", "gx"), None),
    )
    return jax.shard_map(
        per_device, mesh=mesh, in_specs=in_specs, out_specs=out_specs, check_vma=False
    )
```

```python
import functools

import jax
import jax.numpy as jnp
from jax import lax
from jax.experimental import pallas as pl
from jax.experimental.pallas import tpu as pltpu
from jax.sharding import PartitionSpec as P

time_step = 0.4
scale = time_step / 24.0

VX, VY, VZ, SXX, SYY, SZZ, SXY, SXZ, SYZ, MAT = range(10)
LOWER_RAW = (2, 1, 1, 3, 1, 1, 3, 3, 1, 3)
UPPER_RAW = (2, 2, 2, 4, 2, 2, 3, 3, 2, 3)
LOWER_MOVED = ((3, 5), (2, 4), (2, 4))
UPPER_MOVED = ((3, 4), (3, 5), (3, 5))
LOWER_FINE = (VX, VY, VZ, SXX, SXY, SXZ, SYZ)
UPPER_FINE = (VY, VZ, SXX)
RAW, MOVED, FINE = range(3)
EDGE = 5
RIM = 8


def halo_list(raw, moved, fine):
    entries = [(RAW, field, depth) for field in range(10) for depth in range(1, raw[field] + 1)]
    for field, (first, last) in enumerate(moved):
        entries += [(MOVED, field, depth) for depth in range(first, last + 1)]
    return entries + [(FINE, field, 1) for field in fine]


LOWER = halo_list(LOWER_RAW, LOWER_MOVED, LOWER_FINE)
UPPER = halo_list(UPPER_RAW, UPPER_MOVED, UPPER_FINE)
HALO = max(len(LOWER), len(UPPER))

f32 = jnp.float32
bf16 = jnp.bfloat16


def second_core():
    return lax.axis_index("gx") % 2


def fetch_all(sources, targets, sems):
    copies = [
        pltpu.make_async_copy(source, target, sems.at[index])
        for index, (source, target) in enumerate(zip(sources, targets))
    ]
    for copy in copies:
        copy.start()
    return copies


def looked_up(code, tables):
    results = [jnp.zeros(code.shape, f32) for _ in tables]
    for entry in range(tables[0].shape[0]):
        hit = code == entry + 1
        results = [jnp.where(hit, table[entry], result) for table, result in zip(tables, results)]
    return results


def parts_of(behind, here_low, here_high, ahead):
    return here_high - here_low, ahead - behind


def joined(*parts):
    near, far = parts[0]
    for more_near, more_far in parts[1:]:
        near, far = near + more_near, far + more_far
    return 27.0 * near - far


def shifted(values, place, axis, by):
    size = values.shape[axis]
    inside = place < size - by if by > 0 else place >= -by
    return jnp.where(inside, pltpu.roll(values, -by % size, axis), 0.0)


def along(values, place, axis, forward):
    offsets = (-1, 0, 1, 2) if forward else (-2, -1, 0, 1)
    return parts_of(*[values if by == 0 else shifted(values, place, axis, by) for by in offsets])


def pack_kernel(
    velocity_from, stress_from, material_from, buoyancy_from, across, within, velocity, stress, material, buoyancy, sems
):
    copies = fetch_all(
        (stress_from, velocity_from, material_from, buoyancy_from), (stress, velocity, material, buoyancy), sems
    )
    planes, rows, lanes = material.shape
    odd = second_core()
    row = lax.broadcasted_iota(jnp.int32, (rows, lanes), 0)
    lane = lax.broadcasted_iota(jnp.int32, (rows, lanes), 1)
    for copy in copies:
        copy.wait()

    def along_x(field, plane, forward):
        start = plane - 1 if forward else plane - 2
        return parts_of(*[stress[field - 3, start + step] for step in range(4)])

    def along_y(field, plane, forward):
        return along(stress[field - 3, plane], row, 0, forward)

    def along_z(field, plane, forward):
        return along(stress[field - 3, plane], lane, 1, forward)

    def moved(field, plane):
        factor = scale * looked_up(material[plane] + 1, (buoyancy,))[0]
        if field == VX:
            pull = joined(along_x(SXX, plane, True), along_y(SXY, plane, False), along_z(SXZ, plane, False))
        elif field == VY:
            pull = joined(along_x(SXY, plane, False), along_y(SYY, plane, True), along_z(SYZ, plane, False))
        else:
            pull = joined(along_x(SXZ, plane, False), along_y(SYZ, plane, False), along_z(SZZ, plane, True))
        return velocity[field, plane] + factor * pull

    def fill(out, entries, plane_of):
        for index, (what, field, depth) in enumerate(entries):
            plane = plane_of(depth)
            if what == MOVED:
                values = moved(field, plane)
            elif field < 3:
                values = velocity[field, plane]
            elif field < 9:
                values = stress[field - 3, plane]
            else:
                values = (material[plane] + 1).astype(f32)
            if what == FINE:
                values = values - values.astype(bf16).astype(f32)
            out[index] = values.astype(bf16)
        for spare in range(len(entries), out.shape[0]):
            out[spare] = jnp.zeros(out.shape[1:], bf16)

    def upper_face(out):
        fill(out, LOWER, lambda depth: planes - depth)

    def lower_face(out):
        fill(out, UPPER, lambda depth: depth - 1)

    @pl.when(odd == 0)
    def _():
        lower_face(across)
        upper_face(within)

    @pl.when(odd != 0)
    def _():
        upper_face(across)
        lower_face(within)


def history_kernel(
    live,
    weights,
    history,
    material_from,
    buoyancy_from,
    lame_from,
    shear_from,
    partial,
    fields,
    material,
    buoyancy_table,
    lame_table,
    shear_table,
    slips,
    records,
    model_sems,
    slip_sems,
    record_sems,
):
    slots = weights.shape[0]
    tables = (buoyancy_table, lame_table, shear_table)
    model_copies = fetch_all(
        (material_from, buoyancy_from, lame_from, shear_from), (material, *tables), model_sems
    )
    copies = [
        (
            pltpu.make_async_copy(weights.at[slot], slips.at[slot], slip_sems.at[slot]),
            pltpu.make_async_copy(history.at[slot], records.at[slot], record_sems.at[slot]),
        )
        for slot in range(slots)
    ]
    for copy in copies[0]:
        copy.start()
    for slot in range(1, slots):

        @pl.when(slot < live[0])
        def _(slot=slot):
            for copy in copies[slot]:
                copy.start()

    for copy in model_copies:
        copy.wait()
    for plane in range(material.shape[0]):
        buoyancy, lame, shear = looked_up(material[plane] + 1, tables)
        fields[0, plane] = scale * buoyancy
        fields[1, plane] = scale * lame
        fields[2, plane] = scale * shear
        fields[3, plane] = lame / (3.0 * lame + 2.0 * shear)
        fields[4, plane] = 1.0 / (2.0 * shear)

    for copy in copies[0]:
        copy.wait()
    partial[...] = jnp.dot(slips[0], records[0], preferred_element_type=f32)
    for slot in range(1, slots):

        @pl.when(slot < live[0])
        def _(slot=slot):
            for copy in copies[slot]:
                copy.wait()
            partial[...] += jnp.dot(slips[slot], records[slot], preferred_element_type=f32)


def steps_kernel(
    live,
    cells_from,
    buoyancy_from,
    lame_from,
    shear_from,
    velocity,
    stress,
    weights,
    fields,
    across,
    within,
    velocity_out,
    stress_out,
    tail,
    moving,
    pulling,
    factors,
    strains,
    slips,
    cells,
    buoyancy_table,
    lame_table,
    shear_table,
    scalar_sems,
    slab_sems,
    slip_sem,
    out_sems,
):
    planes, rows, lanes = velocity.shape[1:]
    tables = (buoyancy_table, lame_table, shear_table)
    scalar_copies = fetch_all(
        (cells_from, buoyancy_from, lame_from, shear_from), (cells, *tables), scalar_sems
    )
    inner = pl.ds(RIM, rows)
    slab = pl.ds(EDGE, planes)
    odd = second_core()

    slab_copies = [
        pltpu.make_async_copy(stress, pulling.at[:, slab, inner], slab_sems.at[0]),
        pltpu.make_async_copy(velocity, moving.at[:, slab, inner], slab_sems.at[1]),
    ]
    slip_copy = pltpu.make_async_copy(weights, slips, slip_sem)
    for copy in slab_copies:
        copy.start()
    slip_copy.start()

    def store(field, place, values):
        if field < 3:
            moving[field, place, inner] = values
        else:
            pulling[field - 3, place, inner] = values

    def read(field, place, at):
        return moving[field, place, at] if field < 3 else pulling[field - 3, place, at]

    blank = jnp.zeros((moving.shape[1], RIM, lanes), f32)
    for ref, fields_along_y in ((moving, (0, 1, 2)), (pulling, (SXY - 3, SYY - 3, SYZ - 3))):
        for field in fields_along_y:
            ref[field, :, 0:RIM] = blank
            ref[field, :, RIM + rows : 2 * RIM + rows] = blank

    for kind in range(3):
        factors[kind, slab] = fields[kind]
    for copy in scalar_copies:
        copy.wait()

    def unpack(halo, upper):
        entries = UPPER if upper else LOWER
        for index, (what, field, depth) in enumerate(entries):
            if what == FINE:
                continue
            place = EDGE + planes + depth - 1 if upper else EDGE - depth
            values = halo[index].astype(f32)
            if what == RAW and (FINE, field, depth) in entries:
                values = values + halo[entries.index((FINE, field, depth))].astype(f32)
            if field < 9:
                store(field, place, values)
            else:
                found = looked_up(values.astype(jnp.int32), tables)
                for kind in range(3):
                    factors[kind, place] = scale * found[kind]

    @pl.when(odd == 0)
    def _():
        unpack(across, False)
        unpack(within, True)

    @pl.when(odd != 0)
    def _():
        unpack(within, False)
        unpack(across, True)

    lane = lax.broadcasted_iota(jnp.int32, (rows, lanes), 1)

    def along_x(field, place, forward):
        start = place - 1 if forward else place - 2
        return parts_of(*[read(field, start + step, inner) for step in range(4)])

    def along_y(field, place, forward):
        start = RIM - 1 if forward else RIM - 2
        return parts_of(*[read(field, place, pl.ds(start + step, rows)) for step in range(4)])

    def along_z(field, place, forward):
        return along(read(field, place, inner), lane, 1, forward)

    def move(place, do_x=True, do_yz=True):
        buoyancy = factors[0, place]
        pulls = []
        if do_x:
            pulls.append((VX, along_x(SXX, place, True), along_y(SXY, place, False), along_z(SXZ, place, False)))
        if do_yz:
            pulls.append((VY, along_x(SXY, place, False), along_y(SYY, place, True), along_z(SYZ, place, False)))
            pulls.append((VZ, along_x(SXZ, place, False), along_y(SYZ, place, False), along_z(SZZ, place, True)))
        results = [(field, read(field, place, inner) + buoyancy * joined(*parts)) for field, *parts in pulls]
        for field, values in results:
            store(field, place, values)

    def strain(place, do_yz=True, keep=None):
        lame, shear = factors[1, place], factors[2, place]
        twice = 2.0 * shear
        exx = joined(along_x(VX, place, False))
        eyy = joined(along_y(VY, place, False))
        ezz = joined(along_z(VZ, place, False))
        common = lame * (exx + eyy + ezz)
        changes = [(SXX, common + twice * exx)]
        changes.append((SXY, shear * joined(along_y(VX, place, True), along_x(VY, place, True))))
        changes.append((SXZ, shear * joined(along_z(VX, place, True), along_x(VZ, place, True))))
        if do_yz:
            changes.append((SYY, common + twice * eyy))
            changes.append((SZZ, common + twice * ezz))
            changes.append((SYZ, shear * joined(along_z(VY, place, True), along_y(VZ, place, True))))
        results = {field: read(field, place, inner) + change for field, change in changes}
        for field, values in results.items():
            store(field, place, values)
        if keep is not None:
            compliance = fields[4, place - EDGE]
            shift = fields[3, place - EDGE] * (results[SXX] + results[SYY] + results[SZZ])
            first = pl.multiple_of((place - EDGE) * (8 * rows), 8 * rows)
            for field in range(3, 9):
                values = results[field] - shift if field < 6 else results[field]
                strains[keep, pl.ds(first + field - 3, rows, stride=8)] = values * compliance

    def over(first, last, body, width=2):
        def group(index, carry):
            for step in range(width):
                body(EDGE + first + index * width + step)
            return carry

        lax.fori_loop(0, (last - first) // width, group, 0)

    for copy in slab_copies:
        copy.wait()
    top = EDGE + planes
    move(EDGE - 2, do_yz=False)
    move(EDGE - 1)
    over(0, planes + 2, move)
    for place in range(EDGE - 3, EDGE):
        strain(place, do_yz=place == EDGE - 1)
    over(0, planes, functools.partial(strain, keep=0))
    for place in range(top, top + 3):
        strain(place, do_yz=place < top + 2)
    move(EDGE - 2, do_yz=False)
    move(top + 1, do_x=False)
    over(-1, planes + 1, move)
    out_copies = [
        pltpu.make_async_copy(moving.at[:, slab, inner], velocity_out, out_sems.at[0]),
        pltpu.make_async_copy(pulling.at[:, slab, inner], stress_out, out_sems.at[1]),
    ]
    out_copies[0].start()
    over(0, planes, functools.partial(strain, keep=1))
    out_copies[1].start()

    slip_copy.wait()
    points_each = cells.shape[1]
    lane_bits = lanes.bit_length() - 1
    tall = lax.broadcasted_iota(jnp.int32, (8, lanes), 1)

    def add_slot(slot, new):
        found = [jnp.zeros((8, lanes), f32) for _ in range(2)]
        for point in range(points_each):
            cell = cells[slot, point]
            first = pl.multiple_of((cell >> lane_bits) << 3, 8)
            shift = (point - cell) & (lanes - 1)
            hit = tall == point
            for which in range(2):
                turned = pltpu.roll(strains[which, pl.ds(first, 8)], shift, 1)
                found[which] = jnp.where(hit, turned, found[which])
        pair = [jnp.concatenate([values[part : part + 1] for part in range(6)], axis=1) for values in found]
        pair = jnp.concatenate(pair + [jnp.zeros((6, 6 * points_each), f32)], axis=0).astype(bf16)
        return new + lax.dot_general(pair, slips[slot], (((1,), (1,)), ((), ())), preferred_element_type=f32)

    new = lax.fori_loop(0, live[0], add_slot, jnp.zeros((8, weights.shape[1]), f32))
    pieces = weights.shape[1] // lanes
    lines = [new[which : which + 1, piece * lanes : (piece + 1) * lanes] for which in range(2) for piece in range(pieces)]
    lines = jnp.concatenate(lines + [jnp.zeros((8 - 2 * pieces, lanes), f32)], axis=0)
    for device in range(tail.shape[0]):
        tail[device] = lines
    for copy in out_copies:
        copy.wait()


def sum_kernel(partials, out):
    share, samples = out.shape
    total = partials[0:share]
    for device in range(1, partials.shape[0] // share):
        total = total + partials[device * share : (device + 1) * share]
    out[...] = jnp.concatenate([total[:, 2:], jnp.zeros((share, 2), f32)], axis=1)


def finish_kernel(older, tails, out):
    share, samples = out.shape
    lanes = tails.shape[2]
    new = tails[0]
    for device in range(1, tails.shape[0]):
        new = new + tails[device]
    pieces = share * tails.shape[0] // lanes
    row = lax.broadcasted_iota(jnp.int32, (share, lanes), 0) + lax.axis_index("gx") * share
    column = lax.broadcasted_iota(jnp.int32, (share, lanes), 1)
    sample = lax.broadcasted_iota(jnp.int32, (share, samples), 1)
    total = older[...]
    for which in range(2):
        values = jnp.zeros((share, lanes), f32)
        for piece in range(pieces):
            line = which * pieces + piece
            values = values + jnp.where(row == column + piece * lanes, new[line : line + 1], 0.0)
        values = jnp.sum(values, axis=1, keepdims=True)
        total = jnp.where(sample == samples - 2 + which, values, total)
    out[...] = total


def per_device(
    velocity,
    stress,
    material,
    buoyancy_table,
    lame_table,
    shear_table,
    fault_cells,
    block_count,
    strain_history,
    slip_weights,
):
    count = lax.axis_size("gx")
    planes, rows, lanes = material.shape
    slots, parts, points_each, samples = strain_history.shape
    ruptures = slip_weights.shape[1]
    share = ruptures // count
    whole = pl.BlockSpec(memory_space=pltpu.VMEM)
    scalars = pl.BlockSpec(memory_space=pltpu.SMEM)
    anywhere = pl.BlockSpec(memory_space=pl.ANY)
    params = pltpu.CompilerParams(vmem_limit_bytes=24 * 1024 * 1024)

    def stay(array):
        return pltpu.with_memory_space_constraint(array, pltpu.HBM)

    live = block_count
    velocity, stress, material, slip_weights, cells = [
        stay(array) for array in (velocity, stress, material, slip_weights, fault_cells)
    ]
    tables = [stay(table) for table in (buoyancy_table, lame_table, shear_table)]
    table_scratch = [pltpu.SMEM(table.shape, f32) for table in tables]
    history = stay(strain_history.reshape(slots, parts * points_each, samples))

    def cost(flops, size):
        return pl.CostEstimate(flops=flops, bytes_accessed=size, transcendentals=0)

    halo = pltpu.VMEM((HALO, rows, lanes), bf16)
    across, within = pl.pallas_call(
        pack_kernel,
        out_shape=(halo, halo),
        in_specs=[anywhere] * 4,
        out_specs=(whole, whole),
        scratch_shapes=[
            pltpu.VMEM(velocity.shape, f32),
            pltpu.VMEM(stress.shape, f32),
            pltpu.VMEM(material.shape, jnp.int32),
            table_scratch[0],
            pltpu.SemaphoreType.DMA((4,)),
        ],
        compiler_params=params,
        name="pack_halos",
    )(velocity, stress, material, tables[0])
    chips = [(i, i + 1) for i in range(1, count - 1, 2)]
    cores = [(i, i + 1) for i in range(0, count - 1, 2)]
    cores = cores + [(j, i) for i, j in cores]
    across = lax.ppermute(across, "gx", chips + [(j, i) for i, j in chips])
    within = lax.ppermute(within, "gx", cores)

    partial, fields = pl.pallas_call(
        history_kernel,
        out_shape=(
            jax.ShapeDtypeStruct((ruptures, samples), f32),
            pltpu.VMEM((5, planes, rows, lanes), f32),
        ),
        in_specs=[scalars] + [anywhere] * 6,
        out_specs=(whole, whole),
        scratch_shapes=[
            pltpu.VMEM(material.shape, jnp.int32),
            *table_scratch,
            pltpu.VMEM(slip_weights.shape, bf16),
            pltpu.VMEM(history.shape, bf16),
            pltpu.SemaphoreType.DMA((4,)),
            pltpu.SemaphoreType.DMA((slots,)),
            pltpu.SemaphoreType.DMA((slots,)),
        ],
        compiler_params=params,
        cost_estimate=cost(2 * slots * ruptures * parts * points_each * samples, 2 * history.size),
        name="history_product",
    )(live, slip_weights, history, material, *tables)
    partials = lax.all_to_all(partial, "gx", 0, 0, tiled=True)

    extent = planes + 2 * EDGE
    velocity_two, stress_two, tail = pl.pallas_call(
        steps_kernel,
        out_shape=(
            jax.ShapeDtypeStruct(velocity.shape, f32),
            jax.ShapeDtypeStruct(stress.shape, f32),
            jax.ShapeDtypeStruct((count, 8, lanes), f32),
        ),
        in_specs=[scalars] + [anywhere] * 7 + [whole] * 3,
        out_specs=(anywhere, anywhere, whole),
        scratch_shapes=[
            pltpu.VMEM((3, extent, rows + 2 * RIM, lanes), f32),
            pltpu.VMEM((6, extent, rows + 2 * RIM, lanes), f32),
            pltpu.VMEM((3, extent, rows, lanes), f32),
            pltpu.VMEM((2, planes * rows * 8, lanes), f32),
            pltpu.VMEM(slip_weights.shape, bf16),
            pltpu.SMEM(cells.shape, jnp.int32),
            *table_scratch,
            pltpu.SemaphoreType.DMA((4,)),
            pltpu.SemaphoreType.DMA((2,)),
            pltpu.SemaphoreType.DMA,
            pltpu.SemaphoreType.DMA((2,)),
        ],
        compiler_params=params,
        cost_estimate=cost(10**10, 30 * 1024 * 1024),
        name="two_steps",
    )(live, cells, *tables, velocity, stress, slip_weights, fields, across, within)
    tails = lax.all_to_all(tail, "gx", 0, 0, tiled=True)

    older = pl.pallas_call(
        sum_kernel,
        out_shape=pltpu.VMEM((share, samples), f32),
        in_specs=[whole],
        out_specs=whole,
        compiler_params=params,
        cost_estimate=cost(10**6, 1024 * 1024),
        name="sum_partials",
    )(partials)
    seismograms = pl.pallas_call(
        finish_kernel,
        out_shape=jax.ShapeDtypeStruct((share, samples), f32),
        in_specs=[whole, whole],
        out_specs=whole,
        compiler_params=params,
        name="join_samples",
    )(older, tails)
    return (velocity_two, stress_two, seismograms)


def solution(mesh):
    in_specs = (
        P(None, ("site", "gx"), None, None),
        P(None, ("site", "gx"), None, None),
        P("gx", None, None),
        P(),
        P(),
        P(),
        P("gx", None),
        P("gx"),
        P(("site", "gx"), None, None, None),
        P("gx", None, None),
    )
    out_specs = (
        P(None, ("site", "gx"), None, None),
        P(None, ("site", "gx"), None, None),
        P(("site", "gx"), None),
    )
    return jax.shard_map(
        per_device, mesh=mesh, in_specs=in_specs, out_specs=out_specs, check_vma=False
    )
```

```python
import functools

import jax
import jax.numpy as jnp
from jax import lax
from jax.experimental import pallas as pl
from jax.experimental.pallas import tpu as pltpu
from jax.sharding import PartitionSpec as P

time_step = 0.4
scale = time_step / 24.0

VX, VY, VZ, SXX, SYY, SZZ, SXY, SXZ, SYZ, MAT = range(10)
LOWER_RAW = (2, 1, 1, 3, 1, 1, 3, 3, 1, 3)
UPPER_RAW = (1, 2, 2, 3, 2, 2, 3, 3, 2, 3)
LOWER_MOVED = ((3, 5), (2, 4), (2, 4))
UPPER_MOVED = ((2, 4), (3, 5), (3, 5))
LOWER_FINE = (VX, VY, VZ, SXX, SXY, SXZ, SYZ)
UPPER_FINE = (VY, VZ, SXX)
RAW, MOVED, FINE = range(3)
EDGE = 5
RIM = 8


def halo_list(raw, moved, fine):
    entries = [(RAW, field, depth) for field in range(10) for depth in range(1, raw[field] + 1)]
    for field, (first, last) in enumerate(moved):
        entries += [(MOVED, field, depth) for depth in range(first, last + 1)]
    return entries + [(FINE, field, 1) for field in fine]


LOWER = halo_list(LOWER_RAW, LOWER_MOVED, LOWER_FINE)
UPPER = halo_list(UPPER_RAW, UPPER_MOVED, UPPER_FINE)
HALO = max(len(LOWER), len(UPPER))

f32 = jnp.float32
bf16 = jnp.bfloat16


def second_core():
    return lax.axis_index("gx") % 2


def fetch_all(sources, targets, sems):
    copies = [
        pltpu.make_async_copy(source, target, sems.at[index])
        for index, (source, target) in enumerate(zip(sources, targets))
    ]
    for copy in copies:
        copy.start()
    return copies


def looked_up(code, tables):
    results = [jnp.zeros(code.shape, f32) for _ in tables]
    for entry in range(tables[0].shape[0]):
        hit = code == entry + 1
        results = [jnp.where(hit, table[entry], result) for table, result in zip(tables, results)]
    return results


def parts_of(behind, here_low, here_high, ahead):
    return here_high - here_low, ahead - behind


def joined(*parts):
    near, far = parts[0]
    for more_near, more_far in parts[1:]:
        near, far = near + more_near, far + more_far
    return 27.0 * near - far


def shifted(values, place, axis, by):
    size = values.shape[axis]
    inside = place < size - by if by > 0 else place >= -by
    return jnp.where(inside, pltpu.roll(values, -by % size, axis), 0.0)


def along(values, place, axis, forward):
    offsets = (-1, 0, 1, 2) if forward else (-2, -1, 0, 1)
    return parts_of(*[values if by == 0 else shifted(values, place, axis, by) for by in offsets])


def stepping(moving, pulling, rows, lanes):
    inner = pl.ds(RIM, rows)
    lane = lax.broadcasted_iota(jnp.int32, (rows, lanes), 1)

    def store(field, place, values):
        if field < 3:
            moving[field, place, inner] = values
        else:
            pulling[field - 3, place, inner] = values

    def read(field, place, at=inner):
        return moving[field, place, at] if field < 3 else pulling[field - 3, place, at]

    def along_x(field, place, forward):
        start = place - 1 if forward else place - 2
        return parts_of(*[read(field, start + step) for step in range(4)])

    def along_y(field, place, forward):
        start = RIM - 1 if forward else RIM - 2
        return parts_of(*[read(field, place, pl.ds(start + step, rows)) for step in range(4)])

    def along_z(field, place, forward):
        return along(read(field, place), lane, 1, forward)

    def pull(field, place):
        if field == VX:
            return joined(along_x(SXX, place, True), along_y(SXY, place, False), along_z(SXZ, place, False))
        if field == VY:
            return joined(along_x(SXY, place, False), along_y(SYY, place, True), along_z(SYZ, place, False))
        return joined(along_x(SXZ, place, False), along_y(SYZ, place, False), along_z(SZZ, place, True))

    return store, read, along_x, along_y, along_z, pull


def pack_kernel(
    velocity_from, stress_from, material_from, buoyancy_from, across, within, moving, pulling, material, buoyancy, sems
):
    planes, rows, lanes = material.shape
    slab, inner = pl.ds(EDGE, planes), pl.ds(RIM, rows)
    copies = fetch_all(
        (stress_from, velocity_from, material_from, buoyancy_from),
        (pulling.at[:, slab, inner], moving.at[:, slab, inner], material, buoyancy),
        sems,
    )
    blank = jnp.zeros((moving.shape[1], RIM, lanes), f32)
    for ref, fields_along_y in ((moving, (0, 1, 2)), (pulling, (SXY - 3, SYY - 3, SYZ - 3))):
        for field in fields_along_y:
            ref[field, :, 0:RIM] = blank
            ref[field, :, RIM + rows : 2 * RIM + rows] = blank
    store, read, along_x, along_y, along_z, pull = stepping(moving, pulling, rows, lanes)
    odd = second_core()
    for copy in copies:
        copy.wait()

    def moved(field, plane):
        factor = scale * looked_up(material[plane] + 1, (buoyancy,))[0]
        return read(field, EDGE + plane) + factor * pull(field, EDGE + plane)

    def fill(out, entries, plane_of):
        for index, (what, field, depth) in enumerate(entries):
            plane = plane_of(depth)
            if what == MOVED:
                values = moved(field, plane)
            elif field < 9:
                values = read(field, EDGE + plane)
            else:
                values = (material[plane] + 1).astype(f32)
            if what == FINE:
                values = values - values.astype(bf16).astype(f32)
            out[index] = values.astype(bf16)
        for spare in range(len(entries), out.shape[0]):
            out[spare] = jnp.zeros(out.shape[1:], bf16)

    def upper_face(out):
        fill(out, LOWER, lambda depth: planes - depth)

    def lower_face(out):
        fill(out, UPPER, lambda depth: depth - 1)

    @pl.when(odd == 0)
    def _():
        lower_face(across)
        upper_face(within)

    @pl.when(odd != 0)
    def _():
        upper_face(across)
        lower_face(within)


def history_kernel(live, slips, records, after, kept, sent, total):
    del after
    total[...] = jnp.dot(slips[0], records[0], preferred_element_type=f32)
    for slot in range(1, slips.shape[0]):

        @pl.when(slot < live[0])
        def _(slot=slot):
            total[...] += jnp.dot(slips[slot], records[slot], preferred_element_type=f32)

    share = kept.shape[1]
    odd = second_core()
    for pair in range(kept.shape[0]):
        even = total[2 * pair * share : (2 * pair + 1) * share]
        other = total[(2 * pair + 1) * share : (2 * pair + 2) * share]
        kept[pair] = jnp.where(odd == 0, even, other)
        sent[pair] = jnp.where(odd == 0, other, even)


def add_kernel(first, second, out):
    out[...] = first[...] + second[...]


def model_kernel(after, material, buoyancy_from, lame_from, shear_from, fields, buoyancy_table, lame_table, shear_table, sems):
    del after
    tables = (buoyancy_table, lame_table, shear_table)
    for copy in fetch_all((buoyancy_from, lame_from, shear_from), tables, sems):
        copy.wait()
    for plane in range(material.shape[0]):
        buoyancy, lame, shear = looked_up(material[plane] + 1, tables)
        fields[0, plane] = scale * buoyancy
        fields[1, plane] = scale * lame
        fields[2, plane] = scale * shear
        fields[3, plane] = lame / (3.0 * lame + 2.0 * shear)
        fields[4, plane] = 1.0 / (2.0 * shear)


def steps_kernel(
    live,
    cells_from,
    buoyancy_from,
    lame_from,
    shear_from,
    slips,
    fields,
    across,
    within,
    moving_from,
    pulling_from,
    velocity_out,
    stress_out,
    tail,
    moving,
    pulling,
    factors,
    strains,
    cells,
    buoyancy_table,
    lame_table,
    shear_table,
    scalar_sems,
    out_sems,
):
    planes, rows, lanes = fields.shape[1:]
    tables = (buoyancy_table, lame_table, shear_table)
    scalar_copies = fetch_all(
        (cells_from, buoyancy_from, lame_from, shear_from), (cells, *tables), scalar_sems
    )
    inner = pl.ds(RIM, rows)
    slab = pl.ds(EDGE, planes)
    odd = second_core()
    store, read, along_x, along_y, along_z, pull = stepping(moving, pulling, rows, lanes)

    outside = [place for place in range(moving.shape[1]) if not EDGE <= place < EDGE + planes]
    blank = jnp.zeros((RIM, lanes), f32)
    for ref, source in ((moving, moving_from), (pulling, pulling_from)):
        for field in range(ref.shape[0]):
            ref[field, slab] = source[field, slab]
            for place in outside:
                ref[field, place, 0:RIM] = blank
                ref[field, place, RIM + rows : 2 * RIM + rows] = blank

    for kind in range(3):
        factors[kind, slab] = fields[kind]
    for copy in scalar_copies:
        copy.wait()

    def unpack(halo, upper):
        entries = UPPER if upper else LOWER
        for index, (what, field, depth) in enumerate(entries):
            if what == FINE:
                continue
            place = EDGE + planes + depth - 1 if upper else EDGE - depth
            values = halo[index].astype(f32)
            if what == RAW and (FINE, field, depth) in entries:
                values = values + halo[entries.index((FINE, field, depth))].astype(f32)
            if field < 9:
                store(field, place, values)
            else:
                found = looked_up(values.astype(jnp.int32), tables)
                for kind in range(3):
                    factors[kind, place] = scale * found[kind]

    @pl.when(odd == 0)
    def _():
        unpack(across, False)
        unpack(within, True)

    @pl.when(odd != 0)
    def _():
        unpack(within, False)
        unpack(across, True)

    def move(place, do_x=True, do_yz=True):
        buoyancy = factors[0, place]
        chosen = ([VX] if do_x else []) + ([VY, VZ] if do_yz else [])
        results = [read(field, place) + buoyancy * pull(field, place) for field in chosen]
        for field, values in zip(chosen, results):
            store(field, place, values)

    def strain(place, do_yz=True, keep=None):
        lame, shear = factors[1, place], factors[2, place]
        twice = 2.0 * shear
        exx = joined(along_x(VX, place, False))
        eyy = joined(along_y(VY, place, False))
        ezz = joined(along_z(VZ, place, False))
        common = lame * (exx + eyy + ezz)
        changes = [(SXX, common + twice * exx)]
        changes.append((SXY, shear * joined(along_y(VX, place, True), along_x(VY, place, True))))
        changes.append((SXZ, shear * joined(along_z(VX, place, True), along_x(VZ, place, True))))
        if do_yz:
            changes.append((SYY, common + twice * eyy))
            changes.append((SZZ, common + twice * ezz))
            changes.append((SYZ, shear * joined(along_z(VY, place, True), along_y(VZ, place, True))))
        results = {field: read(field, place) + change for field, change in changes}
        for field, values in results.items():
            store(field, place, values)
        if keep is not None:
            compliance = fields[4, place - EDGE]
            shift = fields[3, place - EDGE] * (results[SXX] + results[SYY] + results[SZZ])
            first = pl.multiple_of((place - EDGE) * (8 * rows), 8 * rows)
            for field in range(3, 9):
                values = results[field] - shift if field < 6 else results[field]
                strains[keep, pl.ds(first + field - 3, rows, stride=8)] = values * compliance

    def over(first, last, body, width=2):
        def group(index, carry):
            for step in range(width):
                body(EDGE + first + index * width + step)
            return carry

        lax.fori_loop(0, (last - first) // width, group, 0)

    top = EDGE + planes
    move(EDGE - 2, do_yz=False)
    move(top + 1, do_x=False)
    over(-1, planes + 1, move)
    for place in range(EDGE - 3, EDGE):
        strain(place, do_yz=place == EDGE - 1)
    over(0, planes, functools.partial(strain, keep=0))
    for place in range(top, top + 3):
        strain(place, do_yz=place < top + 2)
    move(EDGE - 2, do_yz=False)
    move(top + 1, do_x=False)
    over(-1, planes + 1, move)
    out_copies = [
        pltpu.make_async_copy(moving.at[:, slab, inner], velocity_out, out_sems.at[0]),
        pltpu.make_async_copy(pulling.at[:, slab, inner], stress_out, out_sems.at[1]),
    ]
    out_copies[0].start()
    over(0, planes, functools.partial(strain, keep=1))
    out_copies[1].start()

    points_each = cells.shape[1]
    lane_bits = lanes.bit_length() - 1
    tall = lax.broadcasted_iota(jnp.int32, (8, lanes), 1)

    def add_slot(slot, new):
        found = [jnp.zeros((8, lanes), f32) for _ in range(2)]
        for point in range(points_each):
            cell = cells[slot, point]
            first = pl.multiple_of((cell >> lane_bits) << 3, 8)
            shift = (point - cell) & (lanes - 1)
            hit = tall == point
            for which in range(2):
                turned = pltpu.roll(strains[which, pl.ds(first, 8)], shift, 1)
                found[which] = jnp.where(hit, turned, found[which])
        pair = [jnp.concatenate([values[part : part + 1] for part in range(6)], axis=1) for values in found]
        pair = jnp.concatenate(pair + [jnp.zeros((6, 6 * points_each), f32)], axis=0).astype(bf16)
        return new + lax.dot_general(pair, slips[slot], (((1,), (1,)), ((), ())), preferred_element_type=f32)

    new = lax.fori_loop(0, live[0], add_slot, jnp.zeros((8, slips.shape[1]), f32))
    pieces = slips.shape[1] // lanes
    lines = [new[which : which + 1, piece * lanes : (piece + 1) * lanes] for which in range(2) for piece in range(pieces)]
    lines = jnp.concatenate(lines + [jnp.zeros((8 - 2 * pieces, lanes), f32)], axis=0)
    for device in range(tail.shape[0]):
        tail[device] = lines
    for copy in out_copies:
        copy.wait()


def sum_kernel(partials, out):
    share, samples = out.shape
    total = partials[0]
    for chip in range(1, partials.shape[0]):
        total = total + partials[chip]
    out[...] = jnp.concatenate([total[:, 2:], jnp.zeros((share, 2), f32)], axis=1)


def finish_kernel(older, tails, out):
    share, samples = out.shape
    lanes = tails.shape[2]
    new = tails[0]
    for device in range(1, tails.shape[0]):
        new = new + tails[device]
    pieces = share * tails.shape[0] // lanes
    row = lax.broadcasted_iota(jnp.int32, (share, lanes), 0) + lax.axis_index("gx") * share
    column = lax.broadcasted_iota(jnp.int32, (share, lanes), 1)
    sample = lax.broadcasted_iota(jnp.int32, (share, samples), 1)
    total = older[...]
    for which in range(2):
        values = jnp.zeros((share, lanes), f32)
        for piece in range(pieces):
            line = which * pieces + piece
            values = values + jnp.where(row == column + piece * lanes, new[line : line + 1], 0.0)
        values = jnp.sum(values, axis=1, keepdims=True)
        total = jnp.where(sample == samples - 2 + which, values, total)
    out[...] = total


def per_device(
    velocity,
    stress,
    material,
    buoyancy_table,
    lame_table,
    shear_table,
    fault_cells,
    block_count,
    strain_history,
    slip_weights,
):
    count = lax.axis_size("gx")
    planes, rows, lanes = material.shape
    slots, parts, points_each, samples = strain_history.shape
    ruptures = slip_weights.shape[1]
    share = ruptures // count
    whole = pl.BlockSpec(memory_space=pltpu.VMEM)
    scalars = pl.BlockSpec(memory_space=pltpu.SMEM)
    anywhere = pl.BlockSpec(memory_space=pl.ANY)
    params = pltpu.CompilerParams(vmem_limit_bytes=24 * 1024 * 1024)

    def stay(array):
        return pltpu.with_memory_space_constraint(array, pltpu.HBM)

    live = block_count
    velocity, stress, material, cells = [stay(array) for array in (velocity, stress, material, fault_cells)]
    tables = [stay(table) for table in (buoyancy_table, lame_table, shear_table)]
    table_scratch = [pltpu.SMEM(table.shape, f32) for table in tables]
    history = strain_history.reshape(slots, parts * points_each, samples)

    def cost(flops, size):
        return pl.CostEstimate(flops=flops, bytes_accessed=size, transcendentals=0)

    halo = pltpu.VMEM((HALO, rows, lanes), bf16)
    extent = planes + 2 * EDGE
    padded = [pltpu.VMEM((fields, extent, rows + 2 * RIM, lanes), f32) for fields in (3, 6)]
    across, within, moving, pulling, material = pl.pallas_call(
        pack_kernel,
        out_shape=(halo, halo, *padded, pltpu.VMEM(material.shape, jnp.int32)),
        in_specs=[anywhere] * 4,
        out_specs=(whole,) * 5,
        scratch_shapes=[table_scratch[0], pltpu.SemaphoreType.DMA((4,))],
        compiler_params=params,
        cost_estimate=cost(10**10, 30 * 1024 * 1024),
        name="pack_halos",
    )(velocity, stress, material, tables[0])
    chips = [(i, i + 1) for i in range(1, count - 1, 2)]
    cores = [(i, i + 1) for i in range(0, count - 1, 2)]
    cores = cores + [(j, i) for i, j in cores]
    across = lax.ppermute(across, "gx", chips + [(j, i) for i, j in chips])
    within = lax.ppermute(within, "gx", cores)

    half = pltpu.VMEM((count // 2, share, samples), f32)
    kept, sent = pl.pallas_call(
        history_kernel,
        out_shape=(half, half),
        in_specs=[scalars, whole, whole, anywhere],
        out_specs=(whole, whole),
        scratch_shapes=[pltpu.VMEM((ruptures, samples), f32)],
        compiler_params=params,
        cost_estimate=cost(2 * slots * ruptures * parts * points_each * samples, 2 * history.size),
        name="history_product",
    )(live, slip_weights, history, moving)
    received = lax.ppermute(sent, "gx", cores)
    fields = pl.pallas_call(
        model_kernel,
        out_shape=pltpu.VMEM((5, planes, rows, lanes), f32),
        in_specs=[anywhere, whole] + [anywhere] * 3,
        out_specs=whole,
        scratch_shapes=table_scratch + [pltpu.SemaphoreType.DMA((3,))],
        compiler_params=params,
        cost_estimate=cost(10**9, 4 * 1024 * 1024),
        name="model_fields",
    )(kept, material, *tables)
    chip_sum = pl.pallas_call(
        add_kernel,
        out_shape=jax.ShapeDtypeStruct((count // 2, share, samples), f32),
        in_specs=[whole] * 2,
        out_specs=whole,
        compiler_params=params,
        cost_estimate=cost(10**6, 1024 * 1024),
        name="add_cores",
    )(kept, received)
    same_core = [list(range(core, count, 2)) for core in range(2)]
    partials = lax.all_to_all(chip_sum, "gx", 0, 0, axis_index_groups=same_core, tiled=True)

    velocity_two, stress_two, tail = pl.pallas_call(
        steps_kernel,
        out_shape=(
            jax.ShapeDtypeStruct(velocity.shape, f32),
            jax.ShapeDtypeStruct(stress.shape, f32),
            jax.ShapeDtypeStruct((count, 8, lanes), f32),
        ),
        in_specs=[scalars] + [anywhere] * 4 + [whole] * 6,
        out_specs=(anywhere, anywhere, whole),
        scratch_shapes=[
            *padded,
            pltpu.VMEM((3, extent, rows, lanes), f32),
            pltpu.VMEM((2, planes * rows * 8, lanes), f32),
            pltpu.SMEM(cells.shape, jnp.int32),
            *table_scratch,
            pltpu.SemaphoreType.DMA((4,)),
            pltpu.SemaphoreType.DMA((2,)),
        ],
        compiler_params=params,
        cost_estimate=cost(10**10, 30 * 1024 * 1024),
        name="two_steps",
    )(live, cells, *tables, slip_weights, fields, across, within, moving, pulling)
    tails = lax.all_to_all(tail, "gx", 0, 0, tiled=True)

    older = pl.pallas_call(
        sum_kernel,
        out_shape=pltpu.VMEM((share, samples), f32),
        in_specs=[whole],
        out_specs=whole,
        compiler_params=params,
        cost_estimate=cost(10**6, 1024 * 1024),
        name="sum_partials",
    )(partials)
    seismograms = pl.pallas_call(
        finish_kernel,
        out_shape=jax.ShapeDtypeStruct((share, samples), f32),
        in_specs=[whole, whole],
        out_specs=whole,
        compiler_params=params,
        name="join_samples",
    )(older, tails)
    return (velocity_two, stress_two, seismograms)


def solution(mesh):
    in_specs = (
        P(None, ("site", "gx"), None, None),
        P(None, ("site", "gx"), None, None),
        P("gx", None, None),
        P(),
        P(),
        P(),
        P("gx", None),
        P("gx"),
        P(("site", "gx"), None, None, None),
        P("gx", None, None),
    )
    out_specs = (
        P(None, ("site", "gx"), None, None),
        P(None, ("site", "gx"), None, None),
        P(("site", "gx"), None),
    )
    return jax.shard_map(
        per_device, mesh=mesh, in_specs=in_specs, out_specs=out_specs, check_vma=False
    )
```

```python
import functools

import jax
import jax.numpy as jnp
from jax import lax
from jax.experimental import pallas as pl
from jax.experimental.pallas import tpu as pltpu
from jax.sharding import PartitionSpec as P

time_step = 0.4
scale = time_step / 24.0

VX, VY, VZ, SXX, SYY, SZZ, SXY, SXZ, SYZ, MAT = range(10)
LOWER_RAW = (2, 1, 1, 3, 1, 1, 3, 3, 1, 3)
UPPER_RAW = (1, 2, 2, 3, 2, 2, 3, 3, 2, 3)
LOWER_MOVED = ((3, 5), (2, 4), (2, 4))
UPPER_MOVED = ((2, 4), (3, 5), (3, 5))
LOWER_FINE = (VX, VY, VZ, SXX, SXY, SXZ, SYZ)
UPPER_FINE = (VY, VZ, SXX)
RAW, MOVED, FINE = range(3)
EDGE = 5
RIM = 8


def halo_list(raw, moved, fine):
    entries = [(RAW, field, depth) for field in range(10) for depth in range(1, raw[field] + 1)]
    for field, (first, last) in enumerate(moved):
        entries += [(MOVED, field, depth) for depth in range(first, last + 1)]
    return entries + [(FINE, field, 1) for field in fine]


LOWER = halo_list(LOWER_RAW, LOWER_MOVED, LOWER_FINE)
UPPER = halo_list(UPPER_RAW, UPPER_MOVED, UPPER_FINE)
HALO = max(len(LOWER), len(UPPER))

f32 = jnp.float32
bf16 = jnp.bfloat16


def second_core():
    return lax.axis_index("gx") % 2


def fetch_all(sources, targets, sems):
    copies = [
        pltpu.make_async_copy(source, target, sems.at[index])
        for index, (source, target) in enumerate(zip(sources, targets))
    ]
    for copy in copies:
        copy.start()
    return copies


def looked_up(code, tables):
    results = [jnp.zeros(code.shape, f32) for _ in tables]
    for entry in range(tables[0].shape[0]):
        hit = code == entry + 1
        results = [jnp.where(hit, table[entry], result) for table, result in zip(tables, results)]
    return results


def parts_of(behind, here_low, here_high, ahead):
    return here_high - here_low, ahead - behind


def joined(*parts):
    near, far = parts[0]
    for more_near, more_far in parts[1:]:
        near, far = near + more_near, far + more_far
    return 27.0 * near - far


def shifted(values, place, axis, by):
    size = values.shape[axis]
    inside = place < size - by if by > 0 else place >= -by
    return jnp.where(inside, pltpu.roll(values, -by % size, axis), 0.0)


def along(values, place, axis, forward):
    offsets = (-1, 0, 1, 2) if forward else (-2, -1, 0, 1)
    return parts_of(*[values if by == 0 else shifted(values, place, axis, by) for by in offsets])


def stepping(moving, pulling, rows, lanes):
    inner = pl.ds(RIM, rows)
    lane = lax.broadcasted_iota(jnp.int32, (rows, lanes), 1)

    def store(field, place, values):
        if field < 3:
            moving[field, place, inner] = values
        else:
            pulling[field - 3, place, inner] = values

    def read(field, place, at=inner):
        return moving[field, place, at] if field < 3 else pulling[field - 3, place, at]

    def along_x(field, place, forward):
        start = place - 1 if forward else place - 2
        return parts_of(*[read(field, start + step) for step in range(4)])

    def along_y(field, place, forward):
        start = RIM - 1 if forward else RIM - 2
        return parts_of(*[read(field, place, pl.ds(start + step, rows)) for step in range(4)])

    def along_z(field, place, forward):
        return along(read(field, place), lane, 1, forward)

    def pull(field, place):
        if field == VX:
            return joined(along_x(SXX, place, True), along_y(SXY, place, False), along_z(SXZ, place, False))
        if field == VY:
            return joined(along_x(SXY, place, False), along_y(SYY, place, True), along_z(SYZ, place, False))
        return joined(along_x(SXZ, place, False), along_y(SYZ, place, False), along_z(SZZ, place, True))

    return store, read, along_x, along_y, along_z, pull


def pack_kernel(
    velocity_from, stress_from, material_from, buoyancy_from, across, within, moving, pulling, material, buoyancy, sems
):
    planes, rows, lanes = material.shape
    slab, inner = pl.ds(EDGE, planes), pl.ds(RIM, rows)
    copies = fetch_all(
        (stress_from, velocity_from, material_from, buoyancy_from),
        (pulling.at[:, slab, inner], moving.at[:, slab, inner], material, buoyancy),
        sems,
    )
    blank = jnp.zeros((moving.shape[1], RIM, lanes), f32)
    for ref, fields_along_y in ((moving, (0, 1, 2)), (pulling, (SXY - 3, SYY - 3, SYZ - 3))):
        for field in fields_along_y:
            ref[field, :, 0:RIM] = blank
            ref[field, :, RIM + rows : 2 * RIM + rows] = blank
    store, read, along_x, along_y, along_z, pull = stepping(moving, pulling, rows, lanes)
    odd = second_core()
    for copy in copies:
        copy.wait()

    def moved(field, plane):
        factor = scale * looked_up(material[plane] + 1, (buoyancy,))[0]
        return read(field, EDGE + plane) + factor * pull(field, EDGE + plane)

    def fill(out, entries, plane_of):
        for index, (what, field, depth) in enumerate(entries):
            plane = plane_of(depth)
            if what == MOVED:
                values = moved(field, plane)
            elif field < 9:
                values = read(field, EDGE + plane)
            else:
                values = (material[plane] + 1).astype(f32)
            if what == FINE:
                values = values - values.astype(bf16).astype(f32)
            out[index] = values.astype(bf16)
        for spare in range(len(entries), out.shape[0]):
            out[spare] = jnp.zeros(out.shape[1:], bf16)

    def upper_face(out):
        fill(out, LOWER, lambda depth: planes - depth)

    def lower_face(out):
        fill(out, UPPER, lambda depth: depth - 1)

    @pl.when(odd == 0)
    def _():
        lower_face(across)
        upper_face(within)

    @pl.when(odd != 0)
    def _():
        upper_face(across)
        lower_face(within)


def history_kernel(live, weights, history, partial, slips, records, slip_sems, record_sems):
    slots = weights.shape[0]
    copies = [
        (
            pltpu.make_async_copy(weights.at[slot], slips.at[slot], slip_sems.at[slot]),
            pltpu.make_async_copy(history.at[slot], records.at[slot], record_sems.at[slot]),
        )
        for slot in range(slots)
    ]
    for copy in copies[0]:
        copy.start()
    for slot in range(1, slots):

        @pl.when(slot < live[0])
        def _(slot=slot):
            for copy in copies[slot]:
                copy.start()

    for copy in copies[0]:
        copy.wait()
    partial[...] = jnp.dot(slips[0], records[0], preferred_element_type=f32)
    for slot in range(1, slots):

        @pl.when(slot < live[0])
        def _(slot=slot):
            for copy in copies[slot]:
                copy.wait()
            partial[...] += jnp.dot(slips[slot], records[slot], preferred_element_type=f32)


def steps_kernel(
    live,
    cells_from,
    buoyancy_from,
    lame_from,
    shear_from,
    material_from,
    velocity,
    stress,
    weights,
    across,
    within,
    velocity_out,
    stress_out,
    tail,
    moving,
    pulling,
    factors,
    strain_factors,
    strains,
    material,
    slips,
    cells,
    buoyancy_table,
    lame_table,
    shear_table,
    scalar_sems,
    slab_sems,
    out_sems,
):
    planes, rows, lanes = velocity.shape[1:]
    tables = (buoyancy_table, lame_table, shear_table)
    inner = pl.ds(RIM, rows)
    slab = pl.ds(EDGE, planes)
    scalar_copies = fetch_all(
        (buoyancy_from, lame_from, shear_from, material_from, cells_from), (*tables, material, cells), scalar_sems
    )
    slab_copies = fetch_all(
        (stress, velocity, weights), (pulling.at[:, slab, inner], moving.at[:, slab, inner], slips), slab_sems
    )
    odd = second_core()
    store, read, along_x, along_y, along_z, pull = stepping(moving, pulling, rows, lanes)

    blank = jnp.zeros((moving.shape[1], RIM, lanes), f32)
    for ref, fields_along_y in ((moving, (0, 1, 2)), (pulling, (SXY - 3, SYY - 3, SYZ - 3))):
        for field in fields_along_y:
            ref[field, :, 0:RIM] = blank
            ref[field, :, RIM + rows : 2 * RIM + rows] = blank

    for copy in scalar_copies:
        copy.wait()
    for plane in range(planes):
        buoyancy, lame, shear = looked_up(material[plane] + 1, tables)
        factors[0, EDGE + plane] = scale * buoyancy
        factors[1, EDGE + plane] = scale * lame
        factors[2, EDGE + plane] = scale * shear
        strain_factors[0, plane] = lame / (3.0 * lame + 2.0 * shear)
        strain_factors[1, plane] = 1.0 / (2.0 * shear)

    def unpack(halo, upper):
        entries = UPPER if upper else LOWER
        for index, (what, field, depth) in enumerate(entries):
            if what == FINE:
                continue
            place = EDGE + planes + depth - 1 if upper else EDGE - depth
            values = halo[index].astype(f32)
            if what == RAW and (FINE, field, depth) in entries:
                values = values + halo[entries.index((FINE, field, depth))].astype(f32)
            if field < 9:
                store(field, place, values)
            else:
                found = looked_up(values.astype(jnp.int32), tables)
                for kind in range(3):
                    factors[kind, place] = scale * found[kind]

    @pl.when(odd == 0)
    def _():
        unpack(across, False)
        unpack(within, True)

    @pl.when(odd != 0)
    def _():
        unpack(within, False)
        unpack(across, True)

    def move(place, do_x=True, do_yz=True):
        buoyancy = factors[0, place]
        chosen = ([VX] if do_x else []) + ([VY, VZ] if do_yz else [])
        results = [read(field, place) + buoyancy * pull(field, place) for field in chosen]
        for field, values in zip(chosen, results):
            store(field, place, values)

    def strain(place, do_yz=True, keep=None):
        lame, shear = factors[1, place], factors[2, place]
        twice = 2.0 * shear
        exx = joined(along_x(VX, place, False))
        eyy = joined(along_y(VY, place, False))
        ezz = joined(along_z(VZ, place, False))
        common = lame * (exx + eyy + ezz)
        changes = [(SXX, common + twice * exx)]
        changes.append((SXY, shear * joined(along_y(VX, place, True), along_x(VY, place, True))))
        changes.append((SXZ, shear * joined(along_z(VX, place, True), along_x(VZ, place, True))))
        if do_yz:
            changes.append((SYY, common + twice * eyy))
            changes.append((SZZ, common + twice * ezz))
            changes.append((SYZ, shear * joined(along_z(VY, place, True), along_y(VZ, place, True))))
        results = {field: read(field, place) + change for field, change in changes}
        for field, values in results.items():
            store(field, place, values)
        if keep is not None:
            compliance = strain_factors[1, place - EDGE]
            shift = strain_factors[0, place - EDGE] * (results[SXX] + results[SYY] + results[SZZ])
            first = pl.multiple_of((place - EDGE) * (8 * rows), 8 * rows)
            for field in range(3, 9):
                values = results[field] - shift if field < 6 else results[field]
                strains[keep, pl.ds(first + field - 3, rows, stride=8)] = values * compliance

    def over(first, last, body, width=2):
        def group(index, carry):
            for step in range(width):
                body(EDGE + first + index * width + step)
            return carry

        lax.fori_loop(0, (last - first) // width, group, 0)

    for copy in slab_copies[:2]:
        copy.wait()
    top = EDGE + planes
    move(EDGE - 2, do_yz=False)
    move(top + 1, do_x=False)
    over(-1, planes + 1, move)
    for place in range(EDGE - 3, EDGE):
        strain(place, do_yz=place == EDGE - 1)
    over(0, planes, functools.partial(strain, keep=0))
    for place in range(top, top + 3):
        strain(place, do_yz=place < top + 2)
    move(EDGE - 2, do_yz=False)
    move(top + 1, do_x=False)
    over(-1, planes + 1, move)
    out_copies = [
        pltpu.make_async_copy(moving.at[:, slab, inner], velocity_out, out_sems.at[0]),
        pltpu.make_async_copy(pulling.at[:, slab, inner], stress_out, out_sems.at[1]),
    ]
    out_copies[0].start()
    over(0, planes, functools.partial(strain, keep=1))
    out_copies[1].start()

    slab_copies[2].wait()
    points_each = cells.shape[1]
    lane_bits = lanes.bit_length() - 1
    tall = lax.broadcasted_iota(jnp.int32, (8, lanes), 1)

    def add_slot(slot, new):
        found = [jnp.zeros((8, lanes), f32) for _ in range(2)]
        for point in range(points_each):
            cell = cells[slot, point]
            first = pl.multiple_of((cell >> lane_bits) << 3, 8)
            shift = (point - cell) & (lanes - 1)
            hit = tall == point
            for which in range(2):
                turned = pltpu.roll(strains[which, pl.ds(first, 8)], shift, 1)
                found[which] = jnp.where(hit, turned, found[which])
        pair = [jnp.concatenate([values[part : part + 1] for part in range(6)], axis=1) for values in found]
        pair = jnp.concatenate(pair + [jnp.zeros((6, 6 * points_each), f32)], axis=0).astype(bf16)
        return new + lax.dot_general(pair, slips[slot], (((1,), (1,)), ((), ())), preferred_element_type=f32)

    new = lax.fori_loop(0, live[0], add_slot, jnp.zeros((8, slips.shape[1]), f32))
    pieces = slips.shape[1] // lanes
    lines = [new[which : which + 1, piece * lanes : (piece + 1) * lanes] for which in range(2) for piece in range(pieces)]
    tail[...] = jnp.concatenate(lines + [jnp.zeros((8 - 2 * pieces, lanes), f32)], axis=0)
    for copy in out_copies:
        copy.wait()


def sum_kernel(partials, out):
    share, samples = out.shape
    total = partials[0:share]
    for device in range(1, partials.shape[0] // share):
        total = total + partials[device * share : (device + 1) * share]
    out[...] = jnp.concatenate([total[:, 2:], jnp.zeros((share, 2), f32)], axis=1)


def finish_kernel(older, new, out):
    share, samples = out.shape
    lanes = new.shape[1]
    pieces = share * lax.axis_size("gx") // lanes
    row = lax.broadcasted_iota(jnp.int32, (share, lanes), 0) + lax.axis_index("gx") * share
    column = lax.broadcasted_iota(jnp.int32, (share, lanes), 1)
    sample = lax.broadcasted_iota(jnp.int32, (share, samples), 1)
    total = older[...]
    for which in range(2):
        values = jnp.zeros((share, lanes), f32)
        for piece in range(pieces):
            line = which * pieces + piece
            values = values + jnp.where(row == column + piece * lanes, new[line : line + 1, :], 0.0)
        values = jnp.sum(values, axis=1, keepdims=True)
        total = jnp.where(sample == samples - 2 + which, values, total)
    out[...] = total


def per_device(
    velocity,
    stress,
    material,
    buoyancy_table,
    lame_table,
    shear_table,
    fault_cells,
    block_count,
    strain_history,
    slip_weights,
):
    count = lax.axis_size("gx")
    planes, rows, lanes = material.shape
    slots, parts, points_each, samples = strain_history.shape
    ruptures = slip_weights.shape[1]
    share = ruptures // count
    whole = pl.BlockSpec(memory_space=pltpu.VMEM)
    scalars = pl.BlockSpec(memory_space=pltpu.SMEM)
    anywhere = pl.BlockSpec(memory_space=pl.ANY)
    params = pltpu.CompilerParams(vmem_limit_bytes=24 * 1024 * 1024)

    def stay(array):
        return pltpu.with_memory_space_constraint(array, pltpu.HBM)

    live = block_count
    velocity, stress, material, slip_weights, cells = [
        stay(array) for array in (velocity, stress, material, slip_weights, fault_cells)
    ]
    tables = [stay(table) for table in (buoyancy_table, lame_table, shear_table)]
    table_scratch = [pltpu.SMEM(table.shape, f32) for table in tables]
    history = stay(strain_history.reshape(slots, parts * points_each, samples))

    def cost(flops, size):
        return pl.CostEstimate(flops=flops, bytes_accessed=size, transcendentals=0)

    halo = pltpu.VMEM((HALO, rows, lanes), bf16)
    extent = planes + 2 * EDGE
    padded = [pltpu.VMEM((fields, extent, rows + 2 * RIM, lanes), f32) for fields in (3, 6)]
    across, within = pl.pallas_call(
        pack_kernel,
        out_shape=(halo, halo),
        in_specs=[anywhere] * 4,
        out_specs=(whole, whole),
        scratch_shapes=[
            *padded,
            pltpu.VMEM(material.shape, jnp.int32),
            table_scratch[0],
            pltpu.SemaphoreType.DMA((4,)),
        ],
        compiler_params=params,
        name="pack_halos",
    )(velocity, stress, material, tables[0])
    chips = [(i, i + 1) for i in range(1, count - 1, 2)]
    cores = [(i, i + 1) for i in range(0, count - 1, 2)]
    cores = cores + [(j, i) for i, j in cores]
    across = lax.ppermute(across, "gx", chips + [(j, i) for i, j in chips])
    within = lax.ppermute(within, "gx", cores)

    partial = pl.pallas_call(
        history_kernel,
        out_shape=jax.ShapeDtypeStruct((ruptures, samples), f32),
        in_specs=[scalars] + [anywhere] * 2,
        out_specs=whole,
        scratch_shapes=[
            pltpu.VMEM(slip_weights.shape, bf16),
            pltpu.VMEM(history.shape, bf16),
            pltpu.SemaphoreType.DMA((slots,)),
            pltpu.SemaphoreType.DMA((slots,)),
        ],
        compiler_params=params,
        cost_estimate=cost(2 * slots * ruptures * parts * points_each * samples, 2 * history.size),
        name="history_product",
    )(live, slip_weights, history)
    partials = lax.all_to_all(partial, "gx", 0, 0, tiled=True)

    velocity_two, stress_two, tail = pl.pallas_call(
        steps_kernel,
        out_shape=(
            jax.ShapeDtypeStruct(velocity.shape, f32),
            jax.ShapeDtypeStruct(stress.shape, f32),
            pltpu.VMEM((8, lanes), f32),
        ),
        in_specs=[scalars] + [anywhere] * 8 + [whole] * 2,
        out_specs=(anywhere, anywhere, whole),
        scratch_shapes=[
            *padded,
            pltpu.VMEM((3, extent, rows, lanes), f32),
            pltpu.VMEM((2, planes, rows, lanes), f32),
            pltpu.VMEM((2, planes * rows * 8, lanes), f32),
            pltpu.VMEM(material.shape, jnp.int32),
            pltpu.VMEM(slip_weights.shape, bf16),
            pltpu.SMEM(cells.shape, jnp.int32),
            *table_scratch,
            pltpu.SemaphoreType.DMA((5,)),
            pltpu.SemaphoreType.DMA((3,)),
            pltpu.SemaphoreType.DMA((2,)),
        ],
        compiler_params=params,
        cost_estimate=cost(10**10, 30 * 1024 * 1024),
        name="two_steps",
    )(live, cells, *tables, material, velocity, stress, slip_weights, across, within)
    new = lax.psum(tail, "gx")

    older = pl.pallas_call(
        sum_kernel,
        out_shape=pltpu.VMEM((share, samples), f32),
        in_specs=[whole],
        out_specs=whole,
        compiler_params=params,
        cost_estimate=cost(10**6, 1024 * 1024),
        name="sum_partials",
    )(partials)
    seismograms = pl.pallas_call(
        finish_kernel,
        out_shape=jax.ShapeDtypeStruct((share, samples), f32),
        in_specs=[whole, whole],
        out_specs=whole,
        compiler_params=params,
        name="join_samples",
    )(older, new)
    return (velocity_two, stress_two, seismograms)


def solution(mesh):
    in_specs = (
        P(None, ("site", "gx"), None, None),
        P(None, ("site", "gx"), None, None),
        P("gx", None, None),
        P(),
        P(),
        P(),
        P("gx", None),
        P("gx"),
        P(("site", "gx"), None, None, None),
        P("gx", None, None),
    )
    out_specs = (
        P(None, ("site", "gx"), None, None),
        P(None, ("site", "gx"), None, None),
        P(("site", "gx"), None),
    )
    return jax.shard_map(
        per_device, mesh=mesh, in_specs=in_specs, out_specs=out_specs, check_vma=False
    )
```

```python
import functools

import jax
import jax.numpy as jnp
from jax import lax
from jax.experimental import pallas as pl
from jax.experimental.pallas import tpu as pltpu
from jax.sharding import PartitionSpec as P

time_step = 0.4
scale = time_step / 24.0

VX, VY, VZ, SXX, SYY, SZZ, SXY, SXZ, SYZ, MAT = range(10)
LOWER_RAW = (2, 1, 1, 3, 1, 1, 3, 3, 1, 3)
UPPER_RAW = (1, 2, 2, 3, 2, 2, 3, 3, 2, 3)
LOWER_MOVED = ((3, 5), (2, 4), (2, 4))
UPPER_MOVED = ((2, 4), (3, 5), (3, 5))
LOWER_FINE = (VX, VY, VZ, SXX, SXY, SXZ, SYZ)
UPPER_FINE = (VY, VZ, SXX)
RAW, MOVED, FINE = range(3)
EDGE = 5
RIM = 8


def halo_list(raw, moved, fine):
    entries = [(RAW, field, depth) for field in range(10) for depth in range(1, raw[field] + 1)]
    for field, (first, last) in enumerate(moved):
        entries += [(MOVED, field, depth) for depth in range(first, last + 1)]
    return entries + [(FINE, field, 1) for field in fine]


LOWER = halo_list(LOWER_RAW, LOWER_MOVED, LOWER_FINE)
UPPER = halo_list(UPPER_RAW, UPPER_MOVED, UPPER_FINE)
HALO = max(len(LOWER), len(UPPER))

f32 = jnp.float32
bf16 = jnp.bfloat16


def second_core():
    return lax.axis_index("gx") % 2


def fetch_all(sources, targets, sems):
    copies = [
        pltpu.make_async_copy(source, target, sems.at[index])
        for index, (source, target) in enumerate(zip(sources, targets))
    ]
    for copy in copies:
        copy.start()
    return copies


def looked_up(code, tables):
    results = [jnp.zeros(code.shape, f32) for _ in tables]
    for entry in range(tables[0].shape[0]):
        hit = code == entry + 1
        results = [jnp.where(hit, table[entry], result) for table, result in zip(tables, results)]
    return results


def parts_of(behind, here_low, here_high, ahead):
    return here_high - here_low, ahead - behind


def joined(*parts):
    near, far = parts[0]
    for more_near, more_far in parts[1:]:
        near, far = near + more_near, far + more_far
    return 27.0 * near - far


def shifted(values, place, axis, by):
    size = values.shape[axis]
    inside = place < size - by if by > 0 else place >= -by
    return jnp.where(inside, pltpu.roll(values, -by % size, axis), 0.0)


def along(values, place, axis, forward):
    offsets = (-1, 0, 1, 2) if forward else (-2, -1, 0, 1)
    return parts_of(*[values if by == 0 else shifted(values, place, axis, by) for by in offsets])


def stepping(moving, pulling, rows, lanes):
    inner = pl.ds(RIM, rows)
    lane = lax.broadcasted_iota(jnp.int32, (rows, lanes), 1)

    def store(field, place, values):
        if field < 3:
            moving[field, place, inner] = values
        else:
            pulling[field - 3, place, inner] = values

    def read(field, place, at=inner):
        return moving[field, place, at] if field < 3 else pulling[field - 3, place, at]

    def along_x(field, place, forward):
        start = place - 1 if forward else place - 2
        return parts_of(*[read(field, start + step) for step in range(4)])

    def along_y(field, place, forward):
        start = RIM - 1 if forward else RIM - 2
        return parts_of(*[read(field, place, pl.ds(start + step, rows)) for step in range(4)])

    def along_z(field, place, forward):
        return along(read(field, place), lane, 1, forward)

    def pull(field, place):
        if field == VX:
            return joined(along_x(SXX, place, True), along_y(SXY, place, False), along_z(SXZ, place, False))
        if field == VY:
            return joined(along_x(SXY, place, False), along_y(SYY, place, True), along_z(SYZ, place, False))
        return joined(along_x(SXZ, place, False), along_y(SYZ, place, False), along_z(SZZ, place, True))

    return store, read, along_x, along_y, along_z, pull


def pack_kernel(
    velocity_from,
    stress_from,
    material_from,
    buoyancy_from,
    weights_from,
    across,
    within,
    weights,
    moving,
    pulling,
    material,
    buoyancy,
    sems,
    weights_sem,
):
    planes, rows, lanes = material.shape
    slab, inner = pl.ds(EDGE, planes), pl.ds(RIM, rows)
    copies = fetch_all(
        (stress_from, velocity_from, material_from, buoyancy_from),
        (pulling.at[:, slab, inner], moving.at[:, slab, inner], material, buoyancy),
        sems,
    )
    weights_copy = pltpu.make_async_copy(weights_from, weights, weights_sem)
    weights_copy.start()
    blank = jnp.zeros((moving.shape[1], RIM, lanes), f32)
    for ref, fields_along_y in ((moving, (0, 1, 2)), (pulling, (SXY - 3, SYY - 3, SYZ - 3))):
        for field in fields_along_y:
            ref[field, :, 0:RIM] = blank
            ref[field, :, RIM + rows : 2 * RIM + rows] = blank
    store, read, along_x, along_y, along_z, pull = stepping(moving, pulling, rows, lanes)
    odd = second_core()
    for copy in copies:
        copy.wait()

    def moved(field, plane):
        factor = scale * looked_up(material[plane] + 1, (buoyancy,))[0]
        return read(field, EDGE + plane) + factor * pull(field, EDGE + plane)

    def fill(out, entries, plane_of):
        for index, (what, field, depth) in enumerate(entries):
            plane = plane_of(depth)
            if what == MOVED:
                values = moved(field, plane)
            elif field < 9:
                values = read(field, EDGE + plane)
            else:
                values = (material[plane] + 1).astype(f32)
            if what == FINE:
                values = values - values.astype(bf16).astype(f32)
            out[index] = values.astype(bf16)
        for spare in range(len(entries), out.shape[0]):
            out[spare] = jnp.zeros(out.shape[1:], bf16)

    def upper_face(out):
        fill(out, LOWER, lambda depth: planes - depth)

    def lower_face(out):
        fill(out, UPPER, lambda depth: depth - 1)

    @pl.when(odd == 0)
    def _():
        lower_face(across)
        upper_face(within)

    @pl.when(odd != 0)
    def _():
        upper_face(across)
        lower_face(within)

    weights_copy.wait()


def history_kernel(live, slips, history, kept, sent, records, total, record_sems):
    slots = slips.shape[0]
    copies = [
        pltpu.make_async_copy(history.at[slot], records.at[slot], record_sems.at[slot]) for slot in range(slots)
    ]
    copies[0].start()
    for slot in range(1, slots):

        @pl.when(slot < live[0])
        def _(slot=slot):
            copies[slot].start()

    copies[0].wait()
    total[...] = jnp.dot(slips[0], records[0], preferred_element_type=f32)
    for slot in range(1, slots):

        @pl.when(slot < live[0])
        def _(slot=slot):
            copies[slot].wait()
            total[...] += jnp.dot(slips[slot], records[slot], preferred_element_type=f32)

    share = kept.shape[1]
    odd = second_core()
    for pair in range(kept.shape[0]):
        even = total[2 * pair * share : (2 * pair + 1) * share]
        other = total[(2 * pair + 1) * share : (2 * pair + 2) * share]
        kept[pair] = jnp.where(odd == 0, even, other)
        sent[pair] = jnp.where(odd == 0, other, even)


def add_kernel(first, second, out):
    out[...] = first[...] + second[...]


def steps_kernel(
    live,
    cells_from,
    buoyancy_from,
    lame_from,
    shear_from,
    material_from,
    velocity,
    stress,
    weights,
    across,
    within,
    velocity_out,
    stress_out,
    tail,
    moving,
    pulling,
    factors,
    strain_factors,
    strains,
    material,
    slips,
    cells,
    buoyancy_table,
    lame_table,
    shear_table,
    scalar_sems,
    slab_sems,
    out_sems,
):
    planes, rows, lanes = velocity.shape[1:]
    tables = (buoyancy_table, lame_table, shear_table)
    inner = pl.ds(RIM, rows)
    slab = pl.ds(EDGE, planes)
    scalar_copies = fetch_all(
        (buoyancy_from, lame_from, shear_from, material_from, cells_from), (*tables, material, cells), scalar_sems
    )
    slab_copies = fetch_all(
        (stress, velocity, weights), (pulling.at[:, slab, inner], moving.at[:, slab, inner], slips), slab_sems
    )
    odd = second_core()
    store, read, along_x, along_y, along_z, pull = stepping(moving, pulling, rows, lanes)

    blank = jnp.zeros((moving.shape[1], RIM, lanes), f32)
    for ref, fields_along_y in ((moving, (0, 1, 2)), (pulling, (SXY - 3, SYY - 3, SYZ - 3))):
        for field in fields_along_y:
            ref[field, :, 0:RIM] = blank
            ref[field, :, RIM + rows : 2 * RIM + rows] = blank

    for copy in scalar_copies:
        copy.wait()
    for plane in range(planes):
        buoyancy, lame, shear = looked_up(material[plane] + 1, tables)
        factors[0, EDGE + plane] = scale * buoyancy
        factors[1, EDGE + plane] = scale * lame
        factors[2, EDGE + plane] = scale * shear
        strain_factors[0, plane] = lame / (3.0 * lame + 2.0 * shear)
        strain_factors[1, plane] = 1.0 / (2.0 * shear)

    def unpack(halo, upper):
        entries = UPPER if upper else LOWER
        for index, (what, field, depth) in enumerate(entries):
            if what == FINE:
                continue
            place = EDGE + planes + depth - 1 if upper else EDGE - depth
            values = halo[index].astype(f32)
            if what == RAW and (FINE, field, depth) in entries:
                values = values + halo[entries.index((FINE, field, depth))].astype(f32)
            if field < 9:
                store(field, place, values)
            else:
                found = looked_up(values.astype(jnp.int32), tables)
                for kind in range(3):
                    factors[kind, place] = scale * found[kind]

    @pl.when(odd == 0)
    def _():
        unpack(across, False)
        unpack(within, True)

    @pl.when(odd != 0)
    def _():
        unpack(within, False)
        unpack(across, True)

    def move(place, do_x=True, do_yz=True):
        buoyancy = factors[0, place]
        chosen = ([VX] if do_x else []) + ([VY, VZ] if do_yz else [])
        results = [read(field, place) + buoyancy * pull(field, place) for field in chosen]
        for field, values in zip(chosen, results):
            store(field, place, values)

    def strain(place, do_yz=True, keep=None):
        lame, shear = factors[1, place], factors[2, place]
        twice = 2.0 * shear
        exx = joined(along_x(VX, place, False))
        eyy = joined(along_y(VY, place, False))
        ezz = joined(along_z(VZ, place, False))
        common = lame * (exx + eyy + ezz)
        changes = [(SXX, common + twice * exx)]
        changes.append((SXY, shear * joined(along_y(VX, place, True), along_x(VY, place, True))))
        changes.append((SXZ, shear * joined(along_z(VX, place, True), along_x(VZ, place, True))))
        if do_yz:
            changes.append((SYY, common + twice * eyy))
            changes.append((SZZ, common + twice * ezz))
            changes.append((SYZ, shear * joined(along_z(VY, place, True), along_y(VZ, place, True))))
        results = {field: read(field, place) + change for field, change in changes}
        for field, values in results.items():
            store(field, place, values)
        if keep is not None:
            compliance = strain_factors[1, place - EDGE]
            shift = strain_factors[0, place - EDGE] * (results[SXX] + results[SYY] + results[SZZ])
            first = pl.multiple_of((place - EDGE) * (8 * rows), 8 * rows)
            for field in range(3, 9):
                values = results[field] - shift if field < 6 else results[field]
                strains[keep, pl.ds(first + field - 3, rows, stride=8)] = values * compliance

    def over(first, last, body, width=2):
        def group(index, carry):
            for step in range(width):
                body(EDGE + first + index * width + step)
            return carry

        lax.fori_loop(0, (last - first) // width, group, 0)

    for copy in slab_copies[:2]:
        copy.wait()
    top = EDGE + planes
    move(EDGE - 2, do_yz=False)
    move(top + 1, do_x=False)
    over(-1, planes + 1, move)
    for place in range(EDGE - 3, EDGE):
        strain(place, do_yz=place == EDGE - 1)
    over(0, planes, functools.partial(strain, keep=0))
    for place in range(top, top + 3):
        strain(place, do_yz=place < top + 2)
    move(EDGE - 2, do_yz=False)
    move(top + 1, do_x=False)
    over(-1, planes + 1, move)
    out_copies = [
        pltpu.make_async_copy(moving.at[:, slab, inner], velocity_out, out_sems.at[0]),
        pltpu.make_async_copy(pulling.at[:, slab, inner], stress_out, out_sems.at[1]),
    ]
    out_copies[0].start()
    over(0, planes, functools.partial(strain, keep=1))
    out_copies[1].start()

    slab_copies[2].wait()
    points_each = cells.shape[1]
    lane_bits = lanes.bit_length() - 1
    tall = lax.broadcasted_iota(jnp.int32, (8, lanes), 1)

    def add_slot(slot, new):
        found = [jnp.zeros((8, lanes), f32) for _ in range(2)]
        for point in range(points_each):
            cell = cells[slot, point]
            first = pl.multiple_of((cell >> lane_bits) << 3, 8)
            shift = (point - cell) & (lanes - 1)
            hit = tall == point
            for which in range(2):
                turned = pltpu.roll(strains[which, pl.ds(first, 8)], shift, 1)
                found[which] = jnp.where(hit, turned, found[which])
        pair = [jnp.concatenate([values[part : part + 1] for part in range(6)], axis=1) for values in found]
        pair = jnp.concatenate(pair + [jnp.zeros((6, 6 * points_each), f32)], axis=0).astype(bf16)
        return new + lax.dot_general(pair, slips[slot], (((1,), (1,)), ((), ())), preferred_element_type=f32)

    new = lax.fori_loop(0, live[0], add_slot, jnp.zeros((8, slips.shape[1]), f32))
    pieces = slips.shape[1] // lanes
    lines = [new[which : which + 1, piece * lanes : (piece + 1) * lanes] for which in range(2) for piece in range(pieces)]
    lines = jnp.concatenate(lines + [jnp.zeros((8 - 2 * pieces, lanes), f32)], axis=0)
    for device in range(tail.shape[0]):
        tail[device] = lines
    for copy in out_copies:
        copy.wait()


def sum_kernel(partials, out):
    share, samples = out.shape
    total = partials[0]
    for chip in range(1, partials.shape[0]):
        total = total + partials[chip]
    out[...] = jnp.concatenate([total[:, 2:], jnp.zeros((share, 2), f32)], axis=1)


def finish_kernel(older, tails, out):
    share, samples = out.shape
    devices, _, lanes = tails.shape
    new = tails[0]
    for device in range(1, devices):
        new = new + tails[device]
    pieces = share * devices // lanes
    row = lax.broadcasted_iota(jnp.int32, (share, lanes), 0) + lax.axis_index("gx") * share
    column = lax.broadcasted_iota(jnp.int32, (share, lanes), 1)
    sample = lax.broadcasted_iota(jnp.int32, (share, samples), 1)
    total = older[...]
    for which in range(2):
        values = jnp.zeros((share, lanes), f32)
        for piece in range(pieces):
            line = which * pieces + piece
            values = values + jnp.where(row == column + piece * lanes, new[line : line + 1], 0.0)
        values = jnp.sum(values, axis=1, keepdims=True)
        total = jnp.where(sample == samples - 2 + which, values, total)
    out[...] = total


def per_device(
    velocity,
    stress,
    material,
    buoyancy_table,
    lame_table,
    shear_table,
    fault_cells,
    block_count,
    strain_history,
    slip_weights,
):
    count = lax.axis_size("gx")
    planes, rows, lanes = material.shape
    slots, parts, points_each, samples = strain_history.shape
    ruptures = slip_weights.shape[1]
    share = ruptures // count
    whole = pl.BlockSpec(memory_space=pltpu.VMEM)
    scalars = pl.BlockSpec(memory_space=pltpu.SMEM)
    anywhere = pl.BlockSpec(memory_space=pl.ANY)
    params = pltpu.CompilerParams(vmem_limit_bytes=24 * 1024 * 1024)

    def stay(array):
        return pltpu.with_memory_space_constraint(array, pltpu.HBM)

    live = block_count
    velocity, stress, material, slip_weights, cells = [
        stay(array) for array in (velocity, stress, material, slip_weights, fault_cells)
    ]
    tables = [stay(table) for table in (buoyancy_table, lame_table, shear_table)]
    table_scratch = [pltpu.SMEM(table.shape, f32) for table in tables]
    history = stay(strain_history.reshape(slots, parts * points_each, samples))

    def cost(flops, size):
        return pl.CostEstimate(flops=flops, bytes_accessed=size, transcendentals=0)

    halo = pltpu.VMEM((HALO, rows, lanes), bf16)
    extent = planes + 2 * EDGE
    padded = [pltpu.VMEM((fields, extent, rows + 2 * RIM, lanes), f32) for fields in (3, 6)]
    across, within, slips = pl.pallas_call(
        pack_kernel,
        out_shape=(halo, halo, pltpu.VMEM(slip_weights.shape, bf16)),
        in_specs=[anywhere] * 5,
        out_specs=(whole,) * 3,
        scratch_shapes=[
            *padded,
            pltpu.VMEM(material.shape, jnp.int32),
            table_scratch[0],
            pltpu.SemaphoreType.DMA((4,)),
            pltpu.SemaphoreType.DMA,
        ],
        compiler_params=params,
        name="pack_halos",
    )(velocity, stress, material, tables[0], slip_weights)
    chips = [(i, i + 1) for i in range(1, count - 1, 2)]
    cores = [(i, i + 1) for i in range(0, count - 1, 2)]
    cores = cores + [(j, i) for i, j in cores]
    across = lax.ppermute(across, "gx", chips + [(j, i) for i, j in chips])
    within = lax.ppermute(within, "gx", cores)

    half = pltpu.VMEM((count // 2, share, samples), f32)
    kept, sent = pl.pallas_call(
        history_kernel,
        out_shape=(half, half),
        in_specs=[scalars, whole, anywhere],
        out_specs=(whole, whole),
        scratch_shapes=[
            pltpu.VMEM(history.shape, bf16),
            pltpu.VMEM((ruptures, samples), f32),
            pltpu.SemaphoreType.DMA((slots,)),
        ],
        compiler_params=params,
        cost_estimate=cost(2 * slots * ruptures * parts * points_each * samples, 2 * history.size),
        name="history_product",
    )(live, slips, history)
    received = lax.ppermute(sent, "gx", cores)
    chip_sum = pl.pallas_call(
        add_kernel,
        out_shape=jax.ShapeDtypeStruct((count // 2, share, samples), f32),
        in_specs=[whole] * 2,
        out_specs=whole,
        compiler_params=params,
        cost_estimate=cost(10**6, 1024 * 1024),
        name="add_cores",
    )(kept, received)
    same_core = [list(range(core, count, 2)) for core in range(2)]
    partials = lax.all_to_all(chip_sum, "gx", 0, 0, axis_index_groups=same_core, tiled=True)

    velocity_two, stress_two, tail = pl.pallas_call(
        steps_kernel,
        out_shape=(
            jax.ShapeDtypeStruct(velocity.shape, f32),
            jax.ShapeDtypeStruct(stress.shape, f32),
            jax.ShapeDtypeStruct((count, 8, lanes), f32),
        ),
        in_specs=[scalars] + [anywhere] * 8 + [whole] * 2,
        out_specs=(anywhere, anywhere, whole),
        scratch_shapes=[
            *padded,
            pltpu.VMEM((3, extent, rows, lanes), f32),
            pltpu.VMEM((2, planes, rows, lanes), f32),
            pltpu.VMEM((2, planes * rows * 8, lanes), f32),
            pltpu.VMEM(material.shape, jnp.int32),
            pltpu.VMEM(slip_weights.shape, bf16),
            pltpu.SMEM(cells.shape, jnp.int32),
            *table_scratch,
            pltpu.SemaphoreType.DMA((5,)),
            pltpu.SemaphoreType.DMA((3,)),
            pltpu.SemaphoreType.DMA((2,)),
        ],
        compiler_params=params,
        cost_estimate=cost(10**10, 30 * 1024 * 1024),
        name="two_steps",
    )(live, cells, *tables, material, velocity, stress, slip_weights, across, within)
    tails = lax.all_to_all(tail, "gx", 0, 0, tiled=True)

    older = pl.pallas_call(
        sum_kernel,
        out_shape=pltpu.VMEM((share, samples), f32),
        in_specs=[whole],
        out_specs=whole,
        compiler_params=params,
        cost_estimate=cost(10**6, 1024 * 1024),
        name="sum_partials",
    )(partials)
    seismograms = pl.pallas_call(
        finish_kernel,
        out_shape=jax.ShapeDtypeStruct((share, samples), f32),
        in_specs=[whole, whole],
        out_specs=whole,
        compiler_params=params,
        name="join_samples",
    )(older, tails)
    return (velocity_two, stress_two, seismograms)


def solution(mesh):
    in_specs = (
        P(None, ("site", "gx"), None, None),
        P(None, ("site", "gx"), None, None),
        P("gx", None, None),
        P(),
        P(),
        P(),
        P("gx", None),
        P("gx"),
        P(("site", "gx"), None, None, None),
        P("gx", None, None),
    )
    out_specs = (
        P(None, ("site", "gx"), None, None),
        P(None, ("site", "gx"), None, None),
        P(("site", "gx"), None),
    )
    return jax.shard_map(
        per_device, mesh=mesh, in_specs=in_specs, out_specs=out_specs, check_vma=False
    )
```

```python
import functools

import jax
import jax.numpy as jnp
from jax import lax
from jax.experimental import pallas as pl
from jax.experimental.pallas import tpu as pltpu
from jax.sharding import PartitionSpec as P

time_step = 0.4
scale = time_step / 24.0

VX, VY, VZ, SXX, SYY, SZZ, SXY, SXZ, SYZ, MAT = range(10)
LOWER_RAW = (2, 1, 1, 3, 1, 1, 3, 3, 1, 3)
UPPER_RAW = (1, 2, 2, 3, 2, 2, 3, 3, 2, 3)
LOWER_MOVED = ((3, 5), (2, 4), (2, 4))
UPPER_MOVED = ((2, 4), (3, 5), (3, 5))
LOWER_FINE = (VX, VY, VZ, SXX, SXY, SXZ, SYZ)
UPPER_FINE = (VY, VZ, SXX)
RAW, MOVED, FINE = range(3)
EDGE = 5
RIM = 8


def halo_list(raw, moved, fine):
    entries = [(RAW, field, depth) for field in range(10) for depth in range(1, raw[field] + 1)]
    for field, (first, last) in enumerate(moved):
        entries += [(MOVED, field, depth) for depth in range(first, last + 1)]
    return entries + [(FINE, field, 1) for field in fine]


LOWER = halo_list(LOWER_RAW, LOWER_MOVED, LOWER_FINE)
UPPER = halo_list(UPPER_RAW, UPPER_MOVED, UPPER_FINE)
HALO = max(len(LOWER), len(UPPER))

f32 = jnp.float32
bf16 = jnp.bfloat16


def second_core():
    return lax.axis_index("gx") % 2


def fetch_all(sources, targets, sems):
    copies = [
        pltpu.make_async_copy(source, target, sems.at[index])
        for index, (source, target) in enumerate(zip(sources, targets))
    ]
    for copy in copies:
        copy.start()
    return copies


def looked_up(code, tables):
    results = [jnp.zeros(code.shape, f32) for _ in tables]
    for entry in range(tables[0].shape[0]):
        hit = code == entry + 1
        results = [jnp.where(hit, table[entry], result) for table, result in zip(tables, results)]
    return results


def parts_of(behind, here_low, here_high, ahead):
    return here_high - here_low, ahead - behind


def joined(*parts):
    near, far = parts[0]
    for more_near, more_far in parts[1:]:
        near, far = near + more_near, far + more_far
    return 27.0 * near - far


def shifted(values, place, axis, by):
    size = values.shape[axis]
    inside = place < size - by if by > 0 else place >= -by
    return jnp.where(inside, pltpu.roll(values, -by % size, axis), 0.0)


def along(values, place, axis, forward):
    offsets = (-1, 0, 1, 2) if forward else (-2, -1, 0, 1)
    return parts_of(*[values if by == 0 else shifted(values, place, axis, by) for by in offsets])


def stepping(moving, pulling, rows, lanes):
    inner = pl.ds(RIM, rows)
    lane = lax.broadcasted_iota(jnp.int32, (rows, lanes), 1)

    def store(field, place, values):
        if field < 3:
            moving[field, place, inner] = values
        else:
            pulling[field - 3, place, inner] = values

    def read(field, place, at=inner):
        return moving[field, place, at] if field < 3 else pulling[field - 3, place, at]

    def along_x(field, place, forward):
        start = place - 1 if forward else place - 2
        return parts_of(*[read(field, start + step) for step in range(4)])

    def along_y(field, place, forward):
        start = RIM - 1 if forward else RIM - 2
        return parts_of(*[read(field, place, pl.ds(start + step, rows)) for step in range(4)])

    def along_z(field, place, forward):
        return along(read(field, place), lane, 1, forward)

    def pull(field, place):
        if field == VX:
            return joined(along_x(SXX, place, True), along_y(SXY, place, False), along_z(SXZ, place, False))
        if field == VY:
            return joined(along_x(SXY, place, False), along_y(SYY, place, True), along_z(SYZ, place, False))
        return joined(along_x(SXZ, place, False), along_y(SYZ, place, False), along_z(SZZ, place, True))

    return store, read, along_x, along_y, along_z, pull


def pack_kernel(
    velocity_from,
    stress_from,
    material_from,
    buoyancy_from,
    weights_from,
    across,
    within,
    weights,
    moving,
    pulling,
    material,
    buoyancy,
    sems,
    weights_sem,
):
    planes, rows, lanes = material.shape
    slab, inner = pl.ds(EDGE, planes), pl.ds(RIM, rows)
    copies = fetch_all(
        (stress_from, velocity_from, material_from, buoyancy_from),
        (pulling.at[:, slab, inner], moving.at[:, slab, inner], material, buoyancy),
        sems,
    )
    weights_copy = pltpu.make_async_copy(weights_from, weights, weights_sem)
    weights_copy.start()
    blank = jnp.zeros((moving.shape[1], RIM, lanes), f32)
    for ref, fields_along_y in ((moving, (0, 1, 2)), (pulling, (SXY - 3, SYY - 3, SYZ - 3))):
        for field in fields_along_y:
            ref[field, :, 0:RIM] = blank
            ref[field, :, RIM + rows : 2 * RIM + rows] = blank
    store, read, along_x, along_y, along_z, pull = stepping(moving, pulling, rows, lanes)
    odd = second_core()
    for copy in copies:
        copy.wait()

    def moved(field, plane):
        factor = scale * looked_up(material[plane] + 1, (buoyancy,))[0]
        return read(field, EDGE + plane) + factor * pull(field, EDGE + plane)

    def fill(out, entries, plane_of):
        for index, (what, field, depth) in enumerate(entries):
            plane = plane_of(depth)
            if what == MOVED:
                values = moved(field, plane)
            elif field < 9:
                values = read(field, EDGE + plane)
            else:
                values = (material[plane] + 1).astype(f32)
            if what == FINE:
                values = values - values.astype(bf16).astype(f32)
            out[index] = values.astype(bf16)
        for spare in range(len(entries), out.shape[0]):
            out[spare] = jnp.zeros(out.shape[1:], bf16)

    def upper_face(out):
        fill(out, LOWER, lambda depth: planes - depth)

    def lower_face(out):
        fill(out, UPPER, lambda depth: depth - 1)

    @pl.when(odd == 0)
    def _():
        lower_face(across)
        upper_face(within)

    @pl.when(odd != 0)
    def _():
        upper_face(across)
        lower_face(within)

    weights_copy.wait()


def history_kernel(live, slips, history, partial, records, total, record_sems):
    slots = slips.shape[0]
    copies = [
        pltpu.make_async_copy(history.at[slot], records.at[slot], record_sems.at[slot]) for slot in range(slots)
    ]
    copies[0].start()
    for slot in range(1, slots):

        @pl.when(slot < live[0])
        def _(slot=slot):
            copies[slot].start()

    copies[0].wait()
    total[...] = jnp.dot(slips[0], records[0], preferred_element_type=f32)
    for slot in range(1, slots):

        @pl.when(slot < live[0])
        def _(slot=slot):
            copies[slot].wait()
            total[...] += jnp.dot(slips[slot], records[slot], preferred_element_type=f32)

    values = total[...]
    sample = lax.broadcasted_iota(jnp.int32, values.shape, 1)
    largest = jnp.max(jnp.where(sample < 2, 0.0, jnp.abs(values)), axis=1, keepdims=True)
    largest = jnp.maximum(largest, 1e-30)
    exponent = jnp.ceil(jnp.log2(largest)) - 14.0
    steps = jnp.clip(jnp.round(values * jnp.exp2(-exponent)), -32767.0, 32767.0)
    partial[...] = jnp.where(sample == 0, exponent, steps).astype(jnp.int32).astype(jnp.int16)


def steps_kernel(
    live,
    cells_from,
    buoyancy_from,
    lame_from,
    shear_from,
    material_from,
    velocity,
    stress,
    weights,
    across,
    within,
    velocity_out,
    stress_out,
    tail,
    moving,
    pulling,
    factors,
    strain_factors,
    strains,
    material,
    slips,
    cells,
    buoyancy_table,
    lame_table,
    shear_table,
    scalar_sems,
    slab_sems,
    out_sems,
):
    planes, rows, lanes = velocity.shape[1:]
    tables = (buoyancy_table, lame_table, shear_table)
    inner = pl.ds(RIM, rows)
    slab = pl.ds(EDGE, planes)
    scalar_copies = fetch_all(
        (buoyancy_from, lame_from, shear_from, material_from, cells_from), (*tables, material, cells), scalar_sems
    )
    slab_copies = fetch_all(
        (stress, velocity, weights), (pulling.at[:, slab, inner], moving.at[:, slab, inner], slips), slab_sems
    )
    odd = second_core()
    store, read, along_x, along_y, along_z, pull = stepping(moving, pulling, rows, lanes)

    blank = jnp.zeros((moving.shape[1], RIM, lanes), f32)
    for ref, fields_along_y in ((moving, (0, 1, 2)), (pulling, (SXY - 3, SYY - 3, SYZ - 3))):
        for field in fields_along_y:
            ref[field, :, 0:RIM] = blank
            ref[field, :, RIM + rows : 2 * RIM + rows] = blank

    for copy in scalar_copies:
        copy.wait()
    for plane in range(planes):
        buoyancy, lame, shear = looked_up(material[plane] + 1, tables)
        factors[0, EDGE + plane] = scale * buoyancy
        factors[1, EDGE + plane] = scale * lame
        factors[2, EDGE + plane] = scale * shear
        strain_factors[0, plane] = lame / (3.0 * lame + 2.0 * shear)
        strain_factors[1, plane] = 1.0 / (2.0 * shear)

    def unpack(halo, upper):
        entries = UPPER if upper else LOWER
        for index, (what, field, depth) in enumerate(entries):
            if what == FINE:
                continue
            place = EDGE + planes + depth - 1 if upper else EDGE - depth
            values = halo[index].astype(f32)
            if what == RAW and (FINE, field, depth) in entries:
                values = values + halo[entries.index((FINE, field, depth))].astype(f32)
            if field < 9:
                store(field, place, values)
            else:
                found = looked_up(values.astype(jnp.int32), tables)
                for kind in range(3):
                    factors[kind, place] = scale * found[kind]

    @pl.when(odd == 0)
    def _():
        unpack(across, False)
        unpack(within, True)

    @pl.when(odd != 0)
    def _():
        unpack(within, False)
        unpack(across, True)

    def move(place, do_x=True, do_yz=True):
        buoyancy = factors[0, place]
        chosen = ([VX] if do_x else []) + ([VY, VZ] if do_yz else [])
        results = [read(field, place) + buoyancy * pull(field, place) for field in chosen]
        for field, values in zip(chosen, results):
            store(field, place, values)

    def strain(place, do_yz=True, keep=None):
        lame, shear = factors[1, place], factors[2, place]
        twice = 2.0 * shear
        exx = joined(along_x(VX, place, False))
        eyy = joined(along_y(VY, place, False))
        ezz = joined(along_z(VZ, place, False))
        common = lame * (exx + eyy + ezz)
        changes = [(SXX, common + twice * exx)]
        changes.append((SXY, shear * joined(along_y(VX, place, True), along_x(VY, place, True))))
        changes.append((SXZ, shear * joined(along_z(VX, place, True), along_x(VZ, place, True))))
        if do_yz:
            changes.append((SYY, common + twice * eyy))
            changes.append((SZZ, common + twice * ezz))
            changes.append((SYZ, shear * joined(along_z(VY, place, True), along_y(VZ, place, True))))
        results = {field: read(field, place) + change for field, change in changes}
        for field, values in results.items():
            store(field, place, values)
        if keep is not None:
            compliance = strain_factors[1, place - EDGE]
            shift = strain_factors[0, place - EDGE] * (results[SXX] + results[SYY] + results[SZZ])
            first = pl.multiple_of((place - EDGE) * (8 * rows), 8 * rows)
            for field in range(3, 9):
                values = results[field] - shift if field < 6 else results[field]
                strains[keep, pl.ds(first + field - 3, rows, stride=8)] = values * compliance

    def over(first, last, body, width=2):
        def group(index, carry):
            for step in range(width):
                body(EDGE + first + index * width + step)
            return carry

        lax.fori_loop(0, (last - first) // width, group, 0)

    for copy in slab_copies[:2]:
        copy.wait()
    top = EDGE + planes
    move(EDGE - 2, do_yz=False)
    move(top + 1, do_x=False)
    over(-1, planes + 1, move)
    for place in range(EDGE - 3, EDGE):
        strain(place, do_yz=place == EDGE - 1)
    over(0, planes, functools.partial(strain, keep=0))
    for place in range(top, top + 3):
        strain(place, do_yz=place < top + 2)
    move(EDGE - 2, do_yz=False)
    move(top + 1, do_x=False)
    over(-1, planes + 1, move)
    out_copies = [
        pltpu.make_async_copy(moving.at[:, slab, inner], velocity_out, out_sems.at[0]),
        pltpu.make_async_copy(pulling.at[:, slab, inner], stress_out, out_sems.at[1]),
    ]
    out_copies[0].start()
    over(0, planes, functools.partial(strain, keep=1))
    out_copies[1].start()

    slab_copies[2].wait()
    points_each = cells.shape[1]
    lane_bits = lanes.bit_length() - 1
    tall = lax.broadcasted_iota(jnp.int32, (8, lanes), 1)

    def add_slot(slot, new):
        found = [jnp.zeros((8, lanes), f32) for _ in range(2)]
        for point in range(points_each):
            cell = cells[slot, point]
            first = pl.multiple_of((cell >> lane_bits) << 3, 8)
            shift = (point - cell) & (lanes - 1)
            hit = tall == point
            for which in range(2):
                turned = pltpu.roll(strains[which, pl.ds(first, 8)], shift, 1)
                found[which] = jnp.where(hit, turned, found[which])
        pair = [jnp.concatenate([values[part : part + 1] for part in range(6)], axis=1) for values in found]
        pair = jnp.concatenate(pair + [jnp.zeros((6, 6 * points_each), f32)], axis=0).astype(bf16)
        return new + lax.dot_general(pair, slips[slot], (((1,), (1,)), ((), ())), preferred_element_type=f32)

    new = lax.fori_loop(0, live[0], add_slot, jnp.zeros((8, slips.shape[1]), f32))
    pieces = slips.shape[1] // lanes
    lines = [new[which : which + 1, piece * lanes : (piece + 1) * lanes] for which in range(2) for piece in range(pieces)]
    lines = jnp.concatenate(lines + [jnp.zeros((8 - 2 * pieces, lanes), f32)], axis=0)
    for device in range(tail.shape[0]):
        tail[device] = lines
    for copy in out_copies:
        copy.wait()


def sum_kernel(partials, out, values):
    share, samples = out.shape
    steps = partials[...].astype(jnp.int32).astype(f32)
    values[...] = steps * jnp.exp2(steps[:, 0:1])
    total = values[0:share]
    for device in range(1, partials.shape[0] // share):
        total = total + values[device * share : (device + 1) * share]
    out[...] = jnp.concatenate([total[:, 2:], jnp.zeros((share, 2), f32)], axis=1)


def finish_kernel(older, tails, out):
    share, samples = out.shape
    devices, _, lanes = tails.shape
    new = tails[0]
    for device in range(1, devices):
        new = new + tails[device]
    pieces = share * devices // lanes
    row = lax.broadcasted_iota(jnp.int32, (share, lanes), 0) + lax.axis_index("gx") * share
    column = lax.broadcasted_iota(jnp.int32, (share, lanes), 1)
    sample = lax.broadcasted_iota(jnp.int32, (share, samples), 1)
    total = older[...]
    for which in range(2):
        values = jnp.zeros((share, lanes), f32)
        for piece in range(pieces):
            line = which * pieces + piece
            values = values + jnp.where(row == column + piece * lanes, new[line : line + 1], 0.0)
        values = jnp.sum(values, axis=1, keepdims=True)
        total = jnp.where(sample == samples - 2 + which, values, total)
    out[...] = total


def per_device(
    velocity,
    stress,
    material,
    buoyancy_table,
    lame_table,
    shear_table,
    fault_cells,
    block_count,
    strain_history,
    slip_weights,
):
    count = lax.axis_size("gx")
    planes, rows, lanes = material.shape
    slots, parts, points_each, samples = strain_history.shape
    ruptures = slip_weights.shape[1]
    share = ruptures // count
    whole = pl.BlockSpec(memory_space=pltpu.VMEM)
    scalars = pl.BlockSpec(memory_space=pltpu.SMEM)
    anywhere = pl.BlockSpec(memory_space=pl.ANY)
    params = pltpu.CompilerParams(vmem_limit_bytes=24 * 1024 * 1024)

    def stay(array):
        return pltpu.with_memory_space_constraint(array, pltpu.HBM)

    live = block_count
    velocity, stress, material, slip_weights, cells = [
        stay(array) for array in (velocity, stress, material, slip_weights, fault_cells)
    ]
    tables = [stay(table) for table in (buoyancy_table, lame_table, shear_table)]
    table_scratch = [pltpu.SMEM(table.shape, f32) for table in tables]
    history = stay(strain_history.reshape(slots, parts * points_each, samples))

    def cost(flops, size):
        return pl.CostEstimate(flops=flops, bytes_accessed=size, transcendentals=0)

    halo = pltpu.VMEM((HALO, rows, lanes), bf16)
    extent = planes + 2 * EDGE
    padded = [pltpu.VMEM((fields, extent, rows + 2 * RIM, lanes), f32) for fields in (3, 6)]
    across, within, slips = pl.pallas_call(
        pack_kernel,
        out_shape=(halo, halo, pltpu.VMEM(slip_weights.shape, bf16)),
        in_specs=[anywhere] * 5,
        out_specs=(whole,) * 3,
        scratch_shapes=[
            *padded,
            pltpu.VMEM(material.shape, jnp.int32),
            table_scratch[0],
            pltpu.SemaphoreType.DMA((4,)),
            pltpu.SemaphoreType.DMA,
        ],
        compiler_params=params,
        name="pack_halos",
    )(velocity, stress, material, tables[0], slip_weights)
    chips = [(i, i + 1) for i in range(1, count - 1, 2)]
    cores = [(i, i + 1) for i in range(0, count - 1, 2)]
    cores = cores + [(j, i) for i, j in cores]
    across = lax.ppermute(across, "gx", chips + [(j, i) for i, j in chips])
    within = lax.ppermute(within, "gx", cores)

    partial = pl.pallas_call(
        history_kernel,
        out_shape=jax.ShapeDtypeStruct((ruptures, samples), jnp.int16),
        in_specs=[scalars, whole, anywhere],
        out_specs=whole,
        scratch_shapes=[
            pltpu.VMEM(history.shape, bf16),
            pltpu.VMEM((ruptures, samples), f32),
            pltpu.SemaphoreType.DMA((slots,)),
        ],
        compiler_params=params,
        cost_estimate=cost(2 * slots * ruptures * parts * points_each * samples, 2 * history.size),
        name="history_product",
    )(live, slips, history)
    partials = lax.all_to_all(partial, "gx", 0, 0, tiled=True)

    velocity_two, stress_two, tail = pl.pallas_call(
        steps_kernel,
        out_shape=(
            jax.ShapeDtypeStruct(velocity.shape, f32),
            jax.ShapeDtypeStruct(stress.shape, f32),
            jax.ShapeDtypeStruct((count, 8, lanes), f32),
        ),
        in_specs=[scalars] + [anywhere] * 8 + [whole] * 2,
        out_specs=(anywhere, anywhere, whole),
        scratch_shapes=[
            *padded,
            pltpu.VMEM((3, extent, rows, lanes), f32),
            pltpu.VMEM((2, planes, rows, lanes), f32),
            pltpu.VMEM((2, planes * rows * 8, lanes), f32),
            pltpu.VMEM(material.shape, jnp.int32),
            pltpu.VMEM(slip_weights.shape, bf16),
            pltpu.SMEM(cells.shape, jnp.int32),
            *table_scratch,
            pltpu.SemaphoreType.DMA((5,)),
            pltpu.SemaphoreType.DMA((3,)),
            pltpu.SemaphoreType.DMA((2,)),
        ],
        compiler_params=params,
        cost_estimate=cost(10**10, 30 * 1024 * 1024),
        name="two_steps",
    )(live, cells, *tables, material, velocity, stress, slip_weights, across, within)
    tails = lax.all_to_all(tail, "gx", 0, 0, tiled=True)

    older = pl.pallas_call(
        sum_kernel,
        out_shape=pltpu.VMEM((share, samples), f32),
        in_specs=[whole],
        out_specs=whole,
        scratch_shapes=[pltpu.VMEM((ruptures, samples), f32)],
        compiler_params=params,
        cost_estimate=cost(10**6, 1024 * 1024),
        name="sum_partials",
    )(partials)
    seismograms = pl.pallas_call(
        finish_kernel,
        out_shape=jax.ShapeDtypeStruct((share, samples), f32),
        in_specs=[whole, whole],
        out_specs=whole,
        compiler_params=params,
        name="join_samples",
    )(older, tails)
    return (velocity_two, stress_two, seismograms)


def solution(mesh):
    in_specs = (
        P(None, ("site", "gx"), None, None),
        P(None, ("site", "gx"), None, None),
        P("gx", None, None),
        P(),
        P(),
        P(),
        P("gx", None),
        P("gx"),
        P(("site", "gx"), None, None, None),
        P("gx", None, None),
    )
    out_specs = (
        P(None, ("site", "gx"), None, None),
        P(None, ("site", "gx"), None, None),
        P(("site", "gx"), None),
    )
    return jax.shard_map(
        per_device, mesh=mesh, in_specs=in_specs, out_specs=out_specs, check_vma=False
    )
```

```python
import functools

import jax
import jax.numpy as jnp
from jax import lax
from jax.experimental import pallas as pl
from jax.experimental.pallas import tpu as pltpu
from jax.sharding import PartitionSpec as P

time_step = 0.4
scale = time_step / 24.0

VX, VY, VZ, SXX, SYY, SZZ, SXY, SXZ, SYZ, MAT = range(10)
LOWER_RAW = (2, 1, 1, 3, 1, 1, 3, 3, 1, 3)
UPPER_RAW = (1, 2, 2, 3, 2, 2, 3, 3, 2, 3)
LOWER_MOVED = ((3, 5), (2, 4), (2, 4))
UPPER_MOVED = ((2, 4), (3, 5), (3, 5))
LOWER_FINE = (VX, VY, VZ, SXX, SXY, SXZ, SYZ)
UPPER_FINE = (VY, VZ, SXX)
RAW, MOVED, FINE = range(3)
EDGE = 5
RIM = 8


def halo_list(raw, moved, fine):
    entries = [(RAW, field, depth) for field in range(10) for depth in range(1, raw[field] + 1)]
    for field, (first, last) in enumerate(moved):
        entries += [(MOVED, field, depth) for depth in range(first, last + 1)]
    return entries + [(FINE, field, 1) for field in fine]


LOWER = halo_list(LOWER_RAW, LOWER_MOVED, LOWER_FINE)
UPPER = halo_list(UPPER_RAW, UPPER_MOVED, UPPER_FINE)
HALO = max(len(LOWER), len(UPPER))

f32 = jnp.float32
bf16 = jnp.bfloat16


def second_core():
    return lax.axis_index("gx") % 2


def fetch_all(sources, targets, sems):
    copies = [
        pltpu.make_async_copy(source, target, sems.at[index])
        for index, (source, target) in enumerate(zip(sources, targets))
    ]
    for copy in copies:
        copy.start()
    return copies


def looked_up(code, tables):
    results = [jnp.zeros(code.shape, f32) for _ in tables]
    for entry in range(tables[0].shape[0]):
        hit = code == entry + 1
        results = [jnp.where(hit, table[entry], result) for table, result in zip(tables, results)]
    return results


def parts_of(behind, here_low, here_high, ahead):
    return here_high - here_low, ahead - behind


def joined(*parts):
    near, far = parts[0]
    for more_near, more_far in parts[1:]:
        near, far = near + more_near, far + more_far
    return 27.0 * near - far


def shifted(values, place, axis, by):
    size = values.shape[axis]
    inside = place < size - by if by > 0 else place >= -by
    return jnp.where(inside, pltpu.roll(values, -by % size, axis), 0.0)


def along(values, place, axis, forward):
    offsets = (-1, 0, 1, 2) if forward else (-2, -1, 0, 1)
    return parts_of(*[values if by == 0 else shifted(values, place, axis, by) for by in offsets])


def stepping(moving, pulling, rows, lanes):
    inner = pl.ds(RIM, rows)
    lane = lax.broadcasted_iota(jnp.int32, (rows, lanes), 1)

    def store(field, place, values):
        if field < 3:
            moving[field, place, inner] = values
        else:
            pulling[field - 3, place, inner] = values

    def read(field, place, at=inner):
        return moving[field, place, at] if field < 3 else pulling[field - 3, place, at]

    def along_x(field, place, forward):
        start = place - 1 if forward else place - 2
        return parts_of(*[read(field, start + step) for step in range(4)])

    def along_y(field, place, forward):
        start = RIM - 1 if forward else RIM - 2
        return parts_of(*[read(field, place, pl.ds(start + step, rows)) for step in range(4)])

    def along_z(field, place, forward):
        return along(read(field, place), lane, 1, forward)

    def pull(field, place):
        if field == VX:
            return joined(along_x(SXX, place, True), along_y(SXY, place, False), along_z(SXZ, place, False))
        if field == VY:
            return joined(along_x(SXY, place, False), along_y(SYY, place, True), along_z(SYZ, place, False))
        return joined(along_x(SXZ, place, False), along_y(SYZ, place, False), along_z(SZZ, place, True))

    return store, read, along_x, along_y, along_z, pull


def pack_kernel(
    velocity_from,
    stress_from,
    material_from,
    buoyancy_from,
    weights_from,
    across,
    within,
    weights,
    moving,
    pulling,
    material,
    buoyancy,
    sems,
    weights_sem,
):
    planes, rows, lanes = material.shape
    slab, inner = pl.ds(EDGE, planes), pl.ds(RIM, rows)
    copies = fetch_all(
        (stress_from, velocity_from, material_from, buoyancy_from),
        (pulling.at[:, slab, inner], moving.at[:, slab, inner], material, buoyancy),
        sems,
    )
    weights_copy = pltpu.make_async_copy(weights_from, weights, weights_sem)
    weights_copy.start()
    blank = jnp.zeros((moving.shape[1], RIM, lanes), f32)
    for ref, fields_along_y in ((moving, (0, 1, 2)), (pulling, (SXY - 3, SYY - 3, SYZ - 3))):
        for field in fields_along_y:
            ref[field, :, 0:RIM] = blank
            ref[field, :, RIM + rows : 2 * RIM + rows] = blank
    store, read, along_x, along_y, along_z, pull = stepping(moving, pulling, rows, lanes)
    odd = second_core()
    for copy in copies:
        copy.wait()

    def moved(field, plane):
        factor = scale * looked_up(material[plane] + 1, (buoyancy,))[0]
        return read(field, EDGE + plane) + factor * pull(field, EDGE + plane)

    def fill(out, entries, plane_of):
        for index, (what, field, depth) in enumerate(entries):
            plane = plane_of(depth)
            if what == MOVED:
                values = moved(field, plane)
            elif field < 9:
                values = read(field, EDGE + plane)
            else:
                values = (material[plane] + 1).astype(f32)
            if what == FINE:
                values = values - values.astype(bf16).astype(f32)
            out[index] = values.astype(bf16)
        for spare in range(len(entries), out.shape[0]):
            out[spare] = jnp.zeros(out.shape[1:], bf16)

    def upper_face(out):
        fill(out, LOWER, lambda depth: planes - depth)

    def lower_face(out):
        fill(out, UPPER, lambda depth: depth - 1)

    @pl.when(odd == 0)
    def _():
        lower_face(across)
        upper_face(within)

    @pl.when(odd != 0)
    def _():
        upper_face(across)
        lower_face(within)

    weights_copy.wait()


def in_steps(values, counted):
    largest = jnp.max(jnp.where(counted, jnp.abs(values), 0.0), axis=1, keepdims=True)
    exponent = jnp.ceil(jnp.log2(jnp.maximum(largest, 1e-30))) - 14.0
    return exponent, jnp.clip(jnp.round(values * jnp.exp2(-exponent)), -32767.0, 32767.0)


def history_kernel(live, slips, history, partial, records, total, record_sems):
    slots = slips.shape[0]
    copies = [
        pltpu.make_async_copy(history.at[slot], records.at[slot], record_sems.at[slot]) for slot in range(slots)
    ]
    copies[0].start()
    for slot in range(1, slots):

        @pl.when(slot < live[0])
        def _(slot=slot):
            copies[slot].start()

    copies[0].wait()
    total[...] = jnp.dot(slips[0], records[0], preferred_element_type=f32)
    for slot in range(1, slots):

        @pl.when(slot < live[0])
        def _(slot=slot):
            copies[slot].wait()
            total[...] += jnp.dot(slips[slot], records[slot], preferred_element_type=f32)

    values = total[...]
    sample = lax.broadcasted_iota(jnp.int32, values.shape, 1)
    exponent, steps = in_steps(values, sample >= 2)
    partial[...] = jnp.where(sample == 0, exponent, steps).astype(jnp.int32).astype(jnp.int16)


def steps_kernel(
    live,
    cells_from,
    buoyancy_from,
    lame_from,
    shear_from,
    material_from,
    velocity,
    stress,
    weights,
    across,
    within,
    partial,
    velocity_out,
    stress_out,
    sums,
    moving,
    pulling,
    factors,
    strain_factors,
    strains,
    material,
    slips,
    cells,
    buoyancy_table,
    lame_table,
    shear_table,
    tail,
    scalar_sems,
    slab_sems,
    out_sems,
):
    planes, rows, lanes = velocity.shape[1:]
    tables = (buoyancy_table, lame_table, shear_table)
    inner = pl.ds(RIM, rows)
    slab = pl.ds(EDGE, planes)
    scalar_copies = fetch_all(
        (buoyancy_from, lame_from, shear_from, material_from, cells_from), (*tables, material, cells), scalar_sems
    )
    slab_copies = fetch_all(
        (stress, velocity, weights), (pulling.at[:, slab, inner], moving.at[:, slab, inner], slips), slab_sems
    )
    samples = partial.shape[1]
    sum_copies = [
        pltpu.make_async_copy(partial, sums.at[:, pl.ds(0, samples)], out_sems.at[2]),
        pltpu.make_async_copy(tail, sums.at[:, pl.ds(samples, lanes)], out_sems.at[3]),
    ]
    sum_copies[0].start()
    odd = second_core()
    store, read, along_x, along_y, along_z, pull = stepping(moving, pulling, rows, lanes)

    blank = jnp.zeros((moving.shape[1], RIM, lanes), f32)
    for ref, fields_along_y in ((moving, (0, 1, 2)), (pulling, (SXY - 3, SYY - 3, SYZ - 3))):
        for field in fields_along_y:
            ref[field, :, 0:RIM] = blank
            ref[field, :, RIM + rows : 2 * RIM + rows] = blank

    for copy in scalar_copies:
        copy.wait()
    for plane in range(planes):
        buoyancy, lame, shear = looked_up(material[plane] + 1, tables)
        factors[0, EDGE + plane] = scale * buoyancy
        factors[1, EDGE + plane] = scale * lame
        factors[2, EDGE + plane] = scale * shear
        strain_factors[0, plane] = lame / (3.0 * lame + 2.0 * shear)
        strain_factors[1, plane] = 1.0 / (2.0 * shear)

    def unpack(halo, upper):
        entries = UPPER if upper else LOWER
        for index, (what, field, depth) in enumerate(entries):
            if what == FINE:
                continue
            place = EDGE + planes + depth - 1 if upper else EDGE - depth
            values = halo[index].astype(f32)
            if what == RAW and (FINE, field, depth) in entries:
                values = values + halo[entries.index((FINE, field, depth))].astype(f32)
            if field < 9:
                store(field, place, values)
            else:
                found = looked_up(values.astype(jnp.int32), tables)
                for kind in range(3):
                    factors[kind, place] = scale * found[kind]

    @pl.when(odd == 0)
    def _():
        unpack(across, False)
        unpack(within, True)

    @pl.when(odd != 0)
    def _():
        unpack(within, False)
        unpack(across, True)

    def move(place, do_x=True, do_yz=True):
        buoyancy = factors[0, place]
        chosen = ([VX] if do_x else []) + ([VY, VZ] if do_yz else [])
        results = [read(field, place) + buoyancy * pull(field, place) for field in chosen]
        for field, values in zip(chosen, results):
            store(field, place, values)

    def strain(place, do_yz=True, keep=None):
        lame, shear = factors[1, place], factors[2, place]
        twice = 2.0 * shear
        exx = joined(along_x(VX, place, False))
        eyy = joined(along_y(VY, place, False))
        ezz = joined(along_z(VZ, place, False))
        common = lame * (exx + eyy + ezz)
        changes = [(SXX, common + twice * exx)]
        changes.append((SXY, shear * joined(along_y(VX, place, True), along_x(VY, place, True))))
        changes.append((SXZ, shear * joined(along_z(VX, place, True), along_x(VZ, place, True))))
        if do_yz:
            changes.append((SYY, common + twice * eyy))
            changes.append((SZZ, common + twice * ezz))
            changes.append((SYZ, shear * joined(along_z(VY, place, True), along_y(VZ, place, True))))
        results = {field: read(field, place) + change for field, change in changes}
        for field, values in results.items():
            store(field, place, values)
        if keep is not None:
            compliance = strain_factors[1, place - EDGE]
            shift = strain_factors[0, place - EDGE] * (results[SXX] + results[SYY] + results[SZZ])
            first = pl.multiple_of((place - EDGE) * (8 * rows), 8 * rows)
            for field in range(3, 9):
                values = results[field] - shift if field < 6 else results[field]
                strains[keep, pl.ds(first + field - 3, rows, stride=8)] = values * compliance

    def over(first, last, body, width=2):
        def group(index, carry):
            for step in range(width):
                body(EDGE + first + index * width + step)
            return carry

        lax.fori_loop(0, (last - first) // width, group, 0)

    for copy in slab_copies[:2]:
        copy.wait()
    top = EDGE + planes
    move(EDGE - 2, do_yz=False)
    move(top + 1, do_x=False)
    over(-1, planes + 1, move)
    for place in range(EDGE - 3, EDGE):
        strain(place, do_yz=place == EDGE - 1)
    over(0, planes, functools.partial(strain, keep=0))
    for place in range(top, top + 3):
        strain(place, do_yz=place < top + 2)
    move(EDGE - 2, do_yz=False)
    move(top + 1, do_x=False)
    over(-1, planes + 1, move)
    out_copies = [
        pltpu.make_async_copy(moving.at[:, slab, inner], velocity_out, out_sems.at[0]),
        pltpu.make_async_copy(pulling.at[:, slab, inner], stress_out, out_sems.at[1]),
    ]
    out_copies[0].start()
    over(0, planes, functools.partial(strain, keep=1))
    out_copies[1].start()

    slab_copies[2].wait()
    points_each = cells.shape[1]
    lane_bits = lanes.bit_length() - 1
    tall = lax.broadcasted_iota(jnp.int32, (8, lanes), 1)

    def add_slot(slot, new):
        found = [jnp.zeros((8, lanes), f32) for _ in range(2)]
        for point in range(points_each):
            cell = cells[slot, point]
            first = pl.multiple_of((cell >> lane_bits) << 3, 8)
            shift = (point - cell) & (lanes - 1)
            hit = tall == point
            for which in range(2):
                turned = pltpu.roll(strains[which, pl.ds(first, 8)], shift, 1)
                found[which] = jnp.where(hit, turned, found[which])
        pair = [jnp.concatenate([values[part : part + 1] for part in range(6)], axis=1) for values in found]
        pair = jnp.concatenate(pair + [jnp.zeros((lanes - 2, 6 * points_each), f32)], axis=0).astype(bf16)
        return new + lax.dot_general(slips[slot], pair, (((1,), (1,)), ((), ())), preferred_element_type=f32)

    new = lax.fori_loop(0, live[0], add_slot, jnp.zeros((slips.shape[1], lanes), f32))
    column = lax.broadcasted_iota(jnp.int32, new.shape, 1)
    exponent, steps = in_steps(new, column < 2)
    tail[...] = jnp.where(column == 2, exponent, steps).astype(jnp.int32).astype(jnp.int16)
    sum_copies[1].start()
    for copy in out_copies + sum_copies:
        copy.wait()


def sum_kernel(sums, out, values, news):
    share, samples = out.shape
    steps = sums[:, 0:samples].astype(jnp.int32).astype(f32)
    values[...] = steps * jnp.exp2(steps[:, 0:1])
    steps = sums[:, samples:].astype(jnp.int32).astype(f32)
    news[...] = steps * jnp.exp2(steps[:, 2:3])
    total, new = values[0:share], news[0:share]
    for device in range(1, sums.shape[0] // share):
        at = slice(device * share, (device + 1) * share)
        total, new = total + values[at], new + news[at]
    out[...] = jnp.concatenate([total[:, 2:], new[:, 0:2]], axis=1)


def per_device(
    velocity,
    stress,
    material,
    buoyancy_table,
    lame_table,
    shear_table,
    fault_cells,
    block_count,
    strain_history,
    slip_weights,
):
    count = lax.axis_size("gx")
    planes, rows, lanes = material.shape
    slots, parts, points_each, samples = strain_history.shape
    ruptures = slip_weights.shape[1]
    share = ruptures // count
    whole = pl.BlockSpec(memory_space=pltpu.VMEM)
    scalars = pl.BlockSpec(memory_space=pltpu.SMEM)
    anywhere = pl.BlockSpec(memory_space=pl.ANY)
    params = pltpu.CompilerParams(vmem_limit_bytes=24 * 1024 * 1024)

    def stay(array):
        return pltpu.with_memory_space_constraint(array, pltpu.HBM)

    live = block_count
    velocity, stress, material, slip_weights, cells = [
        stay(array) for array in (velocity, stress, material, slip_weights, fault_cells)
    ]
    tables = [stay(table) for table in (buoyancy_table, lame_table, shear_table)]
    table_scratch = [pltpu.SMEM(table.shape, f32) for table in tables]
    history = stay(strain_history.reshape(slots, parts * points_each, samples))

    def cost(flops, size):
        return pl.CostEstimate(flops=flops, bytes_accessed=size, transcendentals=0)

    halo = pltpu.VMEM((HALO, rows, lanes), bf16)
    extent = planes + 2 * EDGE
    padded = [pltpu.VMEM((fields, extent, rows + 2 * RIM, lanes), f32) for fields in (3, 6)]
    across, within, slips = pl.pallas_call(
        pack_kernel,
        out_shape=(halo, halo, pltpu.VMEM(slip_weights.shape, bf16)),
        in_specs=[anywhere] * 5,
        out_specs=(whole,) * 3,
        scratch_shapes=[
            *padded,
            pltpu.VMEM(material.shape, jnp.int32),
            table_scratch[0],
            pltpu.SemaphoreType.DMA((4,)),
            pltpu.SemaphoreType.DMA,
        ],
        compiler_params=params,
        name="pack_halos",
    )(velocity, stress, material, tables[0], slip_weights)
    chips = [(i, i + 1) for i in range(1, count - 1, 2)]
    cores = [(i, i + 1) for i in range(0, count - 1, 2)]
    cores = cores + [(j, i) for i, j in cores]
    across = lax.ppermute(across, "gx", chips + [(j, i) for i, j in chips])
    within = lax.ppermute(within, "gx", cores)

    partial = pl.pallas_call(
        history_kernel,
        out_shape=pltpu.VMEM((ruptures, samples), jnp.int16),
        in_specs=[scalars, whole, anywhere],
        out_specs=whole,
        scratch_shapes=[
            pltpu.VMEM(history.shape, bf16),
            pltpu.VMEM((ruptures, samples), f32),
            pltpu.SemaphoreType.DMA((slots,)),
        ],
        compiler_params=params,
        cost_estimate=cost(2 * slots * ruptures * parts * points_each * samples, 2 * history.size),
        name="history_product",
    )(live, slips, history)

    velocity_two, stress_two, sums = pl.pallas_call(
        steps_kernel,
        out_shape=(
            jax.ShapeDtypeStruct(velocity.shape, f32),
            jax.ShapeDtypeStruct(stress.shape, f32),
            jax.ShapeDtypeStruct((ruptures, samples + lanes), jnp.int16),
        ),
        in_specs=[scalars] + [anywhere] * 8 + [whole] * 3,
        out_specs=(anywhere,) * 3,
        scratch_shapes=[
            *padded,
            pltpu.VMEM((3, extent, rows, lanes), f32),
            pltpu.VMEM((2, planes, rows, lanes), f32),
            pltpu.VMEM((2, planes * rows * 8, lanes), f32),
            pltpu.VMEM(material.shape, jnp.int32),
            pltpu.VMEM(slip_weights.shape, bf16),
            pltpu.SMEM(cells.shape, jnp.int32),
            *table_scratch,
            pltpu.VMEM((ruptures, lanes), jnp.int16),
            pltpu.SemaphoreType.DMA((5,)),
            pltpu.SemaphoreType.DMA((3,)),
            pltpu.SemaphoreType.DMA((4,)),
        ],
        compiler_params=params,
        cost_estimate=cost(10**10, 30 * 1024 * 1024),
        name="two_steps",
    )(live, cells, *tables, material, velocity, stress, slip_weights, across, within, partial)
    sums = lax.all_to_all(sums, "gx", 0, 0, tiled=True)
    seismograms = pl.pallas_call(
        sum_kernel,
        out_shape=jax.ShapeDtypeStruct((share, samples), f32),
        in_specs=[whole],
        out_specs=whole,
        scratch_shapes=[pltpu.VMEM((ruptures, samples), f32), pltpu.VMEM((ruptures, lanes), f32)],
        compiler_params=params,
        name="sum_partials",
    )(sums)
    return (velocity_two, stress_two, seismograms)


def solution(mesh):
    in_specs = (
        P(None, ("site", "gx"), None, None),
        P(None, ("site", "gx"), None, None),
        P("gx", None, None),
        P(),
        P(),
        P(),
        P("gx", None),
        P("gx"),
        P(("site", "gx"), None, None, None),
        P("gx", None, None),
    )
    out_specs = (
        P(None, ("site", "gx"), None, None),
        P(None, ("site", "gx"), None, None),
        P(("site", "gx"), None),
    )
    return jax.shard_map(
        per_device, mesh=mesh, in_specs=in_specs, out_specs=out_specs, check_vma=False
    )
```

```python
import functools

import jax
import jax.numpy as jnp
from jax import lax
from jax.experimental import pallas as pl
from jax.experimental.pallas import tpu as pltpu
from jax.sharding import PartitionSpec as P

time_step = 0.4
scale = time_step / 24.0

VX, VY, VZ, SXX, SYY, SZZ, SXY, SXZ, SYZ, MAT = range(10)
LOWER_RAW = (2, 1, 1, 3, 1, 1, 3, 3, 1, 3)
UPPER_RAW = (1, 2, 2, 3, 2, 2, 3, 3, 2, 3)
LOWER_MOVED = ((3, 5), (2, 4), (2, 4))
UPPER_MOVED = ((2, 4), (3, 5), (3, 5))
LOWER_FINE = (VX, VY, VZ, SXX, SXY, SXZ, SYZ)
UPPER_FINE = (VY, VZ, SXX)
RAW, MOVED, FINE = range(3)
EDGE = 5
RIM = 8


def halo_list(raw, moved, fine):
    entries = [(RAW, field, depth) for field in range(10) for depth in range(1, raw[field] + 1)]
    for field, (first, last) in enumerate(moved):
        entries += [(MOVED, field, depth) for depth in range(first, last + 1)]
    return entries + [(FINE, field, 1) for field in fine]


LOWER = halo_list(LOWER_RAW, LOWER_MOVED, LOWER_FINE)
UPPER = halo_list(UPPER_RAW, UPPER_MOVED, UPPER_FINE)
HALO = max(len(LOWER), len(UPPER))

f32 = jnp.float32
bf16 = jnp.bfloat16


def second_core():
    return lax.axis_index("gx") % 2


def fetch_all(sources, targets, sems):
    copies = [
        pltpu.make_async_copy(source, target, sems.at[index])
        for index, (source, target) in enumerate(zip(sources, targets))
    ]
    for copy in copies:
        copy.start()
    return copies


def looked_up(code, tables):
    results = [jnp.zeros(code.shape, f32) for _ in tables]
    for entry in range(tables[0].shape[0]):
        hit = code == entry + 1
        results = [jnp.where(hit, table[entry], result) for table, result in zip(tables, results)]
    return results


def parts_of(behind, here_low, here_high, ahead):
    return here_high - here_low, ahead - behind


def joined(*parts):
    near, far = parts[0]
    for more_near, more_far in parts[1:]:
        near, far = near + more_near, far + more_far
    return 27.0 * near - far


def shifted(values, place, axis, by):
    size = values.shape[axis]
    inside = place < size - by if by > 0 else place >= -by
    return jnp.where(inside, pltpu.roll(values, -by % size, axis), 0.0)


def along(values, place, axis, forward):
    offsets = (-1, 0, 1, 2) if forward else (-2, -1, 0, 1)
    return parts_of(*[values if by == 0 else shifted(values, place, axis, by) for by in offsets])


def stepping(moving, pulling, rows, lanes):
    inner = pl.ds(RIM, rows)
    lane = lax.broadcasted_iota(jnp.int32, (rows, lanes), 1)

    def store(field, place, values):
        if field < 3:
            moving[field, place, inner] = values
        else:
            pulling[field - 3, place, inner] = values

    def read(field, place, at=inner):
        return moving[field, place, at] if field < 3 else pulling[field - 3, place, at]

    def along_x(field, place, forward):
        start = place - 1 if forward else place - 2
        return parts_of(*[read(field, start + step) for step in range(4)])

    def along_y(field, place, forward):
        start = RIM - 1 if forward else RIM - 2
        return parts_of(*[read(field, place, pl.ds(start + step, rows)) for step in range(4)])

    def along_z(field, place, forward):
        return along(read(field, place), lane, 1, forward)

    def pull(field, place):
        if field == VX:
            return joined(along_x(SXX, place, True), along_y(SXY, place, False), along_z(SXZ, place, False))
        if field == VY:
            return joined(along_x(SXY, place, False), along_y(SYY, place, True), along_z(SYZ, place, False))
        return joined(along_x(SXZ, place, False), along_y(SYZ, place, False), along_z(SZZ, place, True))

    return store, read, along_x, along_y, along_z, pull


def pack_kernel(
    velocity_from,
    stress_from,
    material_from,
    buoyancy_from,
    weights_from,
    across,
    within,
    weights,
    moving,
    pulling,
    material,
    buoyancy,
    sems,
    weights_sem,
):
    planes, rows, lanes = material.shape
    slab, inner = pl.ds(EDGE, planes), pl.ds(RIM, rows)
    copies = fetch_all(
        (stress_from, velocity_from, material_from, buoyancy_from),
        (pulling.at[:, slab, inner], moving.at[:, slab, inner], material, buoyancy),
        sems,
    )
    weights_copy = pltpu.make_async_copy(weights_from, weights, weights_sem)
    weights_copy.start()
    blank = jnp.zeros((moving.shape[1], RIM, lanes), f32)
    for ref, fields_along_y in ((moving, (0, 1, 2)), (pulling, (SXY - 3, SYY - 3, SYZ - 3))):
        for field in fields_along_y:
            ref[field, :, 0:RIM] = blank
            ref[field, :, RIM + rows : 2 * RIM + rows] = blank
    store, read, along_x, along_y, along_z, pull = stepping(moving, pulling, rows, lanes)
    odd = second_core()
    for copy in copies:
        copy.wait()

    def moved(field, plane):
        factor = scale * looked_up(material[plane] + 1, (buoyancy,))[0]
        return read(field, EDGE + plane) + factor * pull(field, EDGE + plane)

    def fill(out, entries, plane_of):
        for index, (what, field, depth) in enumerate(entries):
            plane = plane_of(depth)
            if what == MOVED:
                values = moved(field, plane)
            elif field < 9:
                values = read(field, EDGE + plane)
            else:
                values = (material[plane] + 1).astype(f32)
            if what == FINE:
                values = values - values.astype(bf16).astype(f32)
            out[index] = values.astype(bf16)
        for spare in range(len(entries), out.shape[0]):
            out[spare] = jnp.zeros(out.shape[1:], bf16)

    def upper_face(out):
        fill(out, LOWER, lambda depth: planes - depth)

    def lower_face(out):
        fill(out, UPPER, lambda depth: depth - 1)

    @pl.when(odd == 0)
    def _():
        lower_face(across)
        upper_face(within)

    @pl.when(odd != 0)
    def _():
        upper_face(across)
        lower_face(within)

    weights_copy.wait()


def in_steps(values):
    largest = jnp.max(jnp.abs(values), axis=1, keepdims=True)
    exponent = jnp.ceil(jnp.log2(jnp.maximum(largest, 1e-30))) - 14.0
    return exponent, jnp.clip(jnp.round(values * jnp.exp2(-exponent)), -32767.0, 32767.0)


def history_kernel(live, slips, history, kept, sent, records, total, record_sems):
    slots = slips.shape[0]
    copies = [
        pltpu.make_async_copy(history.at[slot], records.at[slot], record_sems.at[slot]) for slot in range(slots)
    ]
    copies[0].start()
    for slot in range(1, slots):

        @pl.when(slot < live[0])
        def _(slot=slot):
            copies[slot].start()

    copies[0].wait()
    total[...] = jnp.dot(slips[0], records[0], preferred_element_type=f32)
    for slot in range(1, slots):

        @pl.when(slot < live[0])
        def _(slot=slot):
            copies[slot].wait()
            total[...] += jnp.dot(slips[slot], records[slot], preferred_element_type=f32)

    half = kept.shape[1]
    first = second_core() == 0
    early, late = total[:, :half], total[:, half:]
    early = jnp.where(lax.broadcasted_iota(jnp.int32, early.shape, 1) < 2, 0.0, early)
    kept[...] = jnp.where(first, early, late)
    sent[...] = jnp.where(first, late, early)


def steps_kernel(
    live,
    cells_from,
    buoyancy_from,
    lame_from,
    shear_from,
    material_from,
    velocity,
    stress,
    weights,
    across,
    within,
    kept,
    received,
    velocity_out,
    stress_out,
    sums,
    moving,
    pulling,
    factors,
    strain_factors,
    strains,
    material,
    slips,
    cells,
    buoyancy_table,
    lame_table,
    shear_table,
    partial,
    tail,
    exponents,
    scalar_sems,
    slab_sems,
    out_sems,
):
    planes, rows, lanes = velocity.shape[1:]
    tables = (buoyancy_table, lame_table, shear_table)
    inner = pl.ds(RIM, rows)
    slab = pl.ds(EDGE, planes)
    scalar_copies = fetch_all(
        (buoyancy_from, lame_from, shear_from, material_from, cells_from), (*tables, material, cells), scalar_sems
    )
    slab_copies = fetch_all(
        (stress, velocity, weights), (pulling.at[:, slab, inner], moving.at[:, slab, inner], slips), slab_sems
    )
    half = partial.shape[1]
    sum_copies = [
        pltpu.make_async_copy(partial, sums.at[:, pl.ds(0, half)], out_sems.at[2]),
        pltpu.make_async_copy(tail, sums.at[:, pl.ds(half, lanes)], out_sems.at[3]),
    ]
    exponent, steps = in_steps(kept[...] + received[...])
    partial[...] = steps.astype(jnp.int32).astype(jnp.int16)
    exponents[...] = jnp.broadcast_to(exponent, exponents.shape)
    sum_copies[0].start()
    odd = second_core()
    store, read, along_x, along_y, along_z, pull = stepping(moving, pulling, rows, lanes)

    blank = jnp.zeros((moving.shape[1], RIM, lanes), f32)
    for ref, fields_along_y in ((moving, (0, 1, 2)), (pulling, (SXY - 3, SYY - 3, SYZ - 3))):
        for field in fields_along_y:
            ref[field, :, 0:RIM] = blank
            ref[field, :, RIM + rows : 2 * RIM + rows] = blank

    for copy in scalar_copies:
        copy.wait()
    for plane in range(planes):
        buoyancy, lame, shear = looked_up(material[plane] + 1, tables)
        factors[0, EDGE + plane] = scale * buoyancy
        factors[1, EDGE + plane] = scale * lame
        factors[2, EDGE + plane] = scale * shear
        strain_factors[0, plane] = lame / (3.0 * lame + 2.0 * shear)
        strain_factors[1, plane] = 1.0 / (2.0 * shear)

    def unpack(halo, upper):
        entries = UPPER if upper else LOWER
        for index, (what, field, depth) in enumerate(entries):
            if what == FINE:
                continue
            place = EDGE + planes + depth - 1 if upper else EDGE - depth
            values = halo[index].astype(f32)
            if what == RAW and (FINE, field, depth) in entries:
                values = values + halo[entries.index((FINE, field, depth))].astype(f32)
            if field < 9:
                store(field, place, values)
            else:
                found = looked_up(values.astype(jnp.int32), tables)
                for kind in range(3):
                    factors[kind, place] = scale * found[kind]

    @pl.when(odd == 0)
    def _():
        unpack(across, False)
        unpack(within, True)

    @pl.when(odd != 0)
    def _():
        unpack(within, False)
        unpack(across, True)

    def move(place, do_x=True, do_yz=True):
        buoyancy = factors[0, place]
        chosen = ([VX] if do_x else []) + ([VY, VZ] if do_yz else [])
        results = [read(field, place) + buoyancy * pull(field, place) for field in chosen]
        for field, values in zip(chosen, results):
            store(field, place, values)

    def strain(place, do_yz=True, keep=None):
        lame, shear = factors[1, place], factors[2, place]
        twice = 2.0 * shear
        exx = joined(along_x(VX, place, False))
        eyy = joined(along_y(VY, place, False))
        ezz = joined(along_z(VZ, place, False))
        common = lame * (exx + eyy + ezz)
        changes = [(SXX, common + twice * exx)]
        changes.append((SXY, shear * joined(along_y(VX, place, True), along_x(VY, place, True))))
        changes.append((SXZ, shear * joined(along_z(VX, place, True), along_x(VZ, place, True))))
        if do_yz:
            changes.append((SYY, common + twice * eyy))
            changes.append((SZZ, common + twice * ezz))
            changes.append((SYZ, shear * joined(along_z(VY, place, True), along_y(VZ, place, True))))
        results = {field: read(field, place) + change for field, change in changes}
        for field, values in results.items():
            store(field, place, values)
        if keep is not None:
            compliance = strain_factors[1, place - EDGE]
            shift = strain_factors[0, place - EDGE] * (results[SXX] + results[SYY] + results[SZZ])
            first = pl.multiple_of((place - EDGE) * (8 * rows), 8 * rows)
            for field in range(3, 9):
                values = results[field] - shift if field < 6 else results[field]
                strains[keep, pl.ds(first + field - 3, rows, stride=8)] = values * compliance

    def over(first, last, body, width=2):
        def group(index, carry):
            for step in range(width):
                body(EDGE + first + index * width + step)
            return carry

        lax.fori_loop(0, (last - first) // width, group, 0)

    for copy in slab_copies[:2]:
        copy.wait()
    top = EDGE + planes
    move(EDGE - 2, do_yz=False)
    move(top + 1, do_x=False)
    over(-1, planes + 1, move)
    for place in range(EDGE - 3, EDGE):
        strain(place, do_yz=place == EDGE - 1)
    over(0, planes, functools.partial(strain, keep=0))
    for place in range(top, top + 3):
        strain(place, do_yz=place < top + 2)
    move(EDGE - 2, do_yz=False)
    move(top + 1, do_x=False)
    over(-1, planes + 1, move)
    out_copies = [
        pltpu.make_async_copy(moving.at[:, slab, inner], velocity_out, out_sems.at[0]),
        pltpu.make_async_copy(pulling.at[:, slab, inner], stress_out, out_sems.at[1]),
    ]
    out_copies[0].start()
    over(0, planes, functools.partial(strain, keep=1))
    out_copies[1].start()

    slab_copies[2].wait()
    points_each = cells.shape[1]
    lane_bits = lanes.bit_length() - 1
    tall = lax.broadcasted_iota(jnp.int32, (8, lanes), 1)

    def add_slot(slot, new):
        found = [jnp.zeros((8, lanes), f32) for _ in range(2)]
        for point in range(points_each):
            cell = cells[slot, point]
            first = pl.multiple_of((cell >> lane_bits) << 3, 8)
            shift = (point - cell) & (lanes - 1)
            hit = tall == point
            for which in range(2):
                turned = pltpu.roll(strains[which, pl.ds(first, 8)], shift, 1)
                found[which] = jnp.where(hit, turned, found[which])
        pair = [jnp.concatenate([values[part : part + 1] for part in range(6)], axis=1) for values in found]
        pair = jnp.concatenate(pair + [jnp.zeros((6, 6 * points_each), f32)], axis=0).astype(bf16)
        return new + lax.dot_general(pair, slips[slot], (((1,), (1,)), ((), ())), preferred_element_type=f32)

    new = lax.fori_loop(0, live[0], add_slot, jnp.zeros((8, slips.shape[1]), f32))
    new = jnp.concatenate([new, jnp.zeros((lanes - 8, slips.shape[1]), f32)], axis=0).T
    column = lax.broadcasted_iota(jnp.int32, new.shape, 1)
    exponent, steps = in_steps(new)
    steps = jnp.where(column == 2, exponent, jnp.where(column == 3, exponents[...], steps))
    tail[...] = steps.astype(jnp.int32).astype(jnp.int16)
    sum_copies[1].start()
    for copy in out_copies + sum_copies:
        copy.wait()


def sum_kernel(sums, out, values, news):
    share, samples = out.shape
    half = samples // 2
    steps = sums[:, half:].astype(jnp.int32).astype(f32)
    news[...] = steps * jnp.exp2(steps[:, 2:3])
    values[...] = sums[:, :half].astype(jnp.int32).astype(f32) * jnp.exp2(steps[:, 3:4])
    halves = [jnp.zeros((share, half), f32) for _ in range(2)]
    new = jnp.zeros((share, news.shape[1]), f32)
    for device in range(sums.shape[0] // share):
        at = slice(device * share, (device + 1) * share)
        halves[device % 2] = halves[device % 2] + values[at]
        new = new + news[at]
    out[...] = jnp.concatenate([jnp.concatenate(halves, axis=1)[:, 2:], new[:, 0:2]], axis=1)


def per_device(
    velocity,
    stress,
    material,
    buoyancy_table,
    lame_table,
    shear_table,
    fault_cells,
    block_count,
    strain_history,
    slip_weights,
):
    count = lax.axis_size("gx")
    planes, rows, lanes = material.shape
    slots, parts, points_each, samples = strain_history.shape
    ruptures = slip_weights.shape[1]
    share = ruptures // count
    whole = pl.BlockSpec(memory_space=pltpu.VMEM)
    scalars = pl.BlockSpec(memory_space=pltpu.SMEM)
    anywhere = pl.BlockSpec(memory_space=pl.ANY)
    params = pltpu.CompilerParams(vmem_limit_bytes=24 * 1024 * 1024)

    def stay(array):
        return pltpu.with_memory_space_constraint(array, pltpu.HBM)

    live = block_count
    velocity, stress, material, slip_weights, cells = [
        stay(array) for array in (velocity, stress, material, slip_weights, fault_cells)
    ]
    tables = [stay(table) for table in (buoyancy_table, lame_table, shear_table)]
    table_scratch = [pltpu.SMEM(table.shape, f32) for table in tables]
    history = stay(strain_history.reshape(slots, parts * points_each, samples))

    def cost(flops, size):
        return pl.CostEstimate(flops=flops, bytes_accessed=size, transcendentals=0)

    halo = pltpu.VMEM((HALO, rows, lanes), bf16)
    extent = planes + 2 * EDGE
    padded = [pltpu.VMEM((fields, extent, rows + 2 * RIM, lanes), f32) for fields in (3, 6)]
    across, within, slips = pl.pallas_call(
        pack_kernel,
        out_shape=(halo, halo, pltpu.VMEM(slip_weights.shape, bf16)),
        in_specs=[anywhere] * 5,
        out_specs=(whole,) * 3,
        scratch_shapes=[
            *padded,
            pltpu.VMEM(material.shape, jnp.int32),
            table_scratch[0],
            pltpu.SemaphoreType.DMA((4,)),
            pltpu.SemaphoreType.DMA,
        ],
        compiler_params=params,
        name="pack_halos",
    )(velocity, stress, material, tables[0], slip_weights)
    chips = [(i, i + 1) for i in range(1, count - 1, 2)]
    cores = [(i, i + 1) for i in range(0, count - 1, 2)]
    cores = cores + [(j, i) for i, j in cores]
    across = lax.ppermute(across, "gx", chips + [(j, i) for i, j in chips])
    within = lax.ppermute(within, "gx", cores)

    half = pltpu.VMEM((ruptures, samples // 2), f32)
    kept, sent = pl.pallas_call(
        history_kernel,
        out_shape=(half, half),
        in_specs=[scalars, whole, anywhere],
        out_specs=(whole, whole),
        scratch_shapes=[
            pltpu.VMEM(history.shape, bf16),
            pltpu.VMEM((ruptures, samples), f32),
            pltpu.SemaphoreType.DMA((slots,)),
        ],
        compiler_params=params,
        cost_estimate=cost(2 * slots * ruptures * parts * points_each * samples, 2 * history.size),
        name="history_product",
    )(live, slips, history)

    received = lax.ppermute(sent, "gx", cores)
    velocity_two, stress_two, sums = pl.pallas_call(
        steps_kernel,
        out_shape=(
            jax.ShapeDtypeStruct(velocity.shape, f32),
            jax.ShapeDtypeStruct(stress.shape, f32),
            jax.ShapeDtypeStruct((ruptures, samples // 2 + lanes), jnp.int16),
        ),
        in_specs=[scalars] + [anywhere] * 8 + [whole] * 4,
        out_specs=(anywhere,) * 3,
        scratch_shapes=[
            *padded,
            pltpu.VMEM((3, extent, rows, lanes), f32),
            pltpu.VMEM((2, planes, rows, lanes), f32),
            pltpu.VMEM((2, planes * rows * 8, lanes), f32),
            pltpu.VMEM(material.shape, jnp.int32),
            pltpu.VMEM(slip_weights.shape, bf16),
            pltpu.SMEM(cells.shape, jnp.int32),
            *table_scratch,
            pltpu.VMEM((ruptures, samples // 2), jnp.int16),
            pltpu.VMEM((ruptures, lanes), jnp.int16),
            pltpu.VMEM((ruptures, lanes), f32),
            pltpu.SemaphoreType.DMA((5,)),
            pltpu.SemaphoreType.DMA((3,)),
            pltpu.SemaphoreType.DMA((4,)),
        ],
        compiler_params=params,
        cost_estimate=cost(10**10, 30 * 1024 * 1024),
        name="two_steps",
    )(live, cells, *tables, material, velocity, stress, slip_weights, across, within, kept, received)
    sums = lax.all_to_all(sums, "gx", 0, 0, tiled=True)
    seismograms = pl.pallas_call(
        sum_kernel,
        out_shape=jax.ShapeDtypeStruct((share, samples), f32),
        in_specs=[whole],
        out_specs=whole,
        scratch_shapes=[pltpu.VMEM((ruptures, samples // 2), f32), pltpu.VMEM((ruptures, lanes), f32)],
        compiler_params=params,
        name="sum_partials",
    )(sums)
    return (velocity_two, stress_two, seismograms)


def solution(mesh):
    in_specs = (
        P(None, ("site", "gx"), None, None),
        P(None, ("site", "gx"), None, None),
        P("gx", None, None),
        P(),
        P(),
        P(),
        P("gx", None),
        P("gx"),
        P(("site", "gx"), None, None, None),
        P("gx", None, None),
    )
    out_specs = (
        P(None, ("site", "gx"), None, None),
        P(None, ("site", "gx"), None, None),
        P(("site", "gx"), None),
    )
    return jax.shard_map(
        per_device, mesh=mesh, in_specs=in_specs, out_specs=out_specs, check_vma=False
    )
```

```python
import functools

import jax
import jax.numpy as jnp
from jax import lax
from jax.experimental import pallas as pl
from jax.experimental.pallas import tpu as pltpu
from jax.sharding import PartitionSpec as P

time_step = 0.4
scale = time_step / 24.0

VX, VY, VZ, SXX, SYY, SZZ, SXY, SXZ, SYZ, MAT = range(10)
LOWER_RAW = (2, 1, 1, 3, 1, 1, 3, 3, 1, 3)
UPPER_RAW = (1, 2, 2, 3, 2, 2, 3, 3, 2, 3)
LOWER_MOVED = ((3, 5), (2, 4), (2, 4))
UPPER_MOVED = ((2, 4), (3, 5), (3, 5))
LOWER_FINE = (VX, VY, VZ, SXX, SXY, SXZ, SYZ)
UPPER_FINE = (VY, VZ, SXX)
RAW, MOVED, FINE = range(3)
EDGE = 5
RIM = 8


def halo_list(raw, moved, fine):
    entries = [(RAW, field, depth) for field in range(10) for depth in range(1, raw[field] + 1)]
    for field, (first, last) in enumerate(moved):
        entries += [(MOVED, field, depth) for depth in range(first, last + 1)]
    return entries + [(FINE, field, 1) for field in fine]


LOWER = halo_list(LOWER_RAW, LOWER_MOVED, LOWER_FINE)
UPPER = halo_list(UPPER_RAW, UPPER_MOVED, UPPER_FINE)
HALO = max(len(LOWER), len(UPPER))

f32 = jnp.float32
bf16 = jnp.bfloat16


def second_core():
    return lax.axis_index("gx") % 2


def fetch_all(sources, targets, sems):
    copies = [
        pltpu.make_async_copy(source, target, sems.at[index])
        for index, (source, target) in enumerate(zip(sources, targets))
    ]
    for copy in copies:
        copy.start()
    return copies


def looked_up(code, tables):
    results = [jnp.zeros(code.shape, f32) for _ in tables]
    for entry in range(len(tables[0])):
        hit = code == entry + 1
        results = [jnp.where(hit, table[entry], result) for table, result in zip(tables, results)]
    return results


def parts_of(behind, here_low, here_high, ahead):
    return here_high - here_low, ahead - behind


def joined(*parts):
    near, far = parts[0]
    for more_near, more_far in parts[1:]:
        near, far = near + more_near, far + more_far
    return 27.0 * near - far


def shifted(values, place, axis, by):
    size = values.shape[axis]
    inside = place < size - by if by > 0 else place >= -by
    return jnp.where(inside, pltpu.roll(values, -by % size, axis), 0.0)


def along(values, place, axis, forward):
    offsets = (-1, 0, 1, 2) if forward else (-2, -1, 0, 1)
    return parts_of(*[values if by == 0 else shifted(values, place, axis, by) for by in offsets])


def stepping(moving, pulling, rows, lanes):
    inner = pl.ds(RIM, rows)
    lane = lax.broadcasted_iota(jnp.int32, (rows, lanes), 1)

    def store(field, place, values):
        if field < 3:
            moving[field, place, inner] = values
        else:
            pulling[field - 3, place, inner] = values

    def read(field, place, at=inner):
        return moving[field, place, at] if field < 3 else pulling[field - 3, place, at]

    def along_x(field, place, forward):
        start = place - 1 if forward else place - 2
        return parts_of(*[read(field, start + step) for step in range(4)])

    def along_y(field, place, forward):
        start = RIM - 1 if forward else RIM - 2
        return parts_of(*[read(field, place, pl.ds(start + step, rows)) for step in range(4)])

    def along_z(field, place, forward):
        return along(read(field, place), lane, 1, forward)

    def pull(field, place):
        if field == VX:
            return joined(along_x(SXX, place, True), along_y(SXY, place, False), along_z(SXZ, place, False))
        if field == VY:
            return joined(along_x(SXY, place, False), along_y(SYY, place, True), along_z(SYZ, place, False))
        return joined(along_x(SXZ, place, False), along_y(SYZ, place, False), along_z(SZZ, place, True))

    return store, read, along_x, along_y, along_z, pull


def pack_kernel(
    velocity_from,
    stress_from,
    material_from,
    buoyancy_from,
    across,
    within,
    moving,
    pulling,
    material,
    buoyancy,
    sems,
):
    planes, rows, lanes = material.shape
    slab, inner = pl.ds(EDGE, planes), pl.ds(RIM, rows)
    copies = fetch_all(
        (stress_from, velocity_from, material_from, buoyancy_from),
        (pulling.at[:, slab, inner], moving.at[:, slab, inner], material, buoyancy),
        sems,
    )
    blank = jnp.zeros((moving.shape[1], RIM, lanes), f32)
    for ref, fields_along_y in ((moving, (0, 1, 2)), (pulling, (SXY - 3, SYY - 3, SYZ - 3))):
        for field in fields_along_y:
            ref[field, :, 0:RIM] = blank
            ref[field, :, RIM + rows : 2 * RIM + rows] = blank
    store, read, along_x, along_y, along_z, pull = stepping(moving, pulling, rows, lanes)
    odd = second_core()
    for copy in copies:
        copy.wait()

    def moved(field, plane):
        entries = [buoyancy[entry] for entry in range(buoyancy.shape[0])]
        factor = scale * looked_up(material[plane] + 1, (entries,))[0]
        return read(field, EDGE + plane) + factor * pull(field, EDGE + plane)

    def fill(out, entries, plane_of):
        for index, (what, field, depth) in enumerate(entries):
            plane = plane_of(depth)
            if what == MOVED:
                values = moved(field, plane)
            elif field < 9:
                values = read(field, EDGE + plane)
            else:
                values = (material[plane] + 1).astype(f32)
            if what == FINE:
                values = values - values.astype(bf16).astype(f32)
            out[index] = values.astype(bf16)
        for spare in range(len(entries), out.shape[0]):
            out[spare] = jnp.zeros(out.shape[1:], bf16)

    def upper_face(out):
        fill(out, LOWER, lambda depth: planes - depth)

    def lower_face(out):
        fill(out, UPPER, lambda depth: depth - 1)

    @pl.when(odd == 0)
    def _():
        lower_face(across)
        upper_face(within)

    @pl.when(odd != 0)
    def _():
        upper_face(across)
        lower_face(within)


def in_steps(values):
    largest = jnp.max(jnp.abs(values), axis=1, keepdims=True)
    exponent = jnp.ceil(jnp.log2(jnp.maximum(largest, 1e-30))) - 14.0
    return exponent, jnp.clip(jnp.round(values * jnp.exp2(-exponent)), -32767.0, 32767.0)


def history_kernel(live, weights, history, after, kept, sent, slips, records, total, slip_sems, record_sems):
    del after
    slots = weights.shape[0]
    copies = [
        (
            pltpu.make_async_copy(weights.at[slot], slips.at[slot], slip_sems.at[slot]),
            pltpu.make_async_copy(history.at[slot], records.at[slot], record_sems.at[slot]),
        )
        for slot in range(slots)
    ]
    for copy in copies[0]:
        copy.start()
    for slot in range(1, slots):

        @pl.when(slot < live[0])
        def _(slot=slot):
            for copy in copies[slot]:
                copy.start()

    for copy in copies[0]:
        copy.wait()
    total[...] = jnp.dot(slips[0], records[0], preferred_element_type=f32)
    for slot in range(1, slots):

        @pl.when(slot < live[0])
        def _(slot=slot):
            for copy in copies[slot]:
                copy.wait()
            total[...] += jnp.dot(slips[slot], records[slot], preferred_element_type=f32)

    half = kept.shape[1]
    first = second_core() == 0
    early, late = total[:, :half], total[:, half:]
    early = jnp.where(lax.broadcasted_iota(jnp.int32, early.shape, 1) < 2, 0.0, early)
    kept[...] = jnp.where(first, early, late)
    sent[...] = jnp.where(first, late, early)


def ready_kernel(
    kept,
    received,
    velocity_from,
    stress_from,
    material_from,
    buoyancy_from,
    lame_from,
    shear_from,
    partial,
    exponents,
    velocity,
    stress,
    material,
    entries,
    buoyancy,
    lame,
    shear,
    sems,
):
    copies = fetch_all(
        (buoyancy_from, lame_from, shear_from, stress_from, velocity_from, material_from),
        (buoyancy, lame, shear, stress, velocity, material),
        sems,
    )
    exponent, steps = in_steps(kept[...] + received[...])
    partial[...] = steps.astype(jnp.int32).astype(jnp.int16)
    exponents[...] = jnp.broadcast_to(exponent, exponents.shape)
    for copy in copies[:3]:
        copy.wait()
    for kind, table in enumerate((buoyancy, lame, shear)):
        for entry in range(table.shape[0]):
            at = kind * table.shape[0] + entry
            entries[at : at + 1] = jnp.full((1, entries.shape[1]), table[entry], f32)
    for copy in copies[3:]:
        copy.wait()


def steps_kernel(
    live,
    cells_from,
    weights,
    velocity,
    stress,
    material,
    entries,
    across,
    within,
    partial,
    exponents,
    velocity_out,
    stress_out,
    sums,
    moving,
    pulling,
    factors,
    strain_factors,
    strains,
    early,
    slips,
    cells,
    tail,
    cell_sem,
    slip_sem,
    out_sems,
):
    planes, rows, lanes = material.shape
    materials = entries.shape[0] // 3
    tables = [
        [entries[at : at + 1] for at in range(kind * materials, (kind + 1) * materials)] for kind in range(3)
    ]
    inner = pl.ds(RIM, rows)
    slab = pl.ds(EDGE, planes)
    cell_copy = pltpu.make_async_copy(cells_from, cells, cell_sem)
    cell_copy.start()
    slip_copy = pltpu.make_async_copy(weights, slips, slip_sem)
    slip_copy.start()
    half = partial.shape[1]
    sum_copies = [
        pltpu.make_async_copy(partial, sums.at[:, pl.ds(0, half)], out_sems.at[2]),
        pltpu.make_async_copy(tail, sums.at[:, pl.ds(half, lanes)], out_sems.at[3]),
    ]
    sum_copies[0].start()
    odd = second_core()
    store, read, along_x, along_y, along_z, pull = stepping(moving, pulling, rows, lanes)

    blank = jnp.zeros((moving.shape[1], RIM, lanes), f32)
    for ref, fields_along_y in ((moving, (0, 1, 2)), (pulling, (SXY - 3, SYY - 3, SYZ - 3))):
        for field in fields_along_y:
            ref[field, :, 0:RIM] = blank
            ref[field, :, RIM + rows : 2 * RIM + rows] = blank
    moving[:, slab, inner] = velocity[...]
    pulling[:, slab, inner] = stress[...]

    for plane in range(planes):
        buoyancy, lame, shear = looked_up(material[plane] + 1, tables)
        factors[0, EDGE + plane] = scale * buoyancy
        factors[1, EDGE + plane] = scale * lame
        factors[2, EDGE + plane] = scale * shear
        strain_factors[0, plane] = lame / (3.0 * lame + 2.0 * shear)
        strain_factors[1, plane] = 1.0 / (2.0 * shear)

    def unpack(halo, upper):
        entries = UPPER if upper else LOWER
        for index, (what, field, depth) in enumerate(entries):
            if what == FINE:
                continue
            place = EDGE + planes + depth - 1 if upper else EDGE - depth
            values = halo[index].astype(f32)
            if what == RAW and (FINE, field, depth) in entries:
                values = values + halo[entries.index((FINE, field, depth))].astype(f32)
            if field < 9:
                store(field, place, values)
            else:
                found = looked_up(values.astype(jnp.int32), tables)
                for kind in range(3):
                    factors[kind, place] = scale * found[kind]

    @pl.when(odd == 0)
    def _():
        unpack(across, False)
        unpack(within, True)

    @pl.when(odd != 0)
    def _():
        unpack(within, False)
        unpack(across, True)

    def move(place, do_x=True, do_yz=True):
        buoyancy = factors[0, place]
        chosen = ([VX] if do_x else []) + ([VY, VZ] if do_yz else [])
        results = [read(field, place) + buoyancy * pull(field, place) for field in chosen]
        for field, values in zip(chosen, results):
            store(field, place, values)

    def strain(place, do_yz=True, keep=None):
        lame, shear = factors[1, place], factors[2, place]
        twice = 2.0 * shear
        exx = joined(along_x(VX, place, False))
        eyy = joined(along_y(VY, place, False))
        ezz = joined(along_z(VZ, place, False))
        common = lame * (exx + eyy + ezz)
        changes = [(SXX, common + twice * exx)]
        changes.append((SXY, shear * joined(along_y(VX, place, True), along_x(VY, place, True))))
        changes.append((SXZ, shear * joined(along_z(VX, place, True), along_x(VZ, place, True))))
        if do_yz:
            changes.append((SYY, common + twice * eyy))
            changes.append((SZZ, common + twice * ezz))
            changes.append((SYZ, shear * joined(along_z(VY, place, True), along_y(VZ, place, True))))
        results = {field: read(field, place) + change for field, change in changes}
        for field, values in results.items():
            store(field, place, values)
        if keep is not None:
            compliance = strain_factors[1, place - EDGE]
            shift = strain_factors[0, place - EDGE] * (results[SXX] + results[SYY] + results[SZZ])
            first = pl.multiple_of((place - EDGE) * (8 * rows), 8 * rows)
            for field in range(3, 9):
                values = results[field] - shift if field < 6 else results[field]
                strains[keep, pl.ds(first + field - 3, rows, stride=8)] = values * compliance

    def over(first, last, body, width=2):
        def group(index, carry):
            for step in range(width):
                body(EDGE + first + index * width + step)
            return carry

        lax.fori_loop(0, (last - first) // width, group, 0)

    top = EDGE + planes
    move(EDGE - 2, do_yz=False)
    move(top + 1, do_x=False)
    over(-1, planes + 1, move)
    for place in range(EDGE - 3, EDGE):
        strain(place, do_yz=place == EDGE - 1)
    over(0, planes, functools.partial(strain, keep=0))
    for place in range(top, top + 3):
        strain(place, do_yz=place < top + 2)
    slots, points_each = cells.shape
    lane_bits = lanes.bit_length() - 1
    tall = lax.broadcasted_iota(jnp.int32, (8, lanes), 1)

    def sampled(which, slot):
        found = jnp.zeros((8, lanes), f32)
        for point in range(points_each):
            cell = cells[slot, point]
            first = pl.multiple_of((cell >> lane_bits) << 3, 8)
            turned = pltpu.roll(strains[which, pl.ds(first, 8)], (point - cell) & (lanes - 1), 1)
            found = jnp.where(tall == point, turned, found)
        return found

    def move_and_sample(index, carry):
        for step in range(2):
            move(EDGE - 1 + 2 * index + step)
        early[index] = sampled(0, index)
        return carry

    cell_copy.wait()
    move(EDGE - 2, do_yz=False)
    move(top + 1, do_x=False)
    together = min(slots, (planes + 2) // 2)
    lax.fori_loop(0, together, move_and_sample, 0)
    over(2 * together - 1, planes + 1, move)
    for slot in range(together, slots):
        early[slot] = sampled(0, slot)
    out_copies = [
        pltpu.make_async_copy(moving.at[:, slab, inner], velocity_out, out_sems.at[0]),
        pltpu.make_async_copy(pulling.at[:, slab, inner], stress_out, out_sems.at[1]),
    ]
    out_copies[0].start()
    over(0, planes, functools.partial(strain, keep=1))
    out_copies[1].start()

    slip_copy.wait()

    def add_slot(slot, new):
        pair = [
            jnp.concatenate([values[part : part + 1] for part in range(6)], axis=1)
            for values in (early[slot], sampled(1, slot))
        ]
        pair = jnp.concatenate(pair + [jnp.zeros((6, 6 * points_each), f32)], axis=0).astype(bf16)
        return new + lax.dot_general(pair, slips[slot], (((1,), (1,)), ((), ())), preferred_element_type=f32)

    new = lax.fori_loop(0, live[0], add_slot, jnp.zeros((8, slips.shape[1]), f32))
    new = jnp.concatenate([new, jnp.zeros((lanes - 8, slips.shape[1]), f32)], axis=0).T
    column = lax.broadcasted_iota(jnp.int32, new.shape, 1)
    exponent, steps = in_steps(new)
    steps = jnp.where(column == 2, exponent, jnp.where(column == 3, exponents[...], steps))
    tail[...] = steps.astype(jnp.int32).astype(jnp.int16)
    sum_copies[1].start()
    for copy in out_copies + sum_copies:
        copy.wait()


def sum_kernel(sums, out, values, news):
    share, samples = out.shape
    half = samples // 2
    steps = sums[:, half:].astype(jnp.int32).astype(f32)
    news[...] = steps * jnp.exp2(steps[:, 2:3])
    values[...] = sums[:, :half].astype(jnp.int32).astype(f32) * jnp.exp2(steps[:, 3:4])
    halves = [jnp.zeros((share, half), f32) for _ in range(2)]
    new = jnp.zeros((share, news.shape[1]), f32)
    for device in range(sums.shape[0] // share):
        at = slice(device * share, (device + 1) * share)
        halves[device % 2] = halves[device % 2] + values[at]
        new = new + news[at]
    out[...] = jnp.concatenate([jnp.concatenate(halves, axis=1)[:, 2:], new[:, 0:2]], axis=1)


def per_device(
    velocity,
    stress,
    material,
    buoyancy_table,
    lame_table,
    shear_table,
    fault_cells,
    block_count,
    strain_history,
    slip_weights,
):
    count = lax.axis_size("gx")
    planes, rows, lanes = material.shape
    slots, parts, points_each, samples = strain_history.shape
    ruptures = slip_weights.shape[1]
    share = ruptures // count
    whole = pl.BlockSpec(memory_space=pltpu.VMEM)
    scalars = pl.BlockSpec(memory_space=pltpu.SMEM)
    anywhere = pl.BlockSpec(memory_space=pl.ANY)
    params = pltpu.CompilerParams(vmem_limit_bytes=24 * 1024 * 1024)

    def stay(array):
        return pltpu.with_memory_space_constraint(array, pltpu.HBM)

    live = block_count
    velocity, stress, material, slip_weights, cells = [
        stay(array) for array in (velocity, stress, material, slip_weights, fault_cells)
    ]
    tables = [stay(table) for table in (buoyancy_table, lame_table, shear_table)]
    table_scratch = [pltpu.SMEM(table.shape, f32) for table in tables]
    history = stay(strain_history.reshape(slots, parts * points_each, samples))

    def cost(flops, size):
        return pl.CostEstimate(flops=flops, bytes_accessed=size, transcendentals=0)

    halo = pltpu.VMEM((HALO, rows, lanes), bf16)
    extent = planes + 2 * EDGE
    padded = [pltpu.VMEM((fields, extent, rows + 2 * RIM, lanes), f32) for fields in (3, 6)]
    across, within = pl.pallas_call(
        pack_kernel,
        out_shape=(halo, halo),
        in_specs=[anywhere] * 4,
        out_specs=(whole, whole),
        scratch_shapes=[
            *padded,
            pltpu.VMEM(material.shape, jnp.int32),
            table_scratch[0],
            pltpu.SemaphoreType.DMA((4,)),
        ],
        compiler_params=params,
        name="pack_halos",
    )(velocity, stress, material, tables[0])
    chips = [(i, i + 1) for i in range(1, count - 1, 2)]
    cores = [(i, i + 1) for i in range(0, count - 1, 2)]
    cores = cores + [(j, i) for i, j in cores]
    packed = within
    across = lax.ppermute(across, "gx", chips + [(j, i) for i, j in chips])
    within = lax.ppermute(within, "gx", cores)

    half = pltpu.VMEM((ruptures, samples // 2), f32)
    kept, sent = pl.pallas_call(
        history_kernel,
        out_shape=(half, half),
        in_specs=[scalars] + [anywhere] * 3,
        out_specs=(whole, whole),
        scratch_shapes=[
            pltpu.VMEM(slip_weights.shape, bf16),
            pltpu.VMEM(history.shape, bf16),
            pltpu.VMEM((ruptures, samples), f32),
            pltpu.SemaphoreType.DMA((slots,)),
            pltpu.SemaphoreType.DMA((slots,)),
        ],
        compiler_params=params,
        cost_estimate=cost(10**10, 2 * (history.size + slip_weights.size)),
        name="history_product",
    )(live, slip_weights, history, packed)

    received = lax.ppermute(sent, "gx", cores)
    slab = [pltpu.VMEM(array.shape, array.dtype) for array in (velocity, stress, material)]
    partial, exponents, *slab, entries = pl.pallas_call(
        ready_kernel,
        out_shape=(
            pltpu.VMEM((ruptures, samples // 2), jnp.int16),
            pltpu.VMEM((ruptures, lanes), f32),
            *slab,
            pltpu.VMEM((3 * buoyancy_table.shape[0], lanes), f32),
        ),
        in_specs=[whole] * 2 + [anywhere] * 6,
        out_specs=(whole,) * 6,
        scratch_shapes=table_scratch + [pltpu.SemaphoreType.DMA((6,))],
        compiler_params=params,
        cost_estimate=cost(10**6, 1024 * 1024),
        name="ready_slab",
    )(kept, received, velocity, stress, material, *tables)
    velocity_two, stress_two, sums = pl.pallas_call(
        steps_kernel,
        out_shape=(
            jax.ShapeDtypeStruct(velocity.shape, f32),
            jax.ShapeDtypeStruct(stress.shape, f32),
            jax.ShapeDtypeStruct((ruptures, samples // 2 + lanes), jnp.int16),
        ),
        in_specs=[scalars] + [anywhere] * 2 + [whole] * 8,
        out_specs=(anywhere,) * 3,
        scratch_shapes=[
            *padded,
            pltpu.VMEM((3, extent, rows, lanes), f32),
            pltpu.VMEM((2, planes, rows, lanes), f32),
            pltpu.VMEM((2, planes * rows * 8, lanes), f32),
            pltpu.VMEM((slots, 8, lanes), f32),
            pltpu.VMEM(slip_weights.shape, bf16),
            pltpu.SMEM(cells.shape, jnp.int32),
            pltpu.VMEM((ruptures, lanes), jnp.int16),
            pltpu.SemaphoreType.DMA,
            pltpu.SemaphoreType.DMA,
            pltpu.SemaphoreType.DMA((4,)),
        ],
        compiler_params=params,
        cost_estimate=cost(10**10, 30 * 1024 * 1024),
        name="two_steps",
    )(live, cells, slip_weights, *slab, entries, across, within, partial, exponents)
    sums = lax.all_to_all(sums, "gx", 0, 0, tiled=True)
    seismograms = pl.pallas_call(
        sum_kernel,
        out_shape=jax.ShapeDtypeStruct((share, samples), f32),
        in_specs=[whole],
        out_specs=whole,
        scratch_shapes=[pltpu.VMEM((ruptures, samples // 2), f32), pltpu.VMEM((ruptures, lanes), f32)],
        compiler_params=params,
        name="sum_partials",
    )(sums)
    return (velocity_two, stress_two, seismograms)


def solution(mesh):
    in_specs = (
        P(None, ("site", "gx"), None, None),
        P(None, ("site", "gx"), None, None),
        P("gx", None, None),
        P(),
        P(),
        P(),
        P("gx", None),
        P("gx"),
        P(("site", "gx"), None, None, None),
        P("gx", None, None),
    )
    out_specs = (
        P(None, ("site", "gx"), None, None),
        P(None, ("site", "gx"), None, None),
        P(("site", "gx"), None),
    )
    return jax.shard_map(
        per_device, mesh=mesh, in_specs=in_specs, out_specs=out_specs, check_vma=False
    )
```

```python
import functools

import jax
import jax.numpy as jnp
from jax import lax
from jax.experimental import pallas as pl
from jax.experimental.pallas import tpu as pltpu
from jax.sharding import PartitionSpec as P

time_step = 0.4
scale = time_step / 24.0

VX, VY, VZ, SXX, SYY, SZZ, SXY, SXZ, SYZ, MAT = range(10)
LOWER_RAW = (2, 1, 1, 3, 1, 1, 3, 3, 1, 3)
UPPER_RAW = (1, 2, 2, 3, 2, 2, 3, 3, 2, 3)
LOWER_MOVED = ((3, 5), (2, 4), (2, 4))
UPPER_MOVED = ((2, 4), (3, 5), (3, 5))
LOWER_FINE = (VX, VY, VZ, SXX, SXY, SXZ, SYZ)
UPPER_FINE = (VY, VZ, SXX)
RAW, MOVED, FINE = range(3)
EDGE = 5
RIM = 8


def halo_list(raw, moved, fine):
    entries = [(RAW, field, depth) for field in range(10) for depth in range(1, raw[field] + 1)]
    for field, (first, last) in enumerate(moved):
        entries += [(MOVED, field, depth) for depth in range(first, last + 1)]
    return entries + [(FINE, field, 1) for field in fine]


LOWER = halo_list(LOWER_RAW, LOWER_MOVED, LOWER_FINE)
UPPER = halo_list(UPPER_RAW, UPPER_MOVED, UPPER_FINE)
HALO = max(len(LOWER), len(UPPER))

f32 = jnp.float32
bf16 = jnp.bfloat16


def second_core():
    return lax.axis_index("gx") % 2


def fetch_all(sources, targets, sems):
    copies = [
        pltpu.make_async_copy(source, target, sems.at[index])
        for index, (source, target) in enumerate(zip(sources, targets))
    ]
    for copy in copies:
        copy.start()
    return copies


def looked_up(code, tables):
    results = [jnp.zeros(code.shape, f32) for _ in tables]
    for entry in range(len(tables[0])):
        hit = code == entry + 1
        results = [jnp.where(hit, table[entry], result) for table, result in zip(tables, results)]
    return results


def parts_of(behind, here_low, here_high, ahead):
    return here_high - here_low, ahead - behind


def joined(*parts):
    near, far = parts[0]
    for more_near, more_far in parts[1:]:
        near, far = near + more_near, far + more_far
    return 27.0 * near - far


def shifted(values, place, axis, by):
    size = values.shape[axis]
    inside = place < size - by if by > 0 else place >= -by
    return jnp.where(inside, pltpu.roll(values, -by % size, axis), 0.0)


def along(values, place, axis, forward):
    offsets = (-1, 0, 1, 2) if forward else (-2, -1, 0, 1)
    return parts_of(*[values if by == 0 else shifted(values, place, axis, by) for by in offsets])


def stepping(moving, pulling, rows, lanes):
    inner = pl.ds(RIM, rows)
    lane = lax.broadcasted_iota(jnp.int32, (rows, lanes), 1)

    def store(field, place, values):
        if field < 3:
            moving[field, place, inner] = values
        else:
            pulling[field - 3, place, inner] = values

    def read(field, place, at=inner):
        return moving[field, place, at] if field < 3 else pulling[field - 3, place, at]

    def along_x(field, place, forward):
        start = place - 1 if forward else place - 2
        return parts_of(*[read(field, start + step) for step in range(4)])

    def along_y(field, place, forward):
        start = RIM - 1 if forward else RIM - 2
        return parts_of(*[read(field, place, pl.ds(start + step, rows)) for step in range(4)])

    def along_z(field, place, forward):
        return along(read(field, place), lane, 1, forward)

    def pull(field, place):
        if field == VX:
            return joined(along_x(SXX, place, True), along_y(SXY, place, False), along_z(SXZ, place, False))
        if field == VY:
            return joined(along_x(SXY, place, False), along_y(SYY, place, True), along_z(SYZ, place, False))
        return joined(along_x(SXZ, place, False), along_y(SYZ, place, False), along_z(SZZ, place, True))

    return store, read, along_x, along_y, along_z, pull


def pack_kernel(
    velocity_from,
    stress_from,
    material_from,
    buoyancy_from,
    across,
    within,
    moving,
    pulling,
    material,
    buoyancy,
    sems,
):
    planes, rows, lanes = material.shape
    slab, inner = pl.ds(EDGE, planes), pl.ds(RIM, rows)
    copies = fetch_all(
        (stress_from, velocity_from, material_from, buoyancy_from),
        (pulling.at[:, slab, inner], moving.at[:, slab, inner], material, buoyancy),
        sems,
    )
    blank = jnp.zeros((moving.shape[1], RIM, lanes), f32)
    for ref, fields_along_y in ((moving, (0, 1, 2)), (pulling, (SXY - 3, SYY - 3, SYZ - 3))):
        for field in fields_along_y:
            ref[field, :, 0:RIM] = blank
            ref[field, :, RIM + rows : 2 * RIM + rows] = blank
    store, read, along_x, along_y, along_z, pull = stepping(moving, pulling, rows, lanes)
    odd = second_core()
    for copy in copies:
        copy.wait()

    def moved(field, plane):
        entries = [buoyancy[entry] for entry in range(buoyancy.shape[0])]
        factor = scale * looked_up(material[plane] + 1, (entries,))[0]
        return read(field, EDGE + plane) + factor * pull(field, EDGE + plane)

    def fill(out, entries, plane_of):
        for index, (what, field, depth) in enumerate(entries):
            plane = plane_of(depth)
            if what == MOVED:
                values = moved(field, plane)
            elif field < 9:
                values = read(field, EDGE + plane)
            else:
                values = (material[plane] + 1).astype(f32)
            if what == FINE:
                values = values - values.astype(bf16).astype(f32)
            out[index] = values.astype(bf16)
        for spare in range(len(entries), out.shape[0]):
            out[spare] = jnp.zeros(out.shape[1:], bf16)

    def upper_face(out):
        fill(out, LOWER, lambda depth: planes - depth)

    def lower_face(out):
        fill(out, UPPER, lambda depth: depth - 1)

    @pl.when(odd == 0)
    def _():
        lower_face(across)
        upper_face(within)

    @pl.when(odd != 0)
    def _():
        upper_face(across)
        lower_face(within)


def in_steps(values):
    largest = jnp.max(jnp.abs(values), axis=1, keepdims=True)
    exponent = jnp.ceil(jnp.log2(jnp.maximum(largest, 1e-30))) - 14.0
    return exponent, jnp.clip(jnp.round(values * jnp.exp2(-exponent)), -32767.0, 32767.0)


def history_kernel(live, weights, history, after, kept, sent, slips, records, total, slip_sems, record_sems):
    del after
    slots = weights.shape[0]
    copies = [
        (
            pltpu.make_async_copy(weights.at[slot], slips.at[slot], slip_sems.at[slot]),
            pltpu.make_async_copy(history.at[slot], records.at[slot], record_sems.at[slot]),
        )
        for slot in range(slots)
    ]
    for copy in copies[0]:
        copy.start()
    for slot in range(1, slots):

        @pl.when(slot < live[0])
        def _(slot=slot):
            for copy in copies[slot]:
                copy.start()

    for copy in copies[0]:
        copy.wait()
    total[...] = jnp.dot(slips[0], records[0], preferred_element_type=f32)
    for slot in range(1, slots):

        @pl.when(slot < live[0])
        def _(slot=slot):
            for copy in copies[slot]:
                copy.wait()
            total[...] += jnp.dot(slips[slot], records[slot], preferred_element_type=f32)

    half = kept.shape[1]
    first = second_core() == 0
    early, late = total[:, :half], total[:, half:]
    early = jnp.where(lax.broadcasted_iota(jnp.int32, early.shape, 1) < 2, 0.0, early)
    kept[...] = jnp.where(first, early, late)
    sent[...] = jnp.where(first, late, early)


def ready_kernel(
    kept,
    received,
    velocity_from,
    stress_from,
    material_from,
    buoyancy_from,
    lame_from,
    shear_from,
    partial,
    exponents,
    velocity,
    stress,
    material,
    entries,
    buoyancy,
    lame,
    shear,
    sems,
):
    copies = fetch_all(
        (buoyancy_from, lame_from, shear_from, stress_from, velocity_from, material_from),
        (buoyancy, lame, shear, stress, velocity, material),
        sems,
    )
    exponent, steps = in_steps(kept[...] + received[...])
    partial[...] = steps.astype(jnp.int32).astype(jnp.int16)
    exponents[...] = jnp.broadcast_to(exponent, exponents.shape)
    for copy in copies[:3]:
        copy.wait()
    for kind, table in enumerate((buoyancy, lame, shear)):
        for entry in range(table.shape[0]):
            at = kind * table.shape[0] + entry
            entries[at : at + 1] = jnp.full((1, entries.shape[1]), table[entry], f32)
    for copy in copies[3:]:
        copy.wait()


def steps_kernel(
    live,
    cells_from,
    weights,
    velocity,
    stress,
    material,
    entries,
    across,
    within,
    partial,
    exponents,
    velocity_out,
    stress_out,
    sums,
    moving,
    pulling,
    factors,
    strain_factors,
    strains,
    pairs,
    slips,
    cells,
    tail,
    cell_sem,
    slip_sem,
    out_sems,
):
    planes, rows, lanes = material.shape
    materials = entries.shape[0] // 3
    tables = [
        [entries[at : at + 1] for at in range(kind * materials, (kind + 1) * materials)] for kind in range(3)
    ]
    inner = pl.ds(RIM, rows)
    slab = pl.ds(EDGE, planes)
    cell_copy = pltpu.make_async_copy(cells_from, cells, cell_sem)
    cell_copy.start()
    slip_copy = pltpu.make_async_copy(weights, slips, slip_sem)
    slip_copy.start()
    half = partial.shape[1]
    sum_copies = [
        pltpu.make_async_copy(partial, sums.at[:, pl.ds(0, half)], out_sems.at[2]),
        pltpu.make_async_copy(tail, sums.at[:, pl.ds(half, lanes)], out_sems.at[3]),
    ]
    sum_copies[0].start()
    odd = second_core()
    store, read, along_x, along_y, along_z, pull = stepping(moving, pulling, rows, lanes)

    blank = jnp.zeros((moving.shape[1], RIM, lanes), f32)
    for ref, fields_along_y in ((moving, (0, 1, 2)), (pulling, (SXY - 3, SYY - 3, SYZ - 3))):
        for field in fields_along_y:
            ref[field, :, 0:RIM] = blank
            ref[field, :, RIM + rows : 2 * RIM + rows] = blank
    moving[:, slab, inner] = velocity[...]
    pulling[:, slab, inner] = stress[...]

    for plane in range(planes):
        buoyancy, lame, shear = looked_up(material[plane] + 1, tables)
        factors[0, EDGE + plane] = scale * buoyancy
        factors[1, EDGE + plane] = scale * lame
        factors[2, EDGE + plane] = scale * shear
        strain_factors[0, plane] = lame / (3.0 * lame + 2.0 * shear)
        strain_factors[1, plane] = 1.0 / (2.0 * shear)

    def unpack(halo, upper):
        entries = UPPER if upper else LOWER
        for index, (what, field, depth) in enumerate(entries):
            if what == FINE:
                continue
            place = EDGE + planes + depth - 1 if upper else EDGE - depth
            values = halo[index].astype(f32)
            if what == RAW and (FINE, field, depth) in entries:
                values = values + halo[entries.index((FINE, field, depth))].astype(f32)
            if field < 9:
                store(field, place, values)
            else:
                found = looked_up(values.astype(jnp.int32), tables)
                for kind in range(3):
                    factors[kind, place] = scale * found[kind]

    @pl.when(odd == 0)
    def _():
        unpack(across, False)
        unpack(within, True)

    @pl.when(odd != 0)
    def _():
        unpack(within, False)
        unpack(across, True)

    def move(place, do_x=True, do_yz=True):
        buoyancy = factors[0, place]
        chosen = ([VX] if do_x else []) + ([VY, VZ] if do_yz else [])
        results = [read(field, place) + buoyancy * pull(field, place) for field in chosen]
        for field, values in zip(chosen, results):
            store(field, place, values)

    def strain(place, do_yz=True, keep=None):
        lame, shear = factors[1, place], factors[2, place]
        twice = 2.0 * shear
        exx = joined(along_x(VX, place, False))
        eyy = joined(along_y(VY, place, False))
        ezz = joined(along_z(VZ, place, False))
        common = lame * (exx + eyy + ezz)
        changes = [(SXX, common + twice * exx)]
        changes.append((SXY, shear * joined(along_y(VX, place, True), along_x(VY, place, True))))
        changes.append((SXZ, shear * joined(along_z(VX, place, True), along_x(VZ, place, True))))
        if do_yz:
            changes.append((SYY, common + twice * eyy))
            changes.append((SZZ, common + twice * ezz))
            changes.append((SYZ, shear * joined(along_z(VY, place, True), along_y(VZ, place, True))))
        results = {field: read(field, place) + change for field, change in changes}
        for field, values in results.items():
            store(field, place, values)
        if keep is not None:
            compliance = strain_factors[1, place - EDGE]
            shift = strain_factors[0, place - EDGE] * (results[SXX] + results[SYY] + results[SZZ])
            first = pl.multiple_of((place - EDGE) * (8 * rows), 8 * rows)
            for field in range(3, 9):
                values = results[field] - shift if field < 6 else results[field]
                strains[keep, pl.ds(first + field - 3, rows, stride=8)] = values * compliance

    def over(first, last, body, width=2):
        def group(index, carry):
            for step in range(width):
                body(EDGE + first + index * width + step)
            return carry

        lax.fori_loop(0, (last - first) // width, group, 0)

    top = EDGE + planes
    move(EDGE - 2, do_yz=False)
    move(top + 1, do_x=False)
    over(-1, planes + 1, move)
    for place in range(EDGE - 3, EDGE):
        strain(place, do_yz=place == EDGE - 1)
    over(0, planes, functools.partial(strain, keep=0))
    for place in range(top, top + 3):
        strain(place, do_yz=place < top + 2)
    slots, points_each = cells.shape
    lane_bits = lanes.bit_length() - 1
    tall = lax.broadcasted_iota(jnp.int32, (8, lanes), 1)

    def sampled(which, slot):
        found = jnp.zeros((8, lanes), f32)
        for point in range(points_each):
            cell = cells[slot, point]
            first = pl.multiple_of((cell >> lane_bits) << 3, 8)
            turned = pltpu.roll(strains[which, pl.ds(first, 8)], (point - cell) & (lanes - 1), 1)
            found = jnp.where(tall == point, turned, found)
        return found

    move(EDGE - 2, do_yz=False)
    move(top + 1, do_x=False)
    over(-1, planes + 1, move)
    out_copies = [
        pltpu.make_async_copy(moving.at[:, slab, inner], velocity_out, out_sems.at[0]),
        pltpu.make_async_copy(pulling.at[:, slab, inner], stress_out, out_sems.at[1]),
    ]
    out_copies[0].start()
    over(0, planes, functools.partial(strain, keep=1))
    out_copies[1].start()

    pairs[...] = jnp.zeros(pairs.shape, f32)
    cell_copy.wait()

    def sample_slot(slot, carry):
        for which in range(2):
            found = sampled(which, slot)
            pairs[slot, which : which + 1] = jnp.concatenate([found[part : part + 1] for part in range(6)], axis=1)
        return carry

    lax.fori_loop(0, live[0], sample_slot, 0)
    slip_copy.wait()
    new = jnp.zeros((8, slips.shape[1]), f32)
    for slot in range(slots):
        pair = pairs[slot].astype(bf16)
        new = new + lax.dot_general(pair, slips[slot], (((1,), (1,)), ((), ())), preferred_element_type=f32)
    new = jnp.concatenate([new, jnp.zeros((lanes - 8, slips.shape[1]), f32)], axis=0).T
    column = lax.broadcasted_iota(jnp.int32, new.shape, 1)
    exponent, steps = in_steps(new)
    steps = jnp.where(column == 2, exponent, jnp.where(column == 3, exponents[...], steps))
    tail[...] = steps.astype(jnp.int32).astype(jnp.int16)
    sum_copies[1].start()
    for copy in out_copies + sum_copies:
        copy.wait()


def sum_kernel(sums, out, values, news):
    share, samples = out.shape
    half = samples // 2
    steps = sums[:, half:].astype(jnp.int32).astype(f32)
    news[...] = steps * jnp.exp2(steps[:, 2:3])
    values[...] = sums[:, :half].astype(jnp.int32).astype(f32) * jnp.exp2(steps[:, 3:4])
    halves = [jnp.zeros((share, half), f32) for _ in range(2)]
    new = jnp.zeros((share, news.shape[1]), f32)
    for device in range(sums.shape[0] // share):
        at = slice(device * share, (device + 1) * share)
        halves[device % 2] = halves[device % 2] + values[at]
        new = new + news[at]
    out[...] = jnp.concatenate([jnp.concatenate(halves, axis=1)[:, 2:], new[:, 0:2]], axis=1)


def per_device(
    velocity,
    stress,
    material,
    buoyancy_table,
    lame_table,
    shear_table,
    fault_cells,
    block_count,
    strain_history,
    slip_weights,
):
    count = lax.axis_size("gx")
    planes, rows, lanes = material.shape
    slots, parts, points_each, samples = strain_history.shape
    ruptures = slip_weights.shape[1]
    share = ruptures // count
    whole = pl.BlockSpec(memory_space=pltpu.VMEM)
    scalars = pl.BlockSpec(memory_space=pltpu.SMEM)
    anywhere = pl.BlockSpec(memory_space=pl.ANY)
    params = pltpu.CompilerParams(vmem_limit_bytes=24 * 1024 * 1024)

    def stay(array):
        return pltpu.with_memory_space_constraint(array, pltpu.HBM)

    live = block_count
    velocity, stress, material, slip_weights, cells = [
        stay(array) for array in (velocity, stress, material, slip_weights, fault_cells)
    ]
    tables = [stay(table) for table in (buoyancy_table, lame_table, shear_table)]
    table_scratch = [pltpu.SMEM(table.shape, f32) for table in tables]
    history = stay(strain_history.reshape(slots, parts * points_each, samples))

    def cost(flops, size):
        return pl.CostEstimate(flops=flops, bytes_accessed=size, transcendentals=0)

    halo = pltpu.VMEM((HALO, rows, lanes), bf16)
    extent = planes + 2 * EDGE
    padded = [pltpu.VMEM((fields, extent, rows + 2 * RIM, lanes), f32) for fields in (3, 6)]
    across, within = pl.pallas_call(
        pack_kernel,
        out_shape=(halo, halo),
        in_specs=[anywhere] * 4,
        out_specs=(whole, whole),
        scratch_shapes=[
            *padded,
            pltpu.VMEM(material.shape, jnp.int32),
            table_scratch[0],
            pltpu.SemaphoreType.DMA((4,)),
        ],
        compiler_params=params,
        name="pack_halos",
    )(velocity, stress, material, tables[0])
    chips = [(i, i + 1) for i in range(1, count - 1, 2)]
    cores = [(i, i + 1) for i in range(0, count - 1, 2)]
    cores = cores + [(j, i) for i, j in cores]
    packed = within
    across = lax.ppermute(across, "gx", chips + [(j, i) for i, j in chips])
    within = lax.ppermute(within, "gx", cores)

    half = pltpu.VMEM((ruptures, samples // 2), f32)
    kept, sent = pl.pallas_call(
        history_kernel,
        out_shape=(half, half),
        in_specs=[scalars] + [anywhere] * 3,
        out_specs=(whole, whole),
        scratch_shapes=[
            pltpu.VMEM(slip_weights.shape, bf16),
            pltpu.VMEM(history.shape, bf16),
            pltpu.VMEM((ruptures, samples), f32),
            pltpu.SemaphoreType.DMA((slots,)),
            pltpu.SemaphoreType.DMA((slots,)),
        ],
        compiler_params=params,
        cost_estimate=cost(10**10, 2 * (history.size + slip_weights.size)),
        name="history_product",
    )(live, slip_weights, history, packed)

    received = lax.ppermute(sent, "gx", cores)
    slab = [pltpu.VMEM(array.shape, array.dtype) for array in (velocity, stress, material)]
    partial, exponents, *slab, entries = pl.pallas_call(
        ready_kernel,
        out_shape=(
            pltpu.VMEM((ruptures, samples // 2), jnp.int16),
            pltpu.VMEM((ruptures, lanes), f32),
            *slab,
            pltpu.VMEM((3 * buoyancy_table.shape[0], lanes), f32),
        ),
        in_specs=[whole] * 2 + [anywhere] * 6,
        out_specs=(whole,) * 6,
        scratch_shapes=table_scratch + [pltpu.SemaphoreType.DMA((6,))],
        compiler_params=params,
        cost_estimate=cost(10**6, 1024 * 1024),
        name="ready_slab",
    )(kept, received, velocity, stress, material, *tables)
    velocity_two, stress_two, sums = pl.pallas_call(
        steps_kernel,
        out_shape=(
            jax.ShapeDtypeStruct(velocity.shape, f32),
            jax.ShapeDtypeStruct(stress.shape, f32),
            jax.ShapeDtypeStruct((ruptures, samples // 2 + lanes), jnp.int16),
        ),
        in_specs=[scalars] + [anywhere] * 2 + [whole] * 8,
        out_specs=(anywhere,) * 3,
        scratch_shapes=[
            *padded,
            pltpu.VMEM((3, extent, rows, lanes), f32),
            pltpu.VMEM((2, planes, rows, lanes), f32),
            pltpu.VMEM((2, planes * rows * 8, lanes), f32),
            pltpu.VMEM((slots, 8, parts * points_each), f32),
            pltpu.VMEM(slip_weights.shape, bf16),
            pltpu.SMEM(cells.shape, jnp.int32),
            pltpu.VMEM((ruptures, lanes), jnp.int16),
            pltpu.SemaphoreType.DMA,
            pltpu.SemaphoreType.DMA,
            pltpu.SemaphoreType.DMA((4,)),
        ],
        compiler_params=params,
        cost_estimate=cost(10**10, 30 * 1024 * 1024),
        name="two_steps",
    )(live, cells, slip_weights, *slab, entries, across, within, partial, exponents)
    sums = lax.all_to_all(sums, "gx", 0, 0, tiled=True)
    seismograms = pl.pallas_call(
        sum_kernel,
        out_shape=jax.ShapeDtypeStruct((share, samples), f32),
        in_specs=[whole],
        out_specs=whole,
        scratch_shapes=[pltpu.VMEM((ruptures, samples // 2), f32), pltpu.VMEM((ruptures, lanes), f32)],
        compiler_params=params,
        name="sum_partials",
    )(sums)
    return (velocity_two, stress_two, seismograms)


def solution(mesh):
    in_specs = (
        P(None, ("site", "gx"), None, None),
        P(None, ("site", "gx"), None, None),
        P("gx", None, None),
        P(),
        P(),
        P(),
        P("gx", None),
        P("gx"),
        P(("site", "gx"), None, None, None),
        P("gx", None, None),
    )
    out_specs = (
        P(None, ("site", "gx"), None, None),
        P(None, ("site", "gx"), None, None),
        P(("site", "gx"), None),
    )
    return jax.shard_map(
        per_device, mesh=mesh, in_specs=in_specs, out_specs=out_specs, check_vma=False
    )
```

```python
import functools

import jax
import jax.numpy as jnp
from jax import lax
from jax.experimental import pallas as pl
from jax.experimental.pallas import tpu as pltpu
from jax.sharding import PartitionSpec as P

time_step = 0.4
scale = time_step / 24.0

VX, VY, VZ, SXX, SYY, SZZ, SXY, SXZ, SYZ, MAT = range(10)
LOWER_RAW = (2, 1, 1, 3, 1, 1, 3, 3, 1, 3)
UPPER_RAW = (1, 2, 2, 3, 2, 2, 3, 3, 2, 3)
LOWER_MOVED = ((3, 5), (2, 4), (2, 4))
UPPER_MOVED = ((2, 4), (3, 5), (3, 5))
LOWER_FINE = (VX, VY, VZ, SXX, SXY, SXZ, SYZ)
UPPER_FINE = (VY, VZ, SXX)
RAW, MOVED, FINE = range(3)
EDGE = 5
RIM = 8


def halo_list(raw, moved, fine):
    entries = [(RAW, field, depth) for field in range(10) for depth in range(1, raw[field] + 1)]
    for field, (first, last) in enumerate(moved):
        entries += [(MOVED, field, depth) for depth in range(first, last + 1)]
    return entries + [(FINE, field, 1) for field in fine]


LOWER = halo_list(LOWER_RAW, LOWER_MOVED, LOWER_FINE)
UPPER = halo_list(UPPER_RAW, UPPER_MOVED, UPPER_FINE)
HALO = max(len(LOWER), len(UPPER))

f32 = jnp.float32
bf16 = jnp.bfloat16


def second_core():
    return lax.axis_index("gx") % 2


def fetch_all(sources, targets, sems):
    copies = [
        pltpu.make_async_copy(source, target, sems.at[index])
        for index, (source, target) in enumerate(zip(sources, targets))
    ]
    for copy in copies:
        copy.start()
    return copies


def looked_up(code, tables):
    results = [jnp.zeros(code.shape, f32) for _ in tables]
    for entry in range(len(tables[0])):
        hit = code == entry + 1
        results = [jnp.where(hit, table[entry], result) for table, result in zip(tables, results)]
    return results


def parts_of(behind, here_low, here_high, ahead):
    return here_high - here_low, ahead - behind


def joined(*parts):
    near, far = parts[0]
    for more_near, more_far in parts[1:]:
        near, far = near + more_near, far + more_far
    return 27.0 * near - far


def shifted(values, place, axis, by):
    size = values.shape[axis]
    inside = place < size - by if by > 0 else place >= -by
    return jnp.where(inside, pltpu.roll(values, -by % size, axis), 0.0)


def along(values, place, axis, forward):
    offsets = (-1, 0, 1, 2) if forward else (-2, -1, 0, 1)
    return parts_of(*[values if by == 0 else shifted(values, place, axis, by) for by in offsets])


def stepping(moving, pulling, rows, lanes):
    inner = pl.ds(RIM, rows)
    lane = lax.broadcasted_iota(jnp.int32, (rows, lanes), 1)

    def store(field, place, values):
        if field < 3:
            moving[field, place, inner] = values
        else:
            pulling[field - 3, place, inner] = values

    def read(field, place, at=inner):
        return moving[field, place, at] if field < 3 else pulling[field - 3, place, at]

    def along_x(field, place, forward):
        start = place - 1 if forward else place - 2
        return parts_of(*[read(field, start + step) for step in range(4)])

    def along_y(field, place, forward):
        start = RIM - 1 if forward else RIM - 2
        return parts_of(*[read(field, place, pl.ds(start + step, rows)) for step in range(4)])

    def along_z(field, place, forward):
        return along(read(field, place), lane, 1, forward)

    def pull(field, place):
        if field == VX:
            return joined(along_x(SXX, place, True), along_y(SXY, place, False), along_z(SXZ, place, False))
        if field == VY:
            return joined(along_x(SXY, place, False), along_y(SYY, place, True), along_z(SYZ, place, False))
        return joined(along_x(SXZ, place, False), along_y(SYZ, place, False), along_z(SZZ, place, True))

    return store, read, along_x, along_y, along_z, pull


def pack_kernel(
    velocity_from,
    stress_from,
    material_from,
    buoyancy_from,
    across,
    within,
    moving,
    pulling,
    material,
    buoyancy,
    sems,
):
    planes, rows, lanes = material.shape
    slab, inner = pl.ds(EDGE, planes), pl.ds(RIM, rows)
    copies = fetch_all(
        (stress_from, velocity_from, material_from, buoyancy_from),
        (pulling.at[:, slab, inner], moving.at[:, slab, inner], material, buoyancy),
        sems,
    )
    blank = jnp.zeros((moving.shape[1], RIM, lanes), f32)
    for ref, fields_along_y in ((moving, (0, 1, 2)), (pulling, (SXY - 3, SYY - 3, SYZ - 3))):
        for field in fields_along_y:
            ref[field, :, 0:RIM] = blank
            ref[field, :, RIM + rows : 2 * RIM + rows] = blank
    store, read, along_x, along_y, along_z, pull = stepping(moving, pulling, rows, lanes)
    odd = second_core()
    for copy in copies:
        copy.wait()

    def moved(field, plane):
        entries = [buoyancy[entry] for entry in range(buoyancy.shape[0])]
        factor = scale * looked_up(material[plane] + 1, (entries,))[0]
        return read(field, EDGE + plane) + factor * pull(field, EDGE + plane)

    def fill(out, entries, plane_of):
        for index, (what, field, depth) in enumerate(entries):
            plane = plane_of(depth)
            if what == MOVED:
                values = moved(field, plane)
            elif field < 9:
                values = read(field, EDGE + plane)
            else:
                values = (material[plane] + 1).astype(f32)
            if what == FINE:
                values = values - values.astype(bf16).astype(f32)
            out[index] = values.astype(bf16)
        for spare in range(len(entries), out.shape[0]):
            out[spare] = jnp.zeros(out.shape[1:], bf16)

    def upper_face(out):
        fill(out, LOWER, lambda depth: planes - depth)

    def lower_face(out):
        fill(out, UPPER, lambda depth: depth - 1)

    @pl.when(odd == 0)
    def _():
        lower_face(across)
        upper_face(within)

    @pl.when(odd != 0)
    def _():
        upper_face(across)
        lower_face(within)


def in_steps(values):
    largest = jnp.max(jnp.abs(values), axis=1, keepdims=True)
    exponent = jnp.ceil(jnp.log2(jnp.maximum(largest, 1e-30))) - 14.0
    return exponent, jnp.clip(jnp.round(values * jnp.exp2(-exponent)), -32767.0, 32767.0)


def history_kernel(live, weights, history, after, kept, sent, slips, records, total, slip_sems, record_sems):
    del after
    slots = weights.shape[0]
    copies = [
        (
            pltpu.make_async_copy(weights.at[slot], slips.at[slot], slip_sems.at[slot]),
            pltpu.make_async_copy(history.at[slot], records.at[slot], record_sems.at[slot]),
        )
        for slot in range(slots)
    ]
    for copy in copies[0]:
        copy.start()
    for slot in range(1, slots):

        @pl.when(slot < live[0])
        def _(slot=slot):
            for copy in copies[slot]:
                copy.start()

    for copy in copies[0]:
        copy.wait()
    total[...] = jnp.dot(slips[0], records[0], preferred_element_type=f32)
    for slot in range(1, slots):

        @pl.when(slot < live[0])
        def _(slot=slot):
            for copy in copies[slot]:
                copy.wait()
            total[...] += jnp.dot(slips[slot], records[slot], preferred_element_type=f32)

    half = kept.shape[1]
    first = second_core() == 0
    early, late = total[:, :half], total[:, half:]
    early = jnp.where(lax.broadcasted_iota(jnp.int32, early.shape, 1) < 2, 0.0, early)
    kept[...] = jnp.where(first, early, late)
    sent[...] = jnp.where(first, late, early)


def ready_kernel(
    kept,
    received,
    velocity_from,
    stress_from,
    material_from,
    buoyancy_from,
    lame_from,
    shear_from,
    partial,
    exponents,
    velocity,
    stress,
    material,
    entries,
    buoyancy,
    lame,
    shear,
    sems,
):
    copies = fetch_all(
        (buoyancy_from, lame_from, shear_from, stress_from, velocity_from, material_from),
        (buoyancy, lame, shear, stress, velocity, material),
        sems,
    )
    exponent, steps = in_steps(kept[...] + received[...])
    partial[...] = steps.astype(jnp.int32).astype(jnp.int16)
    exponents[...] = jnp.broadcast_to(exponent, exponents.shape)
    for copy in copies[:3]:
        copy.wait()
    for kind, table in enumerate((buoyancy, lame, shear)):
        for entry in range(table.shape[0]):
            at = kind * table.shape[0] + entry
            entries[at : at + 1] = jnp.full((1, entries.shape[1]), table[entry], f32)
    for copy in copies[3:]:
        copy.wait()


def steps_kernel(
    live,
    cells_from,
    weights,
    velocity,
    stress,
    material,
    entries,
    across,
    within,
    partial,
    exponents,
    velocity_out,
    stress_out,
    sums,
    moving,
    pulling,
    factors,
    strain_factors,
    strains,
    pairs,
    slips,
    cells,
    tail,
    cell_sem,
    slip_sem,
    out_sems,
):
    planes, rows, lanes = material.shape
    materials = entries.shape[0] // 3
    tables = [
        [entries[at : at + 1] for at in range(kind * materials, (kind + 1) * materials)] for kind in range(3)
    ]
    inner = pl.ds(RIM, rows)
    slab = pl.ds(EDGE, planes)
    cell_copy = pltpu.make_async_copy(cells_from, cells, cell_sem)
    cell_copy.start()
    slip_copy = pltpu.make_async_copy(weights, slips, slip_sem)
    slip_copy.start()
    half = partial.shape[1]
    sum_copies = [
        pltpu.make_async_copy(partial, sums.at[:, pl.ds(0, half)], out_sems.at[2]),
        pltpu.make_async_copy(tail, sums.at[:, pl.ds(half, lanes)], out_sems.at[3]),
    ]
    sum_copies[0].start()
    odd = second_core()
    store, read, along_x, along_y, along_z, pull = stepping(moving, pulling, rows, lanes)

    blank = jnp.zeros((moving.shape[1], RIM, lanes), f32)
    for ref, fields_along_y in ((moving, (0, 1, 2)), (pulling, (SXY - 3, SYY - 3, SYZ - 3))):
        for field in fields_along_y:
            ref[field, :, 0:RIM] = blank
            ref[field, :, RIM + rows : 2 * RIM + rows] = blank
    moving[:, slab, inner] = velocity[...]
    pulling[:, slab, inner] = stress[...]

    for plane in range(planes):
        buoyancy, lame, shear = looked_up(material[plane] + 1, tables)
        factors[0, EDGE + plane] = scale * buoyancy
        factors[1, EDGE + plane] = scale * lame
        factors[2, EDGE + plane] = scale * shear
        strain_factors[0, plane] = lame / (3.0 * lame + 2.0 * shear)
        strain_factors[1, plane] = 1.0 / (2.0 * shear)

    def unpack(halo, upper):
        entries = UPPER if upper else LOWER
        for index, (what, field, depth) in enumerate(entries):
            if what == FINE:
                continue
            place = EDGE + planes + depth - 1 if upper else EDGE - depth
            values = halo[index].astype(f32)
            if what == RAW and (FINE, field, depth) in entries:
                values = values + halo[entries.index((FINE, field, depth))].astype(f32)
            if field < 9:
                store(field, place, values)
            else:
                found = looked_up(values.astype(jnp.int32), tables)
                for kind in range(3):
                    factors[kind, place] = scale * found[kind]

    @pl.when(odd == 0)
    def _():
        unpack(across, False)
        unpack(within, True)

    @pl.when(odd != 0)
    def _():
        unpack(within, False)
        unpack(across, True)

    def move(place, do_x=True, do_yz=True):
        buoyancy = factors[0, place]
        chosen = ([VX] if do_x else []) + ([VY, VZ] if do_yz else [])
        results = [read(field, place) + buoyancy * pull(field, place) for field in chosen]
        for field, values in zip(chosen, results):
            store(field, place, values)

    def strain(place, do_yz=True, keep=None):
        lame, shear = factors[1, place], factors[2, place]
        twice = 2.0 * shear
        exx = joined(along_x(VX, place, False))
        eyy = joined(along_y(VY, place, False))
        ezz = joined(along_z(VZ, place, False))
        common = lame * (exx + eyy + ezz)
        changes = [(SXX, common + twice * exx)]
        changes.append((SXY, shear * joined(along_y(VX, place, True), along_x(VY, place, True))))
        changes.append((SXZ, shear * joined(along_z(VX, place, True), along_x(VZ, place, True))))
        if do_yz:
            changes.append((SYY, common + twice * eyy))
            changes.append((SZZ, common + twice * ezz))
            changes.append((SYZ, shear * joined(along_z(VY, place, True), along_y(VZ, place, True))))
        results = {field: read(field, place) + change for field, change in changes}
        for field, values in results.items():
            store(field, place, values)
        if keep is not None:
            compliance = strain_factors[1, place - EDGE]
            shift = strain_factors[0, place - EDGE] * (results[SXX] + results[SYY] + results[SZZ])
            first = pl.multiple_of((place - EDGE) * (8 * rows), 8 * rows)
            for field in range(3, 9):
                values = results[field] - shift if field < 6 else results[field]
                strains[keep, pl.ds(first + field - 3, rows, stride=8)] = values * compliance

    def over(first, last, body, width=2):
        def group(index, carry):
            for step in range(width):
                body(EDGE + first + index * width + step)
            return carry

        lax.fori_loop(0, (last - first) // width, group, 0)

    top = EDGE + planes
    move(EDGE - 2, do_yz=False)
    move(top + 1, do_x=False)
    over(-1, planes + 1, move)
    for place in range(EDGE - 3, EDGE):
        strain(place, do_yz=place == EDGE - 1)
    over(0, planes, functools.partial(strain, keep=0))
    for place in range(top, top + 3):
        strain(place, do_yz=place < top + 2)
    slots, points_each = cells.shape
    lane_bits = lanes.bit_length() - 1
    tall = lax.broadcasted_iota(jnp.int32, (8, lanes), 1)

    def sampled(slot):
        found = [jnp.zeros((8, lanes), f32) for _ in range(2)]
        for point in range(points_each):
            cell = cells[slot, point]
            first = pl.multiple_of((cell >> lane_bits) << 3, 8)
            shift = (point - cell) & (lanes - 1)
            hit = tall == point
            for which in range(2):
                turned = pltpu.roll(strains[which, pl.ds(first, 8)], shift, 1)
                found[which] = jnp.where(hit, turned, found[which])
        return found

    move(EDGE - 2, do_yz=False)
    move(top + 1, do_x=False)
    over(-1, planes + 1, move)
    out_copies = [
        pltpu.make_async_copy(moving.at[:, slab, inner], velocity_out, out_sems.at[0]),
        pltpu.make_async_copy(pulling.at[:, slab, inner], stress_out, out_sems.at[1]),
    ]
    out_copies[0].start()
    over(0, planes, functools.partial(strain, keep=1))
    out_copies[1].start()

    pairs[...] = jnp.zeros(pairs.shape, f32)
    cell_copy.wait()

    def sample_slot(slot, carry):
        for which, found in enumerate(sampled(slot)):
            pairs[slot, which : which + 1] = jnp.concatenate([found[part : part + 1] for part in range(6)], axis=1)
        return carry

    lax.fori_loop(0, live[0], sample_slot, 0)
    slip_copy.wait()
    new = jnp.zeros((8, slips.shape[1]), f32)
    for slot in range(slots):
        pair = pairs[slot].astype(bf16)
        new = new + lax.dot_general(pair, slips[slot], (((1,), (1,)), ((), ())), preferred_element_type=f32)
    new = jnp.concatenate([new, jnp.zeros((lanes - 8, slips.shape[1]), f32)], axis=0).T
    column = lax.broadcasted_iota(jnp.int32, new.shape, 1)
    exponent, steps = in_steps(new)
    steps = jnp.where(column == 2, exponent, jnp.where(column == 3, exponents[...], steps))
    tail[...] = steps.astype(jnp.int32).astype(jnp.int16)
    sum_copies[1].start()
    for copy in out_copies + sum_copies:
        copy.wait()


def sum_kernel(sums, out, values, news):
    share, samples = out.shape
    half = samples // 2
    steps = sums[:, half:].astype(jnp.int32).astype(f32)
    news[...] = steps * jnp.exp2(steps[:, 2:3])
    values[...] = sums[:, :half].astype(jnp.int32).astype(f32) * jnp.exp2(steps[:, 3:4])
    halves = [jnp.zeros((share, half), f32) for _ in range(2)]
    new = jnp.zeros((share, news.shape[1]), f32)
    for device in range(sums.shape[0] // share):
        at = slice(device * share, (device + 1) * share)
        halves[device % 2] = halves[device % 2] + values[at]
        new = new + news[at]
    out[...] = jnp.concatenate([jnp.concatenate(halves, axis=1)[:, 2:], new[:, 0:2]], axis=1)


def per_device(
    velocity,
    stress,
    material,
    buoyancy_table,
    lame_table,
    shear_table,
    fault_cells,
    block_count,
    strain_history,
    slip_weights,
):
    count = lax.axis_size("gx")
    planes, rows, lanes = material.shape
    slots, parts, points_each, samples = strain_history.shape
    ruptures = slip_weights.shape[1]
    share = ruptures // count
    whole = pl.BlockSpec(memory_space=pltpu.VMEM)
    scalars = pl.BlockSpec(memory_space=pltpu.SMEM)
    anywhere = pl.BlockSpec(memory_space=pl.ANY)
    params = pltpu.CompilerParams(vmem_limit_bytes=24 * 1024 * 1024)

    def stay(array):
        return pltpu.with_memory_space_constraint(array, pltpu.HBM)

    live = block_count
    velocity, stress, material, slip_weights, cells = [
        stay(array) for array in (velocity, stress, material, slip_weights, fault_cells)
    ]
    tables = [stay(table) for table in (buoyancy_table, lame_table, shear_table)]
    table_scratch = [pltpu.SMEM(table.shape, f32) for table in tables]
    history = stay(strain_history.reshape(slots, parts * points_each, samples))

    def cost(flops, size):
        return pl.CostEstimate(flops=flops, bytes_accessed=size, transcendentals=0)

    halo = pltpu.VMEM((HALO, rows, lanes), bf16)
    extent = planes + 2 * EDGE
    padded = [pltpu.VMEM((fields, extent, rows + 2 * RIM, lanes), f32) for fields in (3, 6)]
    across, within = pl.pallas_call(
        pack_kernel,
        out_shape=(halo, halo),
        in_specs=[anywhere] * 4,
        out_specs=(whole, whole),
        scratch_shapes=[
            *padded,
            pltpu.VMEM(material.shape, jnp.int32),
            table_scratch[0],
            pltpu.SemaphoreType.DMA((4,)),
        ],
        compiler_params=params,
        name="pack_halos",
    )(velocity, stress, material, tables[0])
    chips = [(i, i + 1) for i in range(1, count - 1, 2)]
    cores = [(i, i + 1) for i in range(0, count - 1, 2)]
    cores = cores + [(j, i) for i, j in cores]
    packed = within
    across = lax.ppermute(across, "gx", chips + [(j, i) for i, j in chips])
    within = lax.ppermute(within, "gx", cores)

    half = pltpu.VMEM((ruptures, samples // 2), f32)
    kept, sent = pl.pallas_call(
        history_kernel,
        out_shape=(half, half),
        in_specs=[scalars] + [anywhere] * 3,
        out_specs=(whole, whole),
        scratch_shapes=[
            pltpu.VMEM(slip_weights.shape, bf16),
            pltpu.VMEM(history.shape, bf16),
            pltpu.VMEM((ruptures, samples), f32),
            pltpu.SemaphoreType.DMA((slots,)),
            pltpu.SemaphoreType.DMA((slots,)),
        ],
        compiler_params=params,
        cost_estimate=cost(10**10, 2 * (history.size + slip_weights.size)),
        name="history_product",
    )(live, slip_weights, history, packed)

    received = lax.ppermute(sent, "gx", cores)
    slab = [pltpu.VMEM(array.shape, array.dtype) for array in (velocity, stress, material)]
    partial, exponents, *slab, entries = pl.pallas_call(
        ready_kernel,
        out_shape=(
            pltpu.VMEM((ruptures, samples // 2), jnp.int16),
            pltpu.VMEM((ruptures, lanes), f32),
            *slab,
            pltpu.VMEM((3 * buoyancy_table.shape[0], lanes), f32),
        ),
        in_specs=[whole] * 2 + [anywhere] * 6,
        out_specs=(whole,) * 6,
        scratch_shapes=table_scratch + [pltpu.SemaphoreType.DMA((6,))],
        compiler_params=params,
        cost_estimate=cost(10**6, 1024 * 1024),
        name="ready_slab",
    )(kept, received, velocity, stress, material, *tables)
    velocity_two, stress_two, sums = pl.pallas_call(
        steps_kernel,
        out_shape=(
            jax.ShapeDtypeStruct(velocity.shape, f32),
            jax.ShapeDtypeStruct(stress.shape, f32),
            jax.ShapeDtypeStruct((ruptures, samples // 2 + lanes), jnp.int16),
        ),
        in_specs=[scalars] + [anywhere] * 2 + [whole] * 8,
        out_specs=(anywhere,) * 3,
        scratch_shapes=[
            *padded,
            pltpu.VMEM((3, extent, rows, lanes), f32),
            pltpu.VMEM((2, planes, rows, lanes), f32),
            pltpu.VMEM((2, planes * rows * 8, lanes), f32),
            pltpu.VMEM((slots, 8, parts * points_each), f32),
            pltpu.VMEM(slip_weights.shape, bf16),
            pltpu.SMEM(cells.shape, jnp.int32),
            pltpu.VMEM((ruptures, lanes), jnp.int16),
            pltpu.SemaphoreType.DMA,
            pltpu.SemaphoreType.DMA,
            pltpu.SemaphoreType.DMA((4,)),
        ],
        compiler_params=params,
        cost_estimate=cost(10**10, 30 * 1024 * 1024),
        name="two_steps",
    )(live, cells, slip_weights, *slab, entries, across, within, partial, exponents)
    sums = lax.all_to_all(sums, "gx", 0, 0, tiled=True)
    seismograms = pl.pallas_call(
        sum_kernel,
        out_shape=jax.ShapeDtypeStruct((share, samples), f32),
        in_specs=[whole],
        out_specs=whole,
        scratch_shapes=[pltpu.VMEM((ruptures, samples // 2), f32), pltpu.VMEM((ruptures, lanes), f32)],
        compiler_params=params,
        name="sum_partials",
    )(sums)
    return (velocity_two, stress_two, seismograms)


def solution(mesh):
    in_specs = (
        P(None, ("site", "gx"), None, None),
        P(None, ("site", "gx"), None, None),
        P("gx", None, None),
        P(),
        P(),
        P(),
        P("gx", None),
        P("gx"),
        P(("site", "gx"), None, None, None),
        P("gx", None, None),
    )
    out_specs = (
        P(None, ("site", "gx"), None, None),
        P(None, ("site", "gx"), None, None),
        P(("site", "gx"), None),
    )
    return jax.shard_map(
        per_device, mesh=mesh, in_specs=in_specs, out_specs=out_specs, check_vma=False
    )
```
